32 devices in a mesh: dp: 8 (over z, core), tensor: 4 (over y, x).
Axes of the slice: x: 2, y: 2, z: 4, core: 2. Of those that a mesh axis runs over, the one named last changes fastest.
Arguments:
- x_quant: bfloat16 [96, 8192], P('tensor', 'dp'), may hold values from -6 to 6
- x_scale: float32 [4, 64], P('tensor', 'dp'), may hold values from 0.25 to 4
- x_outlier: int32 [4, 64], P('tensor', 'dp'), may hold values 0 or 1
- x_correction: bfloat16 [96, 8192], P('tensor', 'dp'), may hold values from -12 to 12
- g_quant: bfloat16 [96, 8192], P('tensor', 'dp'), may hold values from -6 to 6
- g_scale: float32 [4, 64], P('tensor', 'dp'), may hold values from 0.25 to 4
- g_outlier: int32 [4, 64], P('tensor', 'dp'), may hold values 0 or 1
- g_correction: bfloat16 [96, 8192], P('tensor', 'dp'), may hold values from -12 to 12
- gate_pre: bfloat16 [96, 26624], P('dp', 'tensor'), may hold values from -8 to 8
- up_pre: bfloat16 [96, 26624], P('dp', 'tensor'), may hold values from -6 to 6
- w_gate: bfloat16 [8192, 26624], P('dp', 'tensor'), may hold values from -0.0625 to 0.0625
- w_up: bfloat16 [8192, 26624], P('dp', 'tensor'), may hold values from -0.0625 to 0.0625
- w_down: bfloat16 [26624, 8192], P('tensor', 'dp'), may hold values from -0.0625 to 0.0625
Outputs:
- grad_input: bfloat16 [96, 8192], P('tensor', 'dp')
- grad_gate_weight: bfloat16 [8192, 26624], P('dp', 'tensor')
- grad_up_weight: bfloat16 [8192, 26624], P('dp', 'tensor')
- grad_down_weight: bfloat16 [26624, 8192], P('tensor', 'dp')
The draws below stay inside these ranges and needn't reach their ends.
All inputs are finite; a program needn't handle non-finite values. No bound on the sum of `x_outlier` or of `g_outlier` on one device may be relied on, other than what follows from the above.
Results may differ from the reference program's by a relative error of at most 0.0064.
Values may be sent and summed in bfloat16 or wider, within the bound.
No kernel may reach another device: no remote copies, remote signals or barrier semaphores. Data moves between devices by JAX's collectives and lax.ppermute only.
A program may use at most 128 MiB of HBM per device.

```python
import math
import jax
import jax.numpy as jnp

D = 8192
FF = 26624
BLK_C = 128
TOK_DEV = 24
TOKENS = 96
N_TENSOR = 4


def with_ends(entries, rng, low, high):
    extent = entries.shape
    index_at = [jax.random.randint(jax.random.fold_in(rng, axis), (), 0, extent[axis]) for axis in range(len(extent))]
    entries = entries.at[tuple(index_at)].set(low)
    longest = extent.index(max(extent))
    index_at[longest] = (index_at[longest] + 1) % extent[longest]
    return entries.at[tuple(index_at)].set(high)


def shard_levels(own_key, shape, split, low, high):
    level, own = 1.0, jax.random.fold_in(own_key, 6)
    for axis_at, shards_of in split:
        draws = jnp.exp(jax.random.uniform(jax.random.fold_in(own, axis_at), (shards_of,), jnp.float32, low / len(split), high / len(split)))
        level = level * jnp.repeat(draws, shape[axis_at] // shards_of).reshape([-1 if axis == axis_at else 1 for axis in range(len(shape))])
    return level


def scatter_about(stream_key, shape, width, reach, split=(), held_as=jnp.bfloat16):
    drawn = width * jax.random.normal(stream_key, shape, jnp.float32)
    if split:
        drawn = drawn * shard_levels(stream_key, shape, split, -0.22, 0.18)
    return jnp.clip(drawn, -reach, reach).astype(held_as)


def setup_inputs(seed: int = 0) -> dict:
    arg_keys = jax.random.split(jax.random.key(seed), 14)
    x_quant = scatter_about(arg_keys[0], (TOKENS, D), 1.0, 6.0, ((0, 4), (1, 8)))
    x_scale = jnp.clip(jnp.exp(math.log(4.0) - 2.7725887 * jax.random.uniform(arg_keys[1], (N_TENSOR, D // BLK_C), jnp.float32) ** shard_levels(arg_keys[1], (N_TENSOR, D // BLK_C), ((0, 4), (1, 8)), -0.2, 0.2)), 0.25, 4.0)
    x_outlier = with_ends((jax.random.randint(arg_keys[2], (N_TENSOR, D // BLK_C), 0, 4) < 1).astype(jnp.int32), jax.random.fold_in(arg_keys[2], 1), 0, 1)
    x_correction = scatter_about(arg_keys[3], (TOKENS, D), 3.0, 12.0, ((0, 4), (1, 8)))
    g_quant = scatter_about(arg_keys[4], (TOKENS, D), 1.0, 6.0, ((0, 4), (1, 8)))
    g_scale = jnp.clip(jnp.exp(math.log(4.0) - 2.7725887 * jax.random.uniform(arg_keys[5], (N_TENSOR, D // BLK_C), jnp.float32) ** shard_levels(arg_keys[5], (N_TENSOR, D // BLK_C), ((0, 4), (1, 8)), -0.2, 0.2)), 0.25, 4.0)
    g_outlier = with_ends((jax.random.randint(arg_keys[6], (N_TENSOR, D // BLK_C), 0, 4) < 1).astype(jnp.int32), jax.random.fold_in(arg_keys[6], 1), 0, 1)
    g_correction = scatter_about(arg_keys[7], (TOKENS, D), 3.0, 12.0, ((0, 4), (1, 8)))
    gate_pre = scatter_about(arg_keys[8], (TOKENS, FF), 1.5, 8.0, ((0, 8), (1, 4)))
    up_pre = scatter_about(arg_keys[9], (TOKENS, FF), 1.0, 6.0, ((0, 8), (1, 4)))
    w_gate = scatter_about(arg_keys[10], (D, FF), D ** -0.5, 0.0625, ((0, 8), (1, 4)))
    w_up = scatter_about(arg_keys[11], (D, FF), D ** -0.5, 0.0625, ((0, 8), (1, 4)))
    w_down = scatter_about(arg_keys[12], (FF, D), D ** -0.5, 0.0625, ((0, 4), (1, 8)))
    return {"x_quant": x_quant, "x_scale": x_scale, "x_outlier": x_outlier, "x_correction": x_correction, "g_quant": g_quant, "g_scale": g_scale, "g_outlier": g_outlier, "g_correction": g_correction, "gate_pre": gate_pre, "up_pre": up_pre, "w_gate": w_gate, "w_up": w_up, "w_down": w_down}


def expand(block_values):
    return jnp.repeat(jnp.repeat(block_values, TOK_DEV, axis=0), BLK_C, axis=1)


def dequantize(quant, block_scale, outlier, correction):
    values = expand(block_scale) * quant.astype(jnp.float32) + expand(outlier.astype(jnp.float32)) * correction.astype(jnp.float32)
    return values.astype(jnp.bfloat16)


def reference(x_quant, x_scale, x_outlier, x_correction, g_quant, g_scale, g_outlier, g_correction, gate_pre, up_pre, w_gate, w_up, w_down):
    inputs = dequantize(x_quant, x_scale, x_outlier, x_correction)
    out_grad = dequantize(g_quant, g_scale, g_outlier, g_correction)
    hidden_grad = jnp.dot(out_grad, w_down.T, preferred_element_type=jnp.float32)
    gate_val = gate_pre.astype(jnp.float32)
    up_val = up_pre.astype(jnp.float32)
    sigmoid_gate = jax.nn.sigmoid(gate_val)
    silu_gate = gate_val * sigmoid_gate
    hidden = (silu_gate * up_val).astype(jnp.bfloat16)
    up_grad = (hidden_grad * silu_gate).astype(jnp.bfloat16)
    gate_grad = (hidden_grad * up_val * sigmoid_gate * (1.0 + gate_val * (1.0 - sigmoid_gate))).astype(jnp.bfloat16)
    grad_down_weight = jnp.dot(hidden.T, out_grad, preferred_element_type=jnp.float32).astype(jnp.bfloat16)
    grad_gate_weight = jnp.dot(inputs.T, gate_grad, preferred_element_type=jnp.float32).astype(jnp.bfloat16)
    grad_up_weight = jnp.dot(inputs.T, up_grad, preferred_element_type=jnp.float32).astype(jnp.bfloat16)
    grad_input = (jnp.dot(gate_grad, w_gate.T, preferred_element_type=jnp.float32) + jnp.dot(up_grad, w_up.T, preferred_element_type=jnp.float32)).astype(jnp.bfloat16)
    return grad_input, grad_gate_weight, grad_up_weight, grad_down_weight
```

```python
import functools

import jax
import jax.numpy as jnp
from jax import lax
from jax.experimental import pallas as pl
from jax.experimental.pallas import tpu as pltpu
from jax.sharding import PartitionSpec as P

BLK_C = 128
F32 = jnp.float32
BF16 = jnp.bfloat16
VMEM = pltpu.VMEM
SMEM = pltpu.SMEM


def whole(space=VMEM):
    return pl.BlockSpec(memory_space=space)


def shape(dims, dtype):
    return jax.ShapeDtypeStruct(dims, dtype)


def params(mib=56):
    return pltpu.CompilerParams(vmem_limit_bytes=mib * 1024 * 1024)


def cost(flops, nbytes):
    return pl.CostEstimate(flops=int(flops), bytes_accessed=int(nbytes), transcendentals=0)


def tile_of(extent):
    return next(t for t in (512, 256, 128) if extent % t == 0)


def pieces(extent, step):
    return [(at, min(step, extent - at)) for at in range(0, extent, step)]


def prep_kernel(xq, xs, xo, xc, gq, gs, go, gc, gate, up, xg, gu):
    for at, (quant, scale, flag, corr) in enumerate(((gq, gs, go, gc), (xq, xs, xo, xc))):
        for b in range(scale.shape[1]):
            cols = slice(b * BLK_C, (b + 1) * BLK_C)
            value = scale[0, b] * quant[:, cols].astype(F32) + flag[0, b].astype(F32) * corr[
                :, cols
            ].astype(F32)
            xg[at, :, cols] = value.astype(BF16)
    gu[...] = jnp.concatenate([gate[...].astype(F32), up[...].astype(F32)], 0).astype(BF16)


def prep(xq, xs, xo, xc, gq, gs, go, gc, gate, up):
    rows, width = xq.shape
    tok, ff = gate.shape
    return pl.pallas_call(
        prep_kernel,
        out_shape=(shape((2, rows, width), BF16), shape((2 * tok, ff), BF16)),
        in_specs=[whole(), whole(SMEM), whole(SMEM), whole()] * 2 + [whole()] * 2,
        out_specs=(whole(), whole()),
        compiler_params=params(),
        cost_estimate=cost(0, 4 * xq.size * 2 + gate.size * 8),
    )(xq, xs, xo, xc, gq, gs, go, gc, gate, up)


def load_down(place, half, width, w_hbm, w_vmem, sems):
    copies = []
    for k, (at, size) in enumerate(pieces(width, 256)):
        start = pl.multiple_of(half + at, 16)
        copy = pltpu.make_async_copy(
            w_hbm.at[pl.ds(start, size)], w_vmem.at[pl.ds(at, size)], sems.at[k]
        )
        copy.start()
        copies.append(copy)
    return copies


def hidden_half(copies, grads, width, w_vmem, out):
    groups, rows = out.shape[0], out.shape[1]
    for copy, (at, size) in zip(copies, pieces(width, 256)):
        copy.wait()
        total = lax.dot_general(
            grads, w_vmem[at : at + size, :], (((1,), (1,)), ((), ())), preferred_element_type=F32
        )
        for q in range(groups):
            out[q, :, at : at + size] = total[q * rows : (q + 1) * rows, :].astype(out.dtype)


def first_half_kernel(n_t, offset, place, *refs):
    parts, (w_hbm, grads_out, inputs_t, out, w_vmem, held, sems) = refs[:n_t], refs[n_t:]
    core, me = place[0], place[2]
    width = out.shape[2]
    copies = load_down(place, (1 - core) * offset, width, w_hbm, w_vmem, sems)
    rows = held.shape[1]
    for s in range(n_t):
        held[me ^ s] = parts[s][1].astype(F32)
    inputs = held[...].reshape(n_t * rows, held.shape[2])
    inputs_t[...] = inputs.T.astype(BF16)
    for s in range(n_t):
        held[me ^ s] = parts[s][0].astype(F32)
    grads = held[...].reshape(n_t * rows, held.shape[2]).astype(BF16)
    grads_out[...] = grads
    hidden_half(copies, grads, width, w_vmem, out)


def second_half_kernel(offset, place, grads, w_hbm, out, w_vmem, sems):
    width = out.shape[2]
    copies = load_down(place, place[0] * offset, width, w_hbm, w_vmem, sems)
    hidden_half(copies, grads[...], width, w_vmem, out)


def first_half(place, parts, w_down, n_z, width):
    n_t, rows, chans = len(parts), parts[0].shape[1], parts[0].shape[2]
    tokens = n_t * rows
    n_copies = len(pieces(width, 256))
    return pl.pallas_call(
        functools.partial(first_half_kernel, n_t, w_down.shape[0] - width),
        out_shape=(
            shape((tokens, chans), BF16),
            shape((chans, tokens), BF16),
            shape((n_z, tokens // n_z, width), BF16),
        ),
        in_specs=[whole(SMEM)] + [whole()] * n_t + [whole(pl.ANY)],
        out_specs=(whole(), whole(), whole()),
        scratch_shapes=[
            VMEM((width, chans), BF16),
            VMEM((n_t, rows, chans), F32),
            pltpu.SemaphoreType.DMA((n_copies,)),
        ],
        compiler_params=params(),
        cost_estimate=cost(2 * tokens * chans * width, 2 * chans * width),
    )(place, *parts, w_down)


def second_half(place, grads, w_down, n_z, width):
    tokens, chans = grads.shape
    n_copies = len(pieces(width, 256))
    return pl.pallas_call(
        functools.partial(second_half_kernel, w_down.shape[0] - width),
        out_shape=shape((n_z, tokens // n_z, width), F32),
        in_specs=[whole(SMEM), whole(), whole(pl.ANY)],
        out_specs=whole(),
        scratch_shapes=[VMEM((width, chans), BF16), pltpu.SemaphoreType.DMA((n_copies,))],
        compiler_params=params(),
        cost_estimate=cost(2 * tokens * chans * width, 2 * chans * width),
    )(place, grads, w_down)


def pair_kernel(picks, place, mine, theirs, own, *outs):
    z, n_z = place[1], mine.shape[0]

    def chunk(at):
        return mine[at] + theirs[at].astype(F32)

    own[...] = chunk(z)
    for pick, out in zip(picks, outs):
        out[...] = chunk(pick(z, n_z)).astype(out.dtype)


def pair_sum(place, mine, theirs, picks):
    n_z, rows, width = mine.shape
    return pl.pallas_call(
        functools.partial(pair_kernel, picks),
        out_shape=(shape((rows, width), F32),) + (shape((rows, width), BF16),) * len(picks),
        in_specs=[whole(SMEM), whole(), whole()],
        out_specs=(whole(),) * (1 + len(picks)),
        compiler_params=params(),
        cost_estimate=cost(0, mine.size * 12),
    )(place, mine, theirs)


def add_kernel(*refs):
    *terms, out = refs
    total = terms[0][...].astype(F32)
    for term in terms[1:]:
        total = total + term[...].astype(F32)
    out[...] = total.astype(out.dtype)


def add_all(*terms):
    return pl.pallas_call(
        add_kernel,
        out_shape=shape(terms[0].shape, BF16),
        in_specs=[whole()] * len(terms),
        out_specs=whole(),
        compiler_params=params(),
        cost_estimate=cost(0, terms[0].size * 2 * (len(terms) + 2)),
    )(*terms)


def z_pairs(pairs):
    return [(2 * a + c, 2 * b + c) for a, b in pairs for c in range(2)]


def z_shift(value, pairs):
    return lax.ppermute(value, "dp", z_pairs(pairs))


def swap_cores(value, n_z):
    return lax.ppermute(value, "dp", [(2 * z + c, 2 * z + 1 - c) for z in range(n_z) for c in range(2)])


LINE = 4
RIGHT = [(0, 1), (1, 2), (2, 3)]
LEFT = [(1, 0), (2, 1), (3, 2)]
ACROSS = [(0, 2), (1, 3), (2, 0), (3, 1)]


def gather_kernel(n_z, place, own, *refs):
    *parts, out = refs
    z = place[1]
    out[z] = own[...]
    if n_z == LINE:
        right, left, across, far = parts
        out[z ^ 2] = across[...]

        @pl.when(z == 0)
        def _():
            out[1] = left[...]
            out[3] = far[...]

        @pl.when(z == n_z - 1)
        def _():
            out[2] = right[...]
            out[0] = far[...]

        @pl.when((z > 0) & (z < n_z - 1))
        def _():
            out[z - 1] = right[...]
            out[z + 1] = left[...]

    else:
        for s, part in enumerate(parts, 1):
            out[lax.rem(z + n_z - s, n_z)] = part[...]


def gather_z(place, own, n_z):
    if n_z == LINE:
        across = z_shift(own, ACROSS)
        parts = [z_shift(own, RIGHT), z_shift(own, LEFT), across, z_shift(across, [(2, 3), (1, 0)])]
    else:
        parts = [
            z_shift(own, [(a, (a + s) % n_z) for a in range(n_z)]) for s in range(1, n_z)
        ]
    return pl.pallas_call(
        functools.partial(gather_kernel, n_z),
        out_shape=shape((n_z,) + own.shape, own.dtype),
        in_specs=[whole(SMEM)] + [whole()] * (1 + len(parts)),
        out_specs=whole(),
        compiler_params=params(),
        cost_estimate=cost(0, own.size * 2 * 2 * n_z),
    )(place, own, *parts)


def reduce_z(place, mine, theirs):
    n_z = mine.shape[0]
    if n_z == LINE:
        picks = (
            lambda z, n: lax.rem(z + 1, n),
            lambda z, n: lax.rem(z + n - 1, n),
            lambda z, n: z ^ 2,
            lambda z, n: jnp.where(z == 0, n - 1, 0),
        )
        own, right, left, across, far = pair_sum(place, mine, theirs, picks)
        from_far = z_shift(far, [(3, 2), (0, 1)])
        from_left = z_shift(right, RIGHT)
        from_right = z_shift(left, LEFT)
        from_across = z_shift(add_all(across, from_far), ACROSS)
        return add_all(own, from_left, from_right, from_across)
    picks = tuple(lambda z, n, s=s: lax.rem(z + s, n) for s in range(1, n_z))
    own, *sends = pair_sum(place, mine, theirs, picks)
    got = [
        z_shift(part, [(a, (a + s) % n_z) for a in range(n_z)]) for s, part in enumerate(sends, 1)
    ]
    return add_all(own, *got)


def down_kernel(place, mine, theirs, grads, out, gate_factor, up_factor):
    core0 = place[0] == 0
    n_z, double, _ = mine.shape
    tok = double // 2
    gate, up = [], []
    for q in range(n_z):
        a, b = mine[q].astype(F32), theirs[q].astype(F32)
        first, second = jnp.where(core0, a, b), jnp.where(core0, b, a)
        gate += [first[:tok], second[:tok]]
        up += [first[tok:], second[tok:]]
    gate, up = jnp.concatenate(gate, 0), jnp.concatenate(up, 0)
    sig = 1.0 / (1.0 + jnp.exp(-gate))
    silu = gate * sig
    hidden = (silu * up).astype(BF16)
    gate_factor[...] = up * sig * (1.0 + gate * (1.0 - sig))
    up_factor[...] = silu
    out[...] = lax.dot_general(
        hidden, grads[...], (((0,), (0,)), ((), ())), preferred_element_type=F32
    ).astype(BF16)


def down_grad(place, mine, theirs, grads):
    n_z, double, ff = mine.shape
    tokens, chans = grads.shape
    t = tile_of(ff)
    rows = pl.BlockSpec((n_z, double, t), lambda i: (0, 0, i))
    cols = pl.BlockSpec((tokens, t), lambda i: (0, i))
    return pl.pallas_call(
        down_kernel,
        grid=(ff // t,),
        out_shape=(shape((ff, chans), BF16), shape((tokens, ff), F32), shape((tokens, ff), F32)),
        in_specs=[whole(SMEM), rows, rows, pl.BlockSpec((tokens, chans), lambda i: (0, 0))],
        out_specs=(pl.BlockSpec((t, chans), lambda i: (i, 0)), cols, cols),
        compiler_params=params(),
        cost_estimate=cost(2 * tokens * chans * ff, 2 * chans * ff + 8 * tokens * ff),
    )(place, mine, theirs, grads)


def input_kernel(n_t, place, mine, theirs, gate_factor, up_factor, w_gate, w_up, *refs):
    (gate_grad, up_grad), pieces_out, (hidden_grad, total) = refs[:2], refs[2 : 2 + n_t], refs[2 + n_t :]
    i, steps = pl.program_id(0), pl.num_programs(0)
    n_z, rows, width = mine.shape
    t = gate_grad.shape[1]

    @pl.when(i == 0)
    def _():
        core0 = place[0] == 0
        ff = hidden_grad.shape[0] * t
        low = ff - width
        for q in range(n_z):
            a, b = mine[q].astype(F32), theirs[q].astype(F32)
            line = jnp.concatenate([jnp.where(core0, a, b)[:, :low], jnp.where(core0, b, a)], 1)
            for k in range(ff // t):
                hidden_grad[k, q * rows : (q + 1) * rows, :] = line[:, k * t : (k + 1) * t]
        total[...] = jnp.zeros_like(total)

    hidden = hidden_grad[i]
    gate = (hidden * gate_factor[...]).astype(BF16)
    up = (hidden * up_factor[...]).astype(BF16)
    gate_grad[...] = gate
    up_grad[...] = up
    dims = (((1,), (1,)), ((), ()))
    term = lax.dot_general(gate, w_gate[...], dims, preferred_element_type=F32)
    term += lax.dot_general(up, w_up[...], dims, preferred_element_type=F32)
    total[...] += term.reshape(total.shape)

    @pl.when(i == steps - 1)
    def _():
        for s, out in enumerate(pieces_out):
            out[...] = total[place[2] ^ s].astype(out.dtype)


def input_grad(place, mine, theirs, gate_factor, up_factor, w_gate, w_up, n_t):
    tokens, ff = gate_factor.shape
    chans = w_gate.shape[0]
    t = tile_of(ff)
    rows = tokens // n_t
    cols = pl.BlockSpec((tokens, t), lambda i: (0, i))
    weight = pl.BlockSpec((chans, t), lambda i: (0, i))
    held = pl.BlockSpec(mine.shape, lambda i: (0, 0, 0))
    piece = pl.BlockSpec((rows, chans), lambda i: (0, 0))
    return pl.pallas_call(
        functools.partial(input_kernel, n_t),
        grid=(ff // t,),
        out_shape=(shape((tokens, ff), BF16),) * 2
        + (shape((rows, chans), F32),)
        + (shape((rows, chans), BF16),) * (n_t - 1),
        in_specs=[whole(SMEM), held, held, cols, cols, weight, weight],
        out_specs=(cols, cols) + (piece,) * n_t,
        scratch_shapes=[VMEM((ff // t, tokens, t), F32), VMEM((n_t, rows, chans), F32)],
        compiler_params=params(),
        cost_estimate=cost(4 * tokens * chans * ff, 4 * chans * ff + 12 * tokens * ff),
    )(place, mine, theirs, gate_factor, up_factor, w_gate, w_up)


def weight_kernel(inputs_t, gate_grad, up_grad, gate_out, up_out):
    for grad, out in ((gate_grad, gate_out), (up_grad, up_out)):
        out[...] = lax.dot_general(
            inputs_t[...], grad[...], (((1,), (0,)), ((), ())), preferred_element_type=F32
        ).astype(BF16)


def weight_grads(inputs_t, gate_grad, up_grad):
    chans, tokens = inputs_t.shape
    ff = gate_grad.shape[1]
    t = tile_of(ff)
    cols = pl.BlockSpec((tokens, t), lambda i: (0, i))
    weight = pl.BlockSpec((chans, t), lambda i: (0, i))
    return pl.pallas_call(
        weight_kernel,
        grid=(ff // t,),
        out_shape=(shape((chans, ff), BF16),) * 2,
        in_specs=[pl.BlockSpec((chans, tokens), lambda i: (0, 0)), cols, cols],
        out_specs=(weight, weight),
        compiler_params=params(),
        cost_estimate=cost(4 * tokens * chans * ff, 4 * chans * ff + 4 * tokens * ff),
    )(inputs_t, gate_grad, up_grad)


def on_device(n_z, n_t, xq, xs, xo, xc, gq, gs, go, gc, gate_pre, up_pre, w_gate, w_up, w_down):
    dp = lax.axis_index("dp")
    place = jnp.stack([dp % 2, dp // 2, lax.axis_index("tensor")]).astype(jnp.int32)
    ff = gate_pre.shape[1]
    width = -(-ff // 256) * 128

    def to_tensor(value, s):
        return lax.ppermute(value, "tensor", [(a, a ^ s) for a in range(n_t)])

    own, gate_up = prep(xq, xs, xo, xc, gq, gs, go, gc, gate_pre, up_pre)
    parts = [own] + [to_tensor(own, s) for s in range(1, n_t)]
    gate_up = gather_z(place, gate_up, n_z)
    grads, inputs_t, send = first_half(place, parts, w_down, n_z, width)
    got = swap_cores(send, n_z)
    mine = second_half(place, grads, w_down, n_z, width)
    hidden_grad = gather_z(place, reduce_z(place, mine, got), n_z)
    grad_down, gate_factor, up_factor = down_grad(place, gate_up, swap_cores(gate_up, n_z), grads)
    gate_grad, up_grad, kept, *sends = input_grad(
        place, hidden_grad, swap_cores(hidden_grad, n_z), gate_factor, up_factor, w_gate, w_up, n_t
    )
    terms = [to_tensor(part, s) for s, part in enumerate(sends, 1)]
    grad_gate, grad_up = weight_grads(inputs_t, gate_grad, up_grad)
    return add_all(kept, *terms), grad_gate, grad_up, grad_down


def solution(mesh):
    n_z, n_t = mesh.shape["dp"] // 2, mesh.shape["tensor"]
    by_token, by_dp = P("tensor", "dp"), P("dp", "tensor")
    return jax.shard_map(
        functools.partial(on_device, n_z, n_t),
        mesh=mesh,
        in_specs=(by_token,) * 8 + (by_dp,) * 4 + (by_token,),
        out_specs=(by_token, by_dp, by_dp, by_token),
        check_vma=False,
    )
```

```python
import functools

import jax
import jax.numpy as jnp
from jax import lax
from jax.experimental import pallas as pl
from jax.experimental.pallas import tpu as pltpu
from jax.sharding import Mesh
from jax.sharding import PartitionSpec as P

BLK_C = 128
F32 = jnp.float32
BF16 = jnp.bfloat16
VMEM = pltpu.VMEM
SMEM = pltpu.SMEM


def whole(space=VMEM):
    return pl.BlockSpec(memory_space=space)


def shape(dims, dtype):
    return jax.ShapeDtypeStruct(dims, dtype)


def params(mib=56):
    return pltpu.CompilerParams(vmem_limit_bytes=mib * 1024 * 1024)


def cost(flops, nbytes):
    return pl.CostEstimate(flops=int(flops), bytes_accessed=int(nbytes), transcendentals=0)


def pieces(extent, step):
    return [(at, min(step, extent - at)) for at in range(0, extent, step)]


def prep_kernel(xq, xs, xo, xc, gq, gs, go, gc, gate, up, xg, gu):
    for at, (quant, scale, flag, corr) in enumerate(((gq, gs, go, gc), (xq, xs, xo, xc))):
        for b in range(scale.shape[1]):
            cols = slice(b * BLK_C, (b + 1) * BLK_C)
            value = scale[0, b] * quant[:, cols].astype(F32) + flag[0, b].astype(F32) * corr[
                :, cols
            ].astype(F32)
            xg[at, :, cols] = value.astype(BF16)
    gu[...] = jnp.concatenate([gate[...].astype(F32), up[...].astype(F32)], 0).astype(BF16)


def prep(xq, xs, xo, xc, gq, gs, go, gc, gate, up):
    rows, width = xq.shape
    tok, ff = gate.shape
    return pl.pallas_call(
        prep_kernel,
        out_shape=(shape((2, rows, width), BF16), shape((2 * tok, ff), BF16)),
        in_specs=[whole(), whole(SMEM), whole(SMEM), whole()] * 2 + [whole()] * 2,
        out_specs=(whole(), whole()),
        compiler_params=params(),
        cost_estimate=cost(0, 4 * xq.size * 2 + gate.size * 8),
    )(xq, xs, xo, xc, gq, gs, go, gc, gate, up)


def load_down(start, width, w_hbm, w_vmem, sems):
    copies = []
    for k, (at, size) in enumerate(pieces(width, 256)):
        first = pl.multiple_of(start + at, 16)
        copy = pltpu.make_async_copy(
            w_hbm.at[pl.ds(first, size)], w_vmem.at[pl.ds(at, size)], sems.at[k]
        )
        copy.start()
        copies.append(copy)
    return copies


def hidden_half(copies, grads_t, width, w_vmem, out):
    groups, rows = out.shape[0], out.shape[1]
    for copy, (at, size) in zip(copies, pieces(width, 256)):
        copy.wait()
        total = jnp.dot(w_vmem[at : at + size, :], grads_t, preferred_element_type=F32).T
        for q in range(groups):
            out[q, :, at : at + size] = total[q * rows : (q + 1) * rows, :].astype(out.dtype)


def first_half_kernel(n_t, offset, place, *refs):
    parts, (w_hbm, grads_out, grads_t, inputs_t, out, w_vmem, held, sems) = refs[:n_t], refs[n_t:]
    core, me = place[0], place[2]
    width = out.shape[2]
    copies = load_down((1 - core) * offset, width, w_hbm, w_vmem, sems)
    rows = held.shape[1]
    for s in range(n_t):
        held[me ^ s] = parts[s][1].astype(F32)
    inputs_t[...] = held[...].reshape(n_t * rows, held.shape[2]).T.astype(BF16)
    for s in range(n_t):
        held[me ^ s] = parts[s][0].astype(F32)
    grads = held[...].reshape(n_t * rows, held.shape[2])
    grads_out[...] = grads.astype(BF16)
    grads_t[...] = grads.T.astype(BF16)
    hidden_half(copies, grads_t[...], width, w_vmem, out)


def second_half_kernel(offset, place, grads_t, w_hbm, out, w_vmem, sems):
    width = out.shape[2]
    copies = load_down(place[0] * offset, width, w_hbm, w_vmem, sems)
    hidden_half(copies, grads_t[...], width, w_vmem, out)


def first_half(place, parts, w_down, n_z, width):
    n_t, rows, chans = len(parts), parts[0].shape[1], parts[0].shape[2]
    tokens = n_t * rows
    n_copies = len(pieces(width, 256))
    return pl.pallas_call(
        functools.partial(first_half_kernel, n_t, w_down.shape[0] - width),
        out_shape=(
            shape((tokens, chans), BF16),
            shape((chans, tokens), BF16),
            shape((chans, tokens), BF16),
            shape((n_z, tokens // n_z, width), BF16),
        ),
        in_specs=[whole(SMEM)] + [whole()] * n_t + [whole(pl.ANY)],
        out_specs=(whole(),) * 4,
        scratch_shapes=[
            VMEM((width, chans), BF16),
            VMEM((n_t, rows, chans), F32),
            pltpu.SemaphoreType.DMA((n_copies,)),
        ],
        compiler_params=params(),
        cost_estimate=cost(2 * tokens * chans * width, 2 * chans * width),
    )(place, *parts, w_down)


def second_half(place, grads_t, w_down, n_z, width):
    chans, tokens = grads_t.shape
    n_copies = len(pieces(width, 256))
    return pl.pallas_call(
        functools.partial(second_half_kernel, w_down.shape[0] - width),
        out_shape=shape((n_z, tokens // n_z, width), F32),
        in_specs=[whole(SMEM), whole(), whole(pl.ANY)],
        out_specs=whole(),
        scratch_shapes=[VMEM((width, chans), BF16), pltpu.SemaphoreType.DMA((n_copies,))],
        compiler_params=params(),
        cost_estimate=cost(2 * tokens * chans * width, 2 * chans * width),
    )(place, grads_t, w_down)


def pair_kernel(mine, theirs, out):
    out[...] = (mine[...] + theirs[...].astype(F32)).astype(BF16)


def pair_sum(mine, theirs):
    return pl.pallas_call(
        pair_kernel,
        out_shape=shape(mine.shape, BF16),
        in_specs=[whole(), whole()],
        out_specs=whole(),
        compiler_params=params(),
        cost_estimate=cost(0, mine.size * 8),
    )(mine, theirs)


def spread_kernel(parts, out):
    total = parts[0].astype(F32)
    for q in range(1, parts.shape[0]):
        total = total + parts[q].astype(F32)
    for q in range(parts.shape[0]):
        out[q] = total.astype(BF16)


def spread_sum(parts):
    return pl.pallas_call(
        spread_kernel,
        out_shape=shape(parts.shape, BF16),
        in_specs=[whole()],
        out_specs=whole(),
        compiler_params=params(),
        cost_estimate=cost(0, parts.size * 4),
    )(parts)


def add_kernel(*refs):
    *terms, out = refs
    total = terms[0][...].astype(F32)
    for term in terms[1:]:
        total = total + term[...].astype(F32)
    out[...] = total.astype(out.dtype)


def add_all(*terms):
    return pl.pallas_call(
        add_kernel,
        out_shape=shape(terms[0].shape, BF16),
        in_specs=[whole()] * len(terms),
        out_specs=whole(),
        compiler_params=params(),
        cost_estimate=cost(0, terms[0].size * 2 * (len(terms) + 2)),
    )(*terms)


def down_kernel(place, mine, theirs, grads, out_hbm, gate_factor, up_factor, out, sems):
    core0 = place[0] == 0
    n_z, double, ff = mine.shape
    tok = double // 2
    copies = []
    for k, (at, size) in enumerate(pieces(ff, 512)):
        cols = slice(at, at + size)
        gate, up = [], []
        for q in range(n_z):
            a, b = mine[q, :, cols].astype(F32), theirs[q, :, cols].astype(F32)
            first, second = jnp.where(core0, a, b), jnp.where(core0, b, a)
            gate += [first[:tok], second[:tok]]
            up += [first[tok:], second[tok:]]
        gate, up = jnp.concatenate(gate, 0), jnp.concatenate(up, 0)
        sig = 1.0 / (1.0 + jnp.exp(-gate))
        silu = gate * sig
        hidden = silu * up
        gate_factor[:, cols] = up * sig * (1.0 + gate * (1.0 - sig))
        up_factor[:, cols] = silu
        out[cols, :] = jnp.dot(
            hidden.T.astype(BF16), grads[...], preferred_element_type=F32
        ).astype(BF16)
        copy = pltpu.make_async_copy(out.at[cols], out_hbm.at[cols], sems.at[k])
        copy.start()
        copies.append(copy)
    for copy in copies:
        copy.wait()


def down_grad(place, mine, theirs, grads):
    n_z, double, ff = mine.shape
    tokens, chans = grads.shape
    return pl.pallas_call(
        down_kernel,
        out_shape=(shape((ff, chans), BF16), shape((tokens, ff), F32), shape((tokens, ff), F32)),
        in_specs=[whole(SMEM)] + [whole()] * 3,
        out_specs=(whole(pl.ANY), whole(), whole()),
        scratch_shapes=[
            VMEM((ff, chans), BF16), pltpu.SemaphoreType.DMA((len(pieces(ff, 512)),))
        ],
        compiler_params=params(),
        cost_estimate=cost(2 * tokens * chans * ff, 2 * chans * ff + 8 * tokens * ff),
    )(place, mine, theirs, grads)


def input_kernel(n_t, place, mine, theirs, gate_factor, up_factor, gate_hbm, up_hbm, *refs):
    (gate_grad, up_grad), pieces_out = refs[:2], refs[2 : 2 + n_t]
    w_gate, w_up, total, held, sems = refs[2 + n_t :]
    core0 = place[0] == 0
    n_z, rows, width = mine.shape
    ff = gate_grad.shape[1]
    low = ff - width
    parts = [(0, at, size) for at, size in pieces(low, 512)]
    parts += [(low, at, size) for at, size in pieces(width, 512)]
    copies = []
    for k, (base, at, size) in enumerate(parts):
        cols = slice(base + at, base + at + size)
        pair = [
            pltpu.make_async_copy(hbm.at[:, cols], vmem.at[:, cols], sems.at[n, k])
            for n, (hbm, vmem) in enumerate(((gate_hbm, w_gate), (up_hbm, w_up)))
        ]
        for copy in pair:
            copy.start()
        copies.append(pair)
    dims = (((1,), (1,)), ((), ()))
    for k, (base, at, size) in enumerate(parts):
        cols = slice(base + at, base + at + size)
        first = core0 if base == 0 else ~core0
        hidden = jnp.concatenate(
            [
                jnp.where(first, mine[q, :, at : at + size], theirs[q, :, at : at + size]).astype(F32)
                for q in range(n_z)
            ],
            0,
        )
        gate = (hidden * gate_factor[:, cols]).astype(BF16)
        up = (hidden * up_factor[:, cols]).astype(BF16)
        gate_grad[:, cols] = gate
        up_grad[:, cols] = up
        for copy in copies[k]:
            copy.wait()
        term = lax.dot_general(w_gate[:, cols], gate, dims, preferred_element_type=F32)
        term += lax.dot_general(w_up[:, cols], up, dims, preferred_element_type=F32)
        total[...] = term if k == 0 else total[...] + term
    held[...] = total[...].T.reshape(held.shape)
    for s, out in enumerate(pieces_out):
        out[...] = held[place[2] ^ s].astype(out.dtype)


def input_grad(place, mine, theirs, gate_factor, up_factor, w_gate, w_up, n_t):
    tokens, ff = gate_factor.shape
    chans = w_gate.shape[0]
    rows, width = tokens // n_t, mine.shape[2]
    n_copies = len(pieces(ff - width, 512)) + len(pieces(width, 512))
    return pl.pallas_call(
        functools.partial(input_kernel, n_t),
        out_shape=(shape((tokens, ff), BF16),) * 2
        + (shape((rows, chans), F32),)
        + (shape((rows, chans), BF16),) * (n_t - 1),
        in_specs=[whole(SMEM)] + [whole()] * 4 + [whole(pl.ANY)] * 2,
        out_specs=(whole(),) * (2 + n_t),
        scratch_shapes=[
            VMEM((chans, ff), BF16),
            VMEM((chans, ff), BF16),
            VMEM((chans, tokens), F32),
            VMEM((n_t, rows, chans), F32),
            pltpu.SemaphoreType.DMA((2, n_copies)),
        ],
        compiler_params=params(),
        cost_estimate=cost(4 * tokens * chans * ff, 4 * chans * ff + 12 * tokens * ff),
    )(place, mine, theirs, gate_factor, up_factor, w_gate, w_up)


def weight_kernel(inputs_t, gate_grad, up_grad, gate_hbm, up_hbm, gate_out, up_out, sems):
    copies = []
    ff = gate_grad.shape[1]
    for n, (grad, out, hbm) in enumerate(
        ((gate_grad, gate_out, gate_hbm), (up_grad, up_out, up_hbm))
    ):
        for k, (at, size) in enumerate(pieces(ff, 512)):
            cols = slice(at, at + size)
            out[:, cols] = jnp.dot(
                inputs_t[...], grad[:, cols], preferred_element_type=F32
            ).astype(BF16)
            copy = pltpu.make_async_copy(out.at[:, cols], hbm.at[:, cols], sems.at[n, k])
            copy.start()
            copies.append(copy)
    for copy in copies:
        copy.wait()


def weight_grads(inputs_t, gate_grad, up_grad):
    chans, tokens = inputs_t.shape
    ff = gate_grad.shape[1]
    return pl.pallas_call(
        weight_kernel,
        out_shape=(shape((chans, ff), BF16),) * 2,
        in_specs=[whole()] * 3,
        out_specs=(whole(pl.ANY),) * 2,
        scratch_shapes=[VMEM((chans, ff), BF16)] * 2
        + [pltpu.SemaphoreType.DMA((2, len(pieces(ff, 512))))],
        compiler_params=params(),
        cost_estimate=cost(4 * tokens * chans * ff, 4 * chans * ff + 4 * tokens * ff),
    )(inputs_t, gate_grad, up_grad)


def on_device(n_z, n_t, xq, xs, xo, xc, gq, gs, go, gc, gate_pre, up_pre, w_gate, w_up, w_down):
    place = jnp.stack([lax.axis_index(name) for name in ("core", "z", "tensor")]).astype(jnp.int32)
    ff = gate_pre.shape[1]
    width = -(-ff // 256) * 128

    def to_tensor(value, s):
        return lax.ppermute(value, "tensor", [(a, a ^ s) for a in range(n_t)])

    def to_core(value):
        return lax.ppermute(value, "core", [(0, 1), (1, 0)])

    def to_chips(value):
        return lax.all_to_all(value, "z", 0, 0, tiled=True)

    own, gate_up = prep(xq, xs, xo, xc, gq, gs, go, gc, gate_pre, up_pre)
    parts = [own] + [to_tensor(own, s) for s in range(1, n_t)]
    gate_up = lax.all_gather(gate_up, "z")
    grads, grads_t, inputs_t, send = first_half(place, parts, w_down, n_z, width)
    got = to_core(send)
    mine = second_half(place, grads_t, w_down, n_z, width)
    hidden_grad = to_chips(spread_sum(to_chips(pair_sum(mine, got))))
    grad_down, gate_factor, up_factor = down_grad(place, gate_up, to_core(gate_up), grads)
    gate_grad, up_grad, kept, *sends = input_grad(
        place, hidden_grad, to_core(hidden_grad), gate_factor, up_factor, w_gate, w_up, n_t
    )
    terms = [to_tensor(part, s) for s, part in enumerate(sends, 1)]
    grad_gate, grad_up = weight_grads(inputs_t, gate_grad, up_grad)
    return add_all(kept, *terms), grad_gate, grad_up, grad_down


def solution(mesh):
    n_dp, n_t = mesh.shape["dp"], mesh.shape["tensor"]
    fine = Mesh(mesh.devices.reshape(n_dp // 2, 2, n_t), ("z", "core", "tensor"))
    by_token, by_dp = P("tensor", ("z", "core")), P(("z", "core"), "tensor")
    return jax.shard_map(
        functools.partial(on_device, n_dp // 2, n_t),
        mesh=fine,
        in_specs=(by_token,) * 8 + (by_dp,) * 4 + (by_token,),
        out_specs=(by_token, by_dp, by_dp, by_token),
        check_vma=False,
    )
```

```python
import functools
import math

import jax
import jax.numpy as jnp
from jax import lax
from jax.experimental import pallas as pl
from jax.experimental.pallas import tpu as pltpu
from jax.sharding import Mesh
from jax.sharding import PartitionSpec as P

BLK_C = 128
F32 = jnp.float32
BF16 = jnp.bfloat16
VMEM = pltpu.VMEM
SMEM = pltpu.SMEM


def whole(space=VMEM):
    return pl.BlockSpec(memory_space=space)


def shape(dims, dtype):
    return jax.ShapeDtypeStruct(dims, dtype)


def params(mib):
    return pltpu.CompilerParams(vmem_limit_bytes=mib * 1024 * 1024)


def cost(flops, nbytes):
    return pl.CostEstimate(flops=int(flops), bytes_accessed=int(nbytes), transcendentals=0)


def pieces(extent, step, first=0):
    cuts = [0] + list(range(first or step, extent, step)) + [extent]
    return [(a, b - a) for a, b in zip(cuts[:-1], cuts[1:])]


def prep_kernel(xq, xs, xo, xc, gq, gs, go, gc, gate, up, xg, gu):
    for at, (quant, scale, flag, corr) in enumerate(((gq, gs, go, gc), (xq, xs, xo, xc))):
        for b in range(scale.shape[1]):
            cols = slice(b * BLK_C, (b + 1) * BLK_C)
            value = scale[0, b] * quant[:, cols].astype(F32) + flag[0, b].astype(F32) * corr[
                :, cols
            ].astype(F32)
            for q in range(xg.shape[0]):
                xg[q, at, :, cols] = value.astype(BF16)
    gu[...] = jnp.concatenate([gate[...].astype(F32), up[...].astype(F32)], 0).astype(BF16)


def prep(n_t, xq, xs, xo, xc, gq, gs, go, gc, gate, up):
    rows, width = xq.shape
    tok, ff = gate.shape
    return pl.pallas_call(
        prep_kernel,
        out_shape=(shape((n_t, 2, rows, width), BF16), shape((2 * tok, ff), BF16)),
        in_specs=[whole(), whole(SMEM), whole(SMEM), whole()] * 2 + [whole()] * 2,
        out_specs=(whole(), whole()),
        compiler_params=params(4),
        cost_estimate=cost(0, 4 * xq.size * 2 + gate.size * 8),
    )(xq, xs, xo, xc, gq, gs, go, gc, gate, up)


def load_down(start, width, w_hbm, w_vmem, sems):
    copies = []
    for k, (at, size) in enumerate(pieces(width, 1024, 256)):
        first = pl.multiple_of(start + at, 16)
        copy = pltpu.make_async_copy(
            w_hbm.at[pl.ds(first, size)], w_vmem.at[pl.ds(at, size)], sems.at[k]
        )
        copy.start()
        copies.append(copy)
    return copies


def hidden_half(copies, grads_t, width, w_vmem, out):
    groups, rows = out.shape[0], out.shape[1]
    for copy, (at, size) in zip(copies, pieces(width, 1024, 256)):
        copy.wait()
        total = jnp.dot(w_vmem[at : at + size, :], grads_t, preferred_element_type=F32).T
        for q in range(groups):
            out[q, :, at : at + size] = total[q * rows : (q + 1) * rows, :].astype(out.dtype)


def first_half_kernel(offset, place, parts, w_hbm, grads_out, grads_t, inputs_t, out, w_vmem, held, sems):
    core, z = place[0], place[1]
    n_t, rows = parts.shape[0], parts.shape[2]
    n_z, block, width = out.shape
    copies = load_down((1 - core) * offset, width, w_hbm, w_vmem, sems)

    def blocks():
        return jnp.concatenate(
            [held[pl.ds(pl.multiple_of((z ^ m) * block, math.gcd(block, 8)), block), :] for m in range(n_z)], 0
        )

    for p in range(n_t):
        held[p * rows : (p + 1) * rows, :] = parts[p, 0].astype(F32)
    grads_t[...] = held[...].T.astype(BF16)
    grads_out[...] = blocks().astype(BF16)
    for p in range(n_t):
        held[p * rows : (p + 1) * rows, :] = parts[p, 1].astype(F32)
    inputs_t[...] = blocks().T.astype(BF16)
    hidden_half(copies, grads_t[...], width, w_vmem, out)


def second_half_kernel(offset, place, grads_t, w_hbm, out, w_vmem, sems):
    width = out.shape[2]
    copies = load_down(place[0] * offset, width, w_hbm, w_vmem, sems)
    hidden_half(copies, grads_t[...], width, w_vmem, out)


def first_half(place, parts, w_down, n_z, width):
    n_t, _, rows, chans = parts.shape
    tokens = n_t * rows
    n_copies = len(pieces(width, 1024, 256))
    return pl.pallas_call(
        functools.partial(first_half_kernel, w_down.shape[0] - width),
        out_shape=(
            shape((tokens, chans), BF16),
            shape((chans, tokens), BF16),
            shape((chans, tokens), BF16),
            shape((n_z, tokens // n_z, width), BF16),
        ),
        in_specs=[whole(SMEM), whole(), whole(pl.ANY)],
        out_specs=(whole(),) * 4,
        scratch_shapes=[
            VMEM((width, chans), BF16),
            VMEM((tokens, chans), F32),
            pltpu.SemaphoreType.DMA((n_copies,)),
        ],
        compiler_params=params(13),
        cost_estimate=cost(2 * tokens * chans * width, 2 * chans * width),
    )(place, parts, w_down)


def second_half(place, grads_t, w_down, n_z, width):
    chans, tokens = grads_t.shape
    n_copies = len(pieces(width, 1024, 256))
    return pl.pallas_call(
        functools.partial(second_half_kernel, w_down.shape[0] - width),
        out_shape=shape((n_z, tokens // n_z, width), F32),
        in_specs=[whole(SMEM), whole(), whole(pl.ANY)],
        out_specs=whole(),
        scratch_shapes=[VMEM((width, chans), BF16), pltpu.SemaphoreType.DMA((n_copies,))],
        compiler_params=params(13),
        cost_estimate=cost(2 * tokens * chans * width, 2 * chans * width),
    )(place, grads_t, w_down)


def pair_kernel(place, mine, theirs, *outs):
    for m, out in enumerate(outs):
        at = place[1] ^ m
        out[...] = (mine[at] + theirs[at].astype(F32)).astype(out.dtype)


def pair_sum(place, mine, theirs):
    n_z, rows, width = mine.shape
    return pl.pallas_call(
        pair_kernel,
        out_shape=tuple(shape((rows, width), BF16 if m % 2 else F32) for m in range(n_z)),
        in_specs=[whole(SMEM), whole(), whole()],
        out_specs=(whole(),) * n_z,
        compiler_params=params(5),
        cost_estimate=cost(0, mine.size * 9),
    )(place, mine, theirs)


def add_kernel(*refs):
    *terms, out = refs
    total = terms[0][...].astype(F32)
    for term in terms[1:]:
        total = total + term[...].astype(F32)
    out[...] = total.astype(out.dtype)


def add_all(*terms):
    return pl.pallas_call(
        add_kernel,
        out_shape=shape(terms[0].shape, BF16),
        in_specs=[whole()] * len(terms),
        out_specs=whole(),
        compiler_params=params(3),
        cost_estimate=cost(0, terms[0].size * 2 * (len(terms) + 2)),
    )(*terms)


def sum_kernel(parts, out):
    total = parts[0].astype(F32)
    for p in range(1, parts.shape[0]):
        total = total + parts[p].astype(F32)
    out[...] = total.astype(BF16)


def sum_parts(parts):
    return pl.pallas_call(
        sum_kernel,
        out_shape=shape(parts.shape[1:], BF16),
        in_specs=[whole()],
        out_specs=whole(),
        compiler_params=params(3),
        cost_estimate=cost(0, parts.size * 3),
    )(parts)


def to_chip(value, bit, n_z):
    return lax.ppermute(value, "z", [(a, a ^ bit) for a in range(n_z)])


def to_core(value):
    return lax.ppermute(value, "core", [(0, 1), (1, 0)])


def gather_z(own, n_z):
    held = {0: own}
    bit = n_z // 2
    while bit:
        held.update({m | bit: to_chip(part, bit, n_z) for m, part in held.items()})
        bit //= 2
    return [held[m] for m in range(n_z)]


def reduce_z(terms):
    n_z = len(terms)
    held = {m: [term] for m, term in enumerate(terms)}
    bit = 1
    while bit < n_z:
        for m in sorted((m for m in held if m & bit), reverse=True):
            mine = held.pop(m)
            term = add_all(*mine) if len(mine) > 1 else mine[0].astype(BF16)
            held[m ^ bit].append(to_chip(term, bit, n_z))
        bit *= 2
    return add_all(*held[0])


def down_kernel(n_z, place, *refs):
    mine, theirs = refs[:n_z], refs[n_z : 2 * n_z]
    grads, out_hbm, gate_factor, up_factor, out, sems = refs[2 * n_z :]
    core0 = place[0] == 0
    double, ff = mine[0].shape
    tok = double // 2
    copies = []
    for k, (at, size) in enumerate(pieces(ff, 512)):
        cols, slot = slice(at, at + size), k % out.shape[0]
        gate, up = [], []
        for m in range(n_z):
            a, b = mine[m][:, cols].astype(F32), theirs[m][:, cols].astype(F32)
            first, second = jnp.where(core0, a, b), jnp.where(core0, b, a)
            gate += [first[:tok], second[:tok]]
            up += [first[tok:], second[tok:]]
        gate, up = jnp.concatenate(gate, 0), jnp.concatenate(up, 0)
        sig = 1.0 / (1.0 + jnp.exp(-gate))
        silu = gate * sig
        hidden = silu * up
        gate_factor[:, cols] = up * sig * (1.0 + gate * (1.0 - sig))
        up_factor[:, cols] = silu
        if k >= out.shape[0]:
            copies[k - out.shape[0]].wait()
        out[slot, :size, :] = jnp.dot(
            hidden.T.astype(BF16), grads[...], preferred_element_type=F32
        ).astype(BF16)
        copy = pltpu.make_async_copy(out.at[slot, :size], out_hbm.at[cols], sems.at[slot])
        copy.start()
        copies.append(copy)
    for copy in copies[-out.shape[0] :]:
        copy.wait()


def down_grad(place, mine, theirs, grads):
    n_z, (_, ff) = len(mine), mine[0].shape
    tokens, chans = grads.shape
    slots = min(4, len(pieces(ff, 512)))
    return pl.pallas_call(
        functools.partial(down_kernel, n_z),
        out_shape=(shape((ff, chans), BF16), shape((tokens, ff), F32), shape((tokens, ff), F32)),
        in_specs=[whole(SMEM)] + [whole()] * (2 * n_z + 1),
        out_specs=(whole(pl.ANY), whole(), whole()),
        scratch_shapes=[VMEM((slots, 512, chans), BF16), pltpu.SemaphoreType.DMA((slots,))],
        compiler_params=params(18),
        cost_estimate=cost(2 * tokens * chans * ff, 2 * chans * ff + 8 * tokens * ff),
    )(place, *mine, *theirs, grads)


def input_kernel(n_z, place, *refs):
    mine, theirs = refs[:n_z], refs[n_z : 2 * n_z]
    gate_factor, up_factor, gate_hbm, up_hbm = refs[2 * n_z : 2 * n_z + 4]
    gate_grad, up_grad, out, w_gate, w_up, total, held, sems = refs[2 * n_z + 4 :]
    core0, z = place[0] == 0, place[1]
    rows, width = mine[0].shape
    ff = gate_grad.shape[1]
    low = ff - width
    slots = w_gate.shape[0]
    parts = [(0, at, size) for at, size in pieces(low, 1024, 256)]
    parts += [(low, at, size) for at, size in pieces(width, 1024)]

    def copies(k):
        base, at, size = parts[k]
        return [
            pltpu.make_async_copy(
                hbm.at[:, base + at : base + at + size],
                vmem.at[k % slots, :, :size],
                sems.at[n, k % slots],
            )
            for n, (hbm, vmem) in enumerate(((gate_hbm, w_gate), (up_hbm, w_up)))
        ]

    for k in range(min(slots, len(parts))):
        for copy in copies(k):
            copy.start()
    dims = (((1,), (1,)), ((), ()))
    for k, (base, at, size) in enumerate(parts):
        cols = slice(base + at, base + at + size)
        first = core0 if base == 0 else ~core0
        hidden = jnp.concatenate(
            [
                jnp.where(first, mine[m][:, at : at + size], theirs[m][:, at : at + size]).astype(F32)
                for m in range(n_z)
            ],
            0,
        )
        gate = (hidden * gate_factor[:, cols]).astype(BF16)
        up = (hidden * up_factor[:, cols]).astype(BF16)
        gate_grad[:, cols] = gate
        up_grad[:, cols] = up
        for copy in copies(k):
            copy.wait()
        slot = k % slots
        term = lax.dot_general(w_gate[slot, :, :size], gate, dims, preferred_element_type=F32)
        term += lax.dot_general(w_up[slot, :, :size], up, dims, preferred_element_type=F32)
        total[...] = term if k == 0 else total[...] + term
        if k + slots < len(parts):
            for copy in copies(k + slots):
                copy.start()
    turned = total[...].T
    for m in range(n_z):
        held[pl.ds(pl.multiple_of((z ^ m) * rows, math.gcd(rows, 8)), rows), :] = turned[m * rows : (m + 1) * rows]
    n_t = out.shape[0]
    step = held.shape[0] // n_t
    for p in range(n_t):
        out[p] = held[p * step : (p + 1) * step, :].astype(BF16)


def input_grad(place, mine, theirs, gate_factor, up_factor, w_gate, w_up, n_t):
    tokens, ff = gate_factor.shape
    chans = w_gate.shape[0]
    n_z, slots = len(mine), 3
    return pl.pallas_call(
        functools.partial(input_kernel, n_z),
        out_shape=(shape((tokens, ff), BF16),) * 2 + (shape((n_t, tokens // n_t, chans), BF16),),
        in_specs=[whole(SMEM)] + [whole()] * (2 * n_z + 2) + [whole(pl.ANY)] * 2,
        out_specs=(whole(),) * 3,
        scratch_shapes=[
            VMEM((slots, chans, min(ff, 1024)), BF16),
            VMEM((slots, chans, min(ff, 1024)), BF16),
            VMEM((chans, tokens), F32),
            VMEM((tokens, chans), F32),
            pltpu.SemaphoreType.DMA((2, slots)),
        ],
        compiler_params=params(28),
        cost_estimate=cost(4 * tokens * chans * ff, 4 * chans * ff + 12 * tokens * ff),
    )(place, *mine, *theirs, gate_factor, up_factor, w_gate, w_up)


def weight_kernel(inputs_t, gate_grad, up_grad, gate_hbm, up_hbm, out, sems):
    copies = []
    ff, slots = gate_grad.shape[1], out.shape[0]
    for grad, hbm in ((gate_grad, gate_hbm), (up_grad, up_hbm)):
        for at, size in pieces(ff, 512):
            cols, slot = slice(at, at + size), len(copies) % slots
            if len(copies) >= slots:
                copies[len(copies) - slots].wait()
            out[slot, :, :size] = jnp.dot(
                inputs_t[...], grad[:, cols], preferred_element_type=F32
            ).astype(BF16)
            copy = pltpu.make_async_copy(out.at[slot, :, :size], hbm.at[:, cols], sems.at[slot])
            copy.start()
            copies.append(copy)
    for copy in copies[-slots:]:
        copy.wait()


def weight_grads(inputs_t, gate_grad, up_grad):
    chans, tokens = inputs_t.shape
    ff = gate_grad.shape[1]
    slots = min(8, 2 * len(pieces(ff, 512)))
    return pl.pallas_call(
        weight_kernel,
        out_shape=(shape((chans, ff), BF16),) * 2,
        in_specs=[whole()] * 3,
        out_specs=(whole(pl.ANY),) * 2,
        scratch_shapes=[VMEM((slots, chans, 512), BF16), pltpu.SemaphoreType.DMA((slots,))],
        compiler_params=params(16),
        cost_estimate=cost(4 * tokens * chans * ff, 4 * chans * ff + 4 * tokens * ff),
    )(inputs_t, gate_grad, up_grad)


def on_device(n_z, n_t, xq, xs, xo, xc, gq, gs, go, gc, gate_pre, up_pre, w_gate, w_up, w_down):
    place = jnp.stack([lax.axis_index(name) for name in ("core", "z", "tensor")]).astype(jnp.int32)
    ff = gate_pre.shape[1]
    width = -(-ff // 256) * 128

    def exchange(value):
        return lax.all_to_all(value, "tensor", 0, 0, tiled=True)

    own, gate_up = prep(n_t, xq, xs, xo, xc, gq, gs, go, gc, gate_pre, up_pre)
    parts = exchange(own)
    gate_up = gather_z(gate_up, n_z)
    grads, grads_t, inputs_t, send = first_half(place, parts, w_down, n_z, width)
    got = to_core(send)
    mine = second_half(place, grads_t, w_down, n_z, width)
    hidden_grad = gather_z(reduce_z(pair_sum(place, mine, got)), n_z)
    grad_down, gate_factor, up_factor = down_grad(
        place, gate_up, [to_core(part) for part in gate_up], grads
    )
    gate_grad, up_grad, sends = input_grad(
        place, hidden_grad, [to_core(part) for part in hidden_grad],
        gate_factor, up_factor, w_gate, w_up, n_t,
    )
    terms = exchange(sends)
    grad_gate, grad_up = weight_grads(inputs_t, gate_grad, up_grad)
    return sum_parts(terms), grad_gate, grad_up, grad_down


def solution(mesh):
    n_dp, n_t = mesh.shape["dp"], mesh.shape["tensor"]
    fine = Mesh(mesh.devices.reshape(n_dp // 2, 2, n_t), ("z", "core", "tensor"))
    by_token, by_dp = P("tensor", ("z", "core")), P(("z", "core"), "tensor")
    return jax.shard_map(
        functools.partial(on_device, n_dp // 2, n_t),
        mesh=fine,
        in_specs=(by_token,) * 8 + (by_dp,) * 4 + (by_token,),
        out_specs=(by_token, by_dp, by_dp, by_token),
        check_vma=False,
    )
```

```python
import functools
import math

import jax
import jax.numpy as jnp
from jax import lax
from jax.experimental import pallas as pl
from jax.experimental.pallas import tpu as pltpu
from jax.sharding import Mesh
from jax.sharding import PartitionSpec as P

BLK_C = 128
F32 = jnp.float32
BF16 = jnp.bfloat16
VMEM = pltpu.VMEM
SMEM = pltpu.SMEM


def after(arrays):
    return [pl.BlockSpec(memory_space=pl.ANY)] * len(arrays)


def whole(space=VMEM):
    return pl.BlockSpec(memory_space=space)


def shape(dims, dtype):
    return jax.ShapeDtypeStruct(dims, dtype)


def params(mib):
    return pltpu.CompilerParams(vmem_limit_bytes=mib * 1024 * 1024)


def cost(flops, nbytes):
    return pl.CostEstimate(flops=int(flops) // 64, bytes_accessed=int(nbytes) // 64, transcendentals=0)


def pieces(extent, step, first=0):
    cuts = [0] + list(range(first or step, extent, step)) + [extent]
    return [(a, b - a) for a, b in zip(cuts[:-1], cuts[1:])]


def prep_kernel(xq, xs, xo, xc, gq, gs, go, gc, gate, up, grads, inputs, *halves):
    for out, quant, scale, flag, corr in ((grads, gq, gs, go, gc), (inputs, xq, xs, xo, xc)):
        for b in range(scale.shape[1]):
            cols = slice(b * BLK_C, (b + 1) * BLK_C)
            value = scale[0, b] * quant[:, cols].astype(F32) + flag[0, b].astype(F32) * corr[
                :, cols
            ].astype(F32)
            for p in range(out.shape[0]):
                out[p, :, cols] = value.astype(BF16)
    at = 0
    for half in halves:
        cols = slice(at, at + half.shape[1])
        at += half.shape[1]
        half[...] = jnp.concatenate(
            [gate[:, cols].astype(F32), up[:, cols].astype(F32)], 0
        ).astype(BF16)


def prep(n_t, cuts, xq, xs, xo, xc, gq, gs, go, gc, gate, up):
    rows, width = xq.shape
    tok, ff = gate.shape
    return pl.pallas_call(
        prep_kernel,
        out_shape=(shape((n_t, rows, width), BF16),) * 2
        + tuple(shape((2 * tok, size), BF16) for size in cuts),
        in_specs=[whole(), whole(SMEM), whole(SMEM), whole()] * 2 + [whole()] * 2,
        out_specs=(whole(),) * (2 + len(cuts)),
        compiler_params=params(56),
        cost_estimate=cost(0, 4 * xq.size * 2 + gate.size * 8),
    )(xq, xs, xo, xc, gq, gs, go, gc, gate, up)


def load_down(start, width, w_hbm, w_vmem, sems):
    copies = []
    for k, (at, size) in enumerate(pieces(width, 1024, 256)):
        first = pl.multiple_of(start + at, 16)
        copy = pltpu.make_async_copy(
            w_hbm.at[pl.ds(first, size)], w_vmem.at[pl.ds(at, size)], sems.at[k]
        )
        copy.start()
        copies.append(copy)
    return copies


def hidden_half(copies, grads_t, width, w_vmem, out):
    groups, rows = out.shape[0], out.shape[1]
    for copy, (at, size) in zip(copies, pieces(width, 1024, 256)):
        copy.wait()
        total = jnp.dot(w_vmem[at : at + size, :], grads_t, preferred_element_type=F32).T
        for q in range(groups):
            out[q, :, at : at + size] = total[q * rows : (q + 1) * rows, :].astype(out.dtype)


def blocks_of(held, z, n_z):
    block = held.shape[0] // n_z
    return jnp.concatenate(
        [
            held[pl.ds(pl.multiple_of((z ^ m) * block, math.gcd(block, 8)), block), :]
            for m in range(n_z)
        ],
        0,
    )


def first_half_kernel(offset, place, parts, w_hbm, *refs):
    grads_out, grads_t, out, w_vmem, held, sems = refs[-6:]
    n_t, rows = parts.shape[0], parts.shape[1]
    width = out.shape[2]
    copies = load_down((1 - place[0]) * offset, width, w_hbm, w_vmem, sems)
    for p in range(n_t):
        held[p * rows : (p + 1) * rows, :] = parts[p].astype(F32)
    grads_t[...] = held[...].T.astype(BF16)
    grads_out[...] = blocks_of(held, place[1], out.shape[0]).astype(BF16)
    hidden_half(copies, grads_t[...], width, w_vmem, out)


def second_half_kernel(offset, place, grads_t, w_hbm, *refs):
    out, w_vmem, sems = refs[-3:]
    width = out.shape[2]
    copies = load_down(place[0] * offset, width, w_hbm, w_vmem, sems)
    hidden_half(copies, grads_t[...], width, w_vmem, out)


def first_half(place, parts, w_down, n_z, width, *done):
    n_t, rows, chans = parts.shape
    tokens = n_t * rows
    n_copies = len(pieces(width, 1024, 256))
    return pl.pallas_call(
        functools.partial(first_half_kernel, w_down.shape[0] - width),
        out_shape=(
            shape((tokens, chans), BF16),
            shape((chans, tokens), BF16),
            shape((n_z, tokens // n_z, width), BF16),
        ),
        in_specs=[whole(SMEM), whole(), whole(pltpu.HBM)] + after(done),
        out_specs=(whole(),) * 3,
        scratch_shapes=[
            VMEM((width, chans), BF16),
            VMEM((tokens, chans), F32),
            pltpu.SemaphoreType.DMA((n_copies,)),
        ],
        compiler_params=params(52),
        cost_estimate=cost(2 * tokens * chans * width, 2 * chans * width),
    )(place, parts, w_down, *done)


def second_half(place, grads_t, w_down, n_z, width, *done):
    chans, tokens = grads_t.shape
    n_copies = len(pieces(width, 1024, 256))
    return pl.pallas_call(
        functools.partial(second_half_kernel, w_down.shape[0] - width),
        out_shape=shape((n_z, tokens // n_z, width), F32),
        in_specs=[whole(SMEM), whole(), whole(pltpu.HBM)] + after(done),
        out_specs=whole(),
        scratch_shapes=[VMEM((width, chans), BF16), pltpu.SemaphoreType.DMA((n_copies,))],
        compiler_params=params(52),
        cost_estimate=cost(2 * tokens * chans * width, 2 * chans * width),
    )(place, grads_t, w_down, *done)


def pair_kernel(place, mine, theirs, *refs):
    for m, out in enumerate(refs[-mine.shape[0] :]):
        at = place[1] ^ m
        out[...] = (mine[at] + theirs[at].astype(F32)).astype(out.dtype)


def pair_sum(place, mine, theirs, *done):
    n_z, rows, width = mine.shape
    return pl.pallas_call(
        pair_kernel,
        out_shape=tuple(shape((rows, width), BF16 if m % 2 else F32) for m in range(n_z)),
        in_specs=[whole(SMEM), whole(), whole()] + after(done),
        out_specs=(whole(),) * n_z,
        compiler_params=params(5),
        cost_estimate=cost(0, mine.size * 9),
    )(place, mine, theirs, *done)


def add_kernel(n_terms, *refs):
    terms, out = refs[:n_terms], refs[-1]
    total = terms[0][...].astype(F32)
    for term in terms[1:]:
        total = total + term[...].astype(F32)
    out[...] = total.astype(out.dtype)


def add_all(terms, done=()):
    return pl.pallas_call(
        functools.partial(add_kernel, len(terms)),
        out_shape=shape(terms[0].shape, BF16),
        in_specs=[whole()] * len(terms) + after(done),
        out_specs=whole(),
        compiler_params=params(3),
        cost_estimate=cost(0, terms[0].size * 2 * (len(terms) + 2)),
    )(*terms, *done)


def sum_kernel(parts, out):
    total = parts[0].astype(F32)
    for p in range(1, parts.shape[0]):
        total = total + parts[p].astype(F32)
    out[...] = total.astype(BF16)


def sum_parts(parts):
    return pl.pallas_call(
        sum_kernel,
        out_shape=shape(parts.shape[1:], BF16),
        in_specs=[whole()],
        out_specs=whole(),
        compiler_params=params(3),
        cost_estimate=cost(0, parts.size * 3),
    )(parts)


def to_chip(value, bit, n_z):
    return lax.ppermute(value, "z", [(a, a ^ bit) for a in range(n_z)])


def to_core(value):
    return lax.ppermute(value, "core", [(0, 1), (1, 0)])


def step_z(held, bit, n_z):
    return held | {m | bit: to_chip(part, bit, n_z) for m, part in held.items()}


def gather_z(held, bit, n_z):
    while bit:
        held = step_z(held, bit, n_z)
        bit //= 2
    return [held[m] for m in range(n_z)]


def complete_z(held, n_z):
    bit = n_z // 2
    while bit:
        for m in range(0, n_z, 2 * bit):
            if m in held and m | bit not in held:
                held[m | bit] = to_chip(held[m], bit, n_z)
        bit //= 2
    return [held[m] for m in range(n_z)]


def reduce_z(terms, done):
    n_z = len(terms)
    held = {m: [term] for m, term in enumerate(terms)}
    bit = 1
    while bit < n_z:
        for m in sorted((m for m in held if m & bit), reverse=True):
            mine = held.pop(m)
            term = add_all(mine) if len(mine) > 1 else mine[0].astype(BF16)
            held[m ^ bit].append(to_chip(term, bit, n_z))
        bit *= 2
    return add_all(held[0], done)


def down_kernel(n_z, n_halves, place, *refs):
    n_parts = n_z * n_halves
    grads = refs[2 * n_parts]
    out_hbm, gate_factor, up_factor, out, sems = refs[-5:]
    core0 = place[0] == 0
    copies, steps, base = [], [], 0
    for h in range(n_halves):
        mine = refs[h * n_z : (h + 1) * n_z]
        theirs = refs[n_parts + h * n_z : n_parts + (h + 1) * n_z]
        steps += [(mine, theirs, base, at, size) for at, size in pieces(mine[0].shape[1], 512)]
        base += mine[0].shape[1]
    tok = mine[0].shape[0] // 2
    for k, (mine, theirs, base, at, size) in enumerate(steps):
        cols, slot = slice(base + at, base + at + size), k % out.shape[0]
        gate, up = [], []
        for m in range(n_z):
            a = mine[m][:, at : at + size].astype(F32)
            b = theirs[m][:, at : at + size].astype(F32)
            first, second = jnp.where(core0, a, b), jnp.where(core0, b, a)
            gate += [first[:tok], second[:tok]]
            up += [first[tok:], second[tok:]]
        gate, up = jnp.concatenate(gate, 0), jnp.concatenate(up, 0)
        sig = 1.0 / (1.0 + jnp.exp(-gate))
        silu = gate * sig
        hidden = silu * up
        gate_factor[:, cols] = up * sig * (1.0 + gate * (1.0 - sig))
        up_factor[:, cols] = silu
        if k >= out.shape[0]:
            copies[k - out.shape[0]].wait()
        out[slot, :size, :] = jnp.dot(
            hidden.T.astype(BF16), grads[...], preferred_element_type=F32
        ).astype(BF16)
        copy = pltpu.make_async_copy(out.at[slot, :size], out_hbm.at[cols], sems.at[slot])
        copy.start()
        copies.append(copy)
    for copy in copies[-out.shape[0] :]:
        copy.wait()


def down_grad(place, halves, grads, *done):
    n_z, ff = len(halves[0]), sum(parts[0].shape[1] for parts in halves)
    mine = [part for parts in halves for part in parts]
    theirs = [to_core(part) for part in mine]
    tokens, chans = grads.shape
    slots = min(4, len(pieces(ff, 512)))
    return pl.pallas_call(
        functools.partial(down_kernel, n_z, len(halves)),
        out_shape=(shape((ff, chans), BF16), shape((tokens, ff), F32), shape((tokens, ff), F32)),
        in_specs=[whole(SMEM)] + [whole()] * (2 * len(mine) + 1) + after(done),
        out_specs=(whole(pltpu.HBM), whole(), whole()),
        scratch_shapes=[VMEM((slots, 512, chans), BF16), pltpu.SemaphoreType.DMA((slots,))],
        compiler_params=params(18),
        cost_estimate=cost(2 * tokens * chans * ff, 2 * chans * ff + 8 * tokens * ff),
    )(place, *mine, *theirs, grads, *done)


def input_kernel(n_z, place, *refs):
    mine, theirs = refs[:n_z], refs[n_z : 2 * n_z]
    gate_factor, up_factor, gate_hbm, up_hbm = refs[2 * n_z : 2 * n_z + 4]
    gate_grad, up_grad, out, w_gate, w_up, total, held, sems = refs[2 * n_z + 4 :]
    core0, z = place[0] == 0, place[1]
    rows, width = mine[0].shape
    ff = gate_grad.shape[1]
    low = ff - width
    slots = w_gate.shape[0]
    parts = [(0, at, size) for at, size in pieces(low, 1024, 256)]
    parts += [(low, at, size) for at, size in pieces(width, 1024)]

    def copies(k):
        base, at, size = parts[k]
        return [
            pltpu.make_async_copy(
                hbm.at[:, base + at : base + at + size],
                vmem.at[k % slots, :, :size],
                sems.at[n, k % slots],
            )
            for n, (hbm, vmem) in enumerate(((gate_hbm, w_gate), (up_hbm, w_up)))
        ]

    for k in range(min(slots, len(parts))):
        for copy in copies(k):
            copy.start()
    dims = (((1,), (1,)), ((), ()))
    for k, (base, at, size) in enumerate(parts):
        cols = slice(base + at, base + at + size)
        first = core0 if base == 0 else ~core0
        hidden = jnp.concatenate(
            [
                jnp.where(first, mine[m][:, at : at + size], theirs[m][:, at : at + size]).astype(F32)
                for m in range(n_z)
            ],
            0,
        )
        gate = (hidden * gate_factor[:, cols]).astype(BF16)
        up = (hidden * up_factor[:, cols]).astype(BF16)
        gate_grad[:, cols] = gate
        up_grad[:, cols] = up
        for copy in copies(k):
            copy.wait()
        slot = k % slots
        term = lax.dot_general(w_gate[slot, :, :size], gate, dims, preferred_element_type=F32)
        term += lax.dot_general(w_up[slot, :, :size], up, dims, preferred_element_type=F32)
        total[...] = term if k == 0 else total[...] + term
        if k + slots < len(parts):
            for copy in copies(k + slots):
                copy.start()
    turned = total[...].T
    for m in range(n_z):
        held[pl.ds(pl.multiple_of((z ^ m) * rows, math.gcd(rows, 8)), rows), :] = turned[m * rows : (m + 1) * rows]
    n_t = out.shape[0]
    step = held.shape[0] // n_t
    for p in range(n_t):
        out[p] = held[p * step : (p + 1) * step, :].astype(BF16)


def input_grad(place, mine, theirs, gate_factor, up_factor, w_gate, w_up, n_t):
    tokens, ff = gate_factor.shape
    chans = w_gate.shape[0]
    n_z, slots = len(mine), 3
    return pl.pallas_call(
        functools.partial(input_kernel, n_z),
        out_shape=(shape((tokens, ff), BF16),) * 2 + (shape((n_t, tokens // n_t, chans), BF16),),
        in_specs=[whole(SMEM)] + [whole()] * (2 * n_z + 2) + [whole(pltpu.HBM)] * 2,
        out_specs=(whole(),) * 3,
        scratch_shapes=[
            VMEM((slots, chans, min(ff, 1024)), BF16),
            VMEM((slots, chans, min(ff, 1024)), BF16),
            VMEM((chans, tokens), F32),
            VMEM((tokens, chans), F32),
            pltpu.SemaphoreType.DMA((2, slots)),
        ],
        compiler_params=params(50),
        cost_estimate=cost(4 * tokens * chans * ff, 4 * chans * ff + 12 * tokens * ff),
    )(place, *mine, *theirs, gate_factor, up_factor, w_gate, w_up)


def weight_kernel(n_z, place, parts, gate_grad, up_grad, gate_hbm, up_hbm, out, held, inputs_t, sems):
    rows = parts.shape[1]
    for p in range(parts.shape[0]):
        held[p * rows : (p + 1) * rows, :] = parts[p].astype(F32)
    inputs_t[...] = blocks_of(held, place[1], n_z).T.astype(BF16)
    copies = []
    ff, slots = gate_grad.shape[1], out.shape[0]
    for grad, hbm in ((gate_grad, gate_hbm), (up_grad, up_hbm)):
        for at, size in pieces(ff, 512):
            cols, slot = slice(at, at + size), len(copies) % slots
            if len(copies) >= slots:
                copies[len(copies) - slots].wait()
            out[slot, :, :size] = jnp.dot(
                inputs_t[...], grad[:, cols], preferred_element_type=F32
            ).astype(BF16)
            copy = pltpu.make_async_copy(out.at[slot, :, :size], hbm.at[:, cols], sems.at[slot])
            copy.start()
            copies.append(copy)
    for copy in copies[-slots:]:
        copy.wait()


def weight_grads(place, parts, gate_grad, up_grad, n_z):
    chans, tokens = parts.shape[2], gate_grad.shape[0]
    ff = gate_grad.shape[1]
    slots = min(8, 2 * len(pieces(ff, 512)))
    return pl.pallas_call(
        functools.partial(weight_kernel, n_z),
        out_shape=(shape((chans, ff), BF16),) * 2,
        in_specs=[whole(SMEM)] + [whole()] * 3,
        out_specs=(whole(pltpu.HBM),) * 2,
        scratch_shapes=[
            VMEM((slots, chans, 512), BF16),
            VMEM((tokens, chans), F32),
            VMEM((chans, tokens), BF16),
            pltpu.SemaphoreType.DMA((slots,)),
        ],
        compiler_params=params(16),
        cost_estimate=cost(4 * tokens * chans * ff, 4 * chans * ff + 4 * tokens * ff),
    )(place, parts, gate_grad, up_grad)


def on_device(n_z, n_t, xq, xs, xo, xc, gq, gs, go, gc, gate_pre, up_pre, w_gate, w_up, w_down):
    place = jnp.stack([lax.axis_index(name) for name in ("core", "z", "tensor")]).astype(jnp.int32)
    ff = gate_pre.shape[1]
    width = -(-ff // 256) * 128

    def exchange(value):
        return lax.all_to_all(value, "tensor", 0, 0, tiled=True)

    cuts = (ff - width, width)
    grads, inputs, *halves = prep(
        n_t, cuts, xq, xs, xo, xc, gq, gs, go, gc, gate_pre, up_pre
    )
    grads = exchange(grads)
    bit = n_z // 2
    a, b = {0: halves[0]}, {0: halves[1]}
    a |= {bit: to_chip(a[0], bit, n_z), 1: to_chip(a[0], 1, n_z)}
    grads, grads_t, send = first_half(place, grads, w_down, n_z, width, a[bit], a[1])
    got = to_core(send)
    a[bit | 1] = to_chip(a[bit], 1, n_z)
    b[bit] = to_chip(b[0], bit, n_z)
    mine = second_half(place, grads_t, w_down, n_z, width, a[bit | 1], b[bit])
    b |= {1: to_chip(b[0], 1, n_z), bit | 1: to_chip(b[bit], 1, n_z)}
    terms = pair_sum(place, mine, got, b[1], b[bit | 1])
    gate_up = [complete_z(held, n_z) for held in (a, b)]
    inputs = exchange(inputs)
    grad_down, gate_factor, up_factor = down_grad(place, gate_up, grads, inputs)
    hidden_grad = gather_z({0: reduce_z(terms, [gate_factor])}, bit, n_z)
    gate_grad, up_grad, sends = input_grad(
        place, hidden_grad, [to_core(part) for part in hidden_grad],
        gate_factor, up_factor, w_gate, w_up, n_t,
    )
    terms = exchange(sends)
    grad_gate, grad_up = weight_grads(place, inputs, gate_grad, up_grad, n_z)
    return sum_parts(terms), grad_gate, grad_up, grad_down


def solution(mesh):
    n_dp, n_t = mesh.shape["dp"], mesh.shape["tensor"]
    fine = Mesh(mesh.devices.reshape(n_dp // 2, 2, n_t), ("z", "core", "tensor"))
    by_token, by_dp = P("tensor", ("z", "core")), P(("z", "core"), "tensor")
    return jax.shard_map(
        functools.partial(on_device, n_dp // 2, n_t),
        mesh=fine,
        in_specs=(by_token,) * 8 + (by_dp,) * 4 + (by_token,),
        out_specs=(by_token, by_dp, by_dp, by_token),
        check_vma=False,
    )
```

```python
import functools
import math

import jax
import jax.numpy as jnp
from jax import lax
from jax.experimental import pallas as pl
from jax.experimental.pallas import tpu as pltpu
from jax.sharding import Mesh
from jax.sharding import PartitionSpec as P

BLK_C = 128
F32 = jnp.float32
BF16 = jnp.bfloat16
VMEM = pltpu.VMEM
SMEM = pltpu.SMEM


def after(arrays):
    return [pl.BlockSpec(memory_space=pl.ANY)] * len(arrays)


def whole(space=VMEM):
    return pl.BlockSpec(memory_space=space)


def shape(dims, dtype):
    return jax.ShapeDtypeStruct(dims, dtype)


def params(mib):
    return pltpu.CompilerParams(vmem_limit_bytes=mib * 1024 * 1024)


def cost(flops, nbytes):
    return pl.CostEstimate(flops=int(flops) // 64, bytes_accessed=int(nbytes) // 64, transcendentals=0)


def pieces(extent, step, first=0):
    cuts = [0] + list(range(first or step, extent, step)) + [extent]
    return [(a, b - a) for a, b in zip(cuts[:-1], cuts[1:])]


def prep_kernel(xq, xs, xo, xc, gq, gs, go, gc, gate, up, grads, inputs, *halves):
    for out, quant, scale, flag, corr in ((grads, gq, gs, go, gc), (inputs, xq, xs, xo, xc)):
        for b in range(scale.shape[1]):
            cols = slice(b * BLK_C, (b + 1) * BLK_C)
            value = scale[0, b] * quant[:, cols].astype(F32) + flag[0, b].astype(F32) * corr[
                :, cols
            ].astype(F32)
            out[:, cols] = value.astype(BF16)
    at = 0
    for half in halves:
        cols = slice(at, at + half.shape[1])
        at += half.shape[1]
        half[...] = jnp.concatenate(
            [gate[:, cols].astype(F32), up[:, cols].astype(F32)], 0
        ).astype(BF16)


def prep(cuts, xq, xs, xo, xc, gq, gs, go, gc, gate, up):
    rows, width = xq.shape
    tok, ff = gate.shape
    return pl.pallas_call(
        prep_kernel,
        out_shape=(shape((rows, width), BF16),) * 2
        + tuple(shape((2 * tok, size), BF16) for size in cuts),
        in_specs=[whole(), whole(SMEM), whole(SMEM), whole()] * 2 + [whole()] * 2,
        out_specs=(whole(),) * (2 + len(cuts)),
        compiler_params=params(56),
        cost_estimate=cost(0, 4 * xq.size * 2 + gate.size * 8),
    )(xq, xs, xo, xc, gq, gs, go, gc, gate, up)


def load_down(start, width, w_hbm, w_vmem, sems):
    copies = []
    for k, (at, size) in enumerate(pieces(width, 1024, 256)):
        first = pl.multiple_of(start + at, 16)
        copy = pltpu.make_async_copy(
            w_hbm.at[pl.ds(first, size)], w_vmem.at[pl.ds(at, size)], sems.at[k]
        )
        copy.start()
        copies.append(copy)
    return copies


def hidden_half(copies, grads_t, width, w_vmem, out):
    groups, rows = out.shape[0], out.shape[1]
    for copy, (at, size) in zip(copies, pieces(width, 1024, 256)):
        copy.wait()
        total = jnp.dot(w_vmem[at : at + size, :], grads_t, preferred_element_type=F32).T
        for q in range(groups):
            out[q, :, at : at + size] = total[q * rows : (q + 1) * rows, :].astype(out.dtype)


def blocks_of(held, z, n_z):
    block = held.shape[0] // n_z
    return jnp.concatenate(
        [
            held[pl.ds(pl.multiple_of((z ^ m) * block, math.gcd(block, 8)), block), :]
            for m in range(n_z)
        ],
        0,
    )


def hold(parts, me, held):
    rows = parts[0].shape[0]
    for s, part in enumerate(parts):
        start = pl.multiple_of((me ^ s) * rows, math.gcd(rows, 8))
        held[pl.ds(start, rows), :] = part[...].astype(F32)


def first_half_kernel(n_t, offset, place, *refs):
    parts, w_hbm = refs[:n_t], refs[n_t]
    grads_out, grads_t, out, w_vmem, held, sems = refs[-6:]
    width = out.shape[2]
    copies = load_down((1 - place[0]) * offset, width, w_hbm, w_vmem, sems)
    hold(parts, place[2], held)
    grads_t[...] = held[...].T.astype(BF16)
    grads_out[...] = blocks_of(held, place[1], out.shape[0]).astype(BF16)
    hidden_half(copies, grads_t[...], width, w_vmem, out)


def second_half_kernel(offset, place, grads_t, w_hbm, *refs):
    out, w_vmem, sems = refs[-3:]
    width = out.shape[2]
    copies = load_down(place[0] * offset, width, w_hbm, w_vmem, sems)
    hidden_half(copies, grads_t[...], width, w_vmem, out)


def first_half(place, parts, w_down, n_z, width, *done):
    n_t, (rows, chans) = len(parts), parts[0].shape
    tokens = n_t * rows
    n_copies = len(pieces(width, 1024, 256))
    return pl.pallas_call(
        functools.partial(first_half_kernel, n_t, w_down.shape[0] - width),
        out_shape=(
            shape((tokens, chans), BF16),
            shape((chans, tokens), BF16),
            shape((n_z, tokens // n_z, width), BF16),
        ),
        in_specs=[whole(SMEM)] + [whole()] * n_t + [whole(pltpu.HBM)] + after(done),
        out_specs=(whole(),) * 3,
        scratch_shapes=[
            VMEM((width, chans), BF16),
            VMEM((tokens, chans), F32),
            pltpu.SemaphoreType.DMA((n_copies,)),
        ],
        compiler_params=params(52),
        cost_estimate=cost(2 * tokens * chans * width, 2 * chans * width),
    )(place, *parts, w_down, *done)


def second_half(place, grads_t, w_down, n_z, width, *done):
    chans, tokens = grads_t.shape
    n_copies = len(pieces(width, 1024, 256))
    return pl.pallas_call(
        functools.partial(second_half_kernel, w_down.shape[0] - width),
        out_shape=shape((n_z, tokens // n_z, width), F32),
        in_specs=[whole(SMEM), whole(), whole(pltpu.HBM)] + after(done),
        out_specs=whole(),
        scratch_shapes=[VMEM((width, chans), BF16), pltpu.SemaphoreType.DMA((n_copies,))],
        compiler_params=params(52),
        cost_estimate=cost(2 * tokens * chans * width, 2 * chans * width),
    )(place, grads_t, w_down, *done)


def pair_kernel(place, mine, theirs, *refs):
    for m, out in enumerate(refs[-mine.shape[0] :]):
        at = place[1] ^ m
        out[...] = (mine[at] + theirs[at].astype(F32)).astype(out.dtype)


def pair_sum(place, mine, theirs, *done):
    n_z, rows, width = mine.shape
    return pl.pallas_call(
        pair_kernel,
        out_shape=tuple(shape((rows, width), BF16 if m % 2 else F32) for m in range(n_z)),
        in_specs=[whole(SMEM), whole(), whole()] + after(done),
        out_specs=(whole(),) * n_z,
        compiler_params=params(5),
        cost_estimate=cost(0, mine.size * 9),
    )(place, mine, theirs, *done)


def add_kernel(n_terms, *refs):
    terms, out = refs[:n_terms], refs[-1]
    total = terms[0][...].astype(F32)
    for term in terms[1:]:
        total = total + term[...].astype(F32)
    out[...] = total.astype(out.dtype)


def add_all(terms, done=()):
    return pl.pallas_call(
        functools.partial(add_kernel, len(terms)),
        out_shape=shape(terms[0].shape, BF16),
        in_specs=[whole()] * len(terms) + after(done),
        out_specs=whole(),
        compiler_params=params(3),
        cost_estimate=cost(0, terms[0].size * 2 * (len(terms) + 2)),
    )(*terms, *done)


def sum_kernel(parts, out):
    total = parts[0].astype(F32)
    for p in range(1, parts.shape[0]):
        total = total + parts[p].astype(F32)
    out[...] = total.astype(BF16)


def sum_parts(parts):
    return pl.pallas_call(
        sum_kernel,
        out_shape=shape(parts.shape[1:], BF16),
        in_specs=[whole()],
        out_specs=whole(),
        compiler_params=params(3),
        cost_estimate=cost(0, parts.size * 3),
    )(parts)


def to_chip(value, bit, n_z):
    return lax.ppermute(value, "z", [(a, a ^ bit) for a in range(n_z)])


def to_core(value):
    return lax.ppermute(value, "core", [(0, 1), (1, 0)])


def complete_z(held, n_z):
    bit = n_z // 2
    while bit:
        for m in range(0, n_z, 2 * bit):
            if m in held and m | bit not in held:
                held[m | bit] = to_chip(held[m], bit, n_z)
        bit //= 2
    return [held[m] for m in range(n_z)]


def reduce_z(terms, done):
    n_z = len(terms)
    held = {m: [term] for m, term in enumerate(terms)}
    bit = 1
    while bit < n_z:
        for m in sorted((m for m in held if m & bit), reverse=True):
            mine = held.pop(m)
            term = add_all(mine) if len(mine) > 1 else mine[0].astype(BF16)
            held[m ^ bit].append(to_chip(term, bit, n_z))
        bit *= 2
    return add_all(held[0], done)


def down_kernel(n_z, n_halves, place, *refs):
    n_parts = n_z * n_halves
    grads = refs[2 * n_parts]
    out_hbm, gate_factor, up_factor, out, sems = refs[-5:]
    core0 = place[0] == 0
    copies, steps, base = [], [], 0
    for h in range(n_halves):
        mine = refs[h * n_z : (h + 1) * n_z]
        theirs = refs[n_parts + h * n_z : n_parts + (h + 1) * n_z]
        steps += [(mine, theirs, base, at, size) for at, size in pieces(mine[0].shape[1], 512)]
        base += mine[0].shape[1]
    tok = mine[0].shape[0] // 2
    for k, (mine, theirs, base, at, size) in enumerate(steps):
        cols, slot = slice(base + at, base + at + size), k % out.shape[0]
        gate, up = [], []
        for m in range(n_z):
            a = mine[m][:, at : at + size].astype(F32)
            b = theirs[m][:, at : at + size].astype(F32)
            first, second = jnp.where(core0, a, b), jnp.where(core0, b, a)
            gate += [first[:tok], second[:tok]]
            up += [first[tok:], second[tok:]]
        gate, up = jnp.concatenate(gate, 0), jnp.concatenate(up, 0)
        sig = 1.0 / (1.0 + jnp.exp(-gate))
        silu = gate * sig
        hidden = silu * up
        gate_factor[:, cols] = up * sig * (1.0 + gate * (1.0 - sig))
        up_factor[:, cols] = silu
        if k >= out.shape[0]:
            copies[k - out.shape[0]].wait()
        out[slot, :size, :] = jnp.dot(
            hidden.T.astype(BF16), grads[...], preferred_element_type=F32
        ).astype(BF16)
        copy = pltpu.make_async_copy(out.at[slot, :size], out_hbm.at[cols], sems.at[slot])
        copy.start()
        copies.append(copy)
    for copy in copies[-out.shape[0] :]:
        copy.wait()


def down_grad(place, mine, theirs, grads):
    n_z, ff = len(mine) // 2, mine[0].shape[1] + mine[-1].shape[1]
    tokens, chans = grads.shape
    slots = min(4, len(pieces(ff, 512)))
    return pl.pallas_call(
        functools.partial(down_kernel, n_z, 2),
        out_shape=(shape((ff, chans), BF16), shape((tokens, ff), F32), shape((tokens, ff), F32)),
        in_specs=[whole(SMEM)] + [whole()] * (2 * len(mine) + 1),
        out_specs=(whole(pltpu.HBM), whole(), whole()),
        scratch_shapes=[VMEM((slots, 512, chans), BF16), pltpu.SemaphoreType.DMA((slots,))],
        compiler_params=params(18),
        cost_estimate=cost(2 * tokens * chans * ff, 2 * chans * ff + 8 * tokens * ff),
    )(place, *mine, *theirs, grads)


def input_kernel(n_z, place, *refs):
    mine, theirs = refs[:n_z], refs[n_z : 2 * n_z]
    gate_factor, up_factor, gate_hbm, up_hbm = refs[2 * n_z : 2 * n_z + 4]
    gate_grad, up_grad, out, w_gate, w_up, total, held, sems = refs[2 * n_z + 4 :]
    core0, z = place[0] == 0, place[1]
    rows, width = mine[0].shape
    ff = gate_grad.shape[1]
    low = ff - width
    slots = w_gate.shape[0]
    parts = [(0, at, size) for at, size in pieces(low, 1024, 256)]
    parts += [(low, at, size) for at, size in pieces(width, 1024)]

    def copies(k):
        base, at, size = parts[k]
        return [
            pltpu.make_async_copy(
                hbm.at[:, base + at : base + at + size],
                vmem.at[k % slots, :, :size],
                sems.at[n, k % slots],
            )
            for n, (hbm, vmem) in enumerate(((gate_hbm, w_gate), (up_hbm, w_up)))
        ]

    for k in range(min(slots, len(parts))):
        for copy in copies(k):
            copy.start()
    dims = (((1,), (1,)), ((), ()))
    for k, (base, at, size) in enumerate(parts):
        cols = slice(base + at, base + at + size)
        first = core0 if base == 0 else ~core0
        hidden = jnp.concatenate(
            [
                jnp.where(first, mine[m][:, at : at + size], theirs[m][:, at : at + size]).astype(F32)
                for m in range(n_z)
            ],
            0,
        )
        gate = (hidden * gate_factor[:, cols]).astype(BF16)
        up = (hidden * up_factor[:, cols]).astype(BF16)
        gate_grad[:, cols] = gate
        up_grad[:, cols] = up
        for copy in copies(k):
            copy.wait()
        slot = k % slots
        term = lax.dot_general(w_gate[slot, :, :size], gate, dims, preferred_element_type=F32)
        term += lax.dot_general(w_up[slot, :, :size], up, dims, preferred_element_type=F32)
        total[...] = term if k == 0 else total[...] + term
        if k + slots < len(parts):
            for copy in copies(k + slots):
                copy.start()
    turned = total[...].T
    for m in range(n_z):
        held[pl.ds(pl.multiple_of((z ^ m) * rows, math.gcd(rows, 8)), rows), :] = turned[m * rows : (m + 1) * rows]
    n_t = out.shape[0]
    step = held.shape[0] // n_t
    for p in range(n_t):
        out[p] = held[p * step : (p + 1) * step, :].astype(BF16)


def input_grad(place, mine, theirs, gate_factor, up_factor, w_gate, w_up, n_t):
    tokens, ff = gate_factor.shape
    chans = w_gate.shape[0]
    n_z, slots = len(mine), 3
    return pl.pallas_call(
        functools.partial(input_kernel, n_z),
        out_shape=(shape((tokens, ff), BF16),) * 2 + (shape((n_t, tokens // n_t, chans), BF16),),
        in_specs=[whole(SMEM)] + [whole()] * (2 * n_z + 2) + [whole(pltpu.HBM)] * 2,
        out_specs=(whole(),) * 3,
        scratch_shapes=[
            VMEM((slots, chans, min(ff, 1024)), BF16),
            VMEM((slots, chans, min(ff, 1024)), BF16),
            VMEM((chans, tokens), F32),
            VMEM((tokens, chans), F32),
            pltpu.SemaphoreType.DMA((2, slots)),
        ],
        compiler_params=params(50),
        cost_estimate=cost(4 * tokens * chans * ff, 4 * chans * ff + 12 * tokens * ff),
    )(place, *mine, *theirs, gate_factor, up_factor, w_gate, w_up)


def weight_kernel(n_z, n_t, place, *refs):
    gate_grad, up_grad, gate_hbm, up_hbm, out, held, inputs_t, sems = refs[n_t:]
    hold(refs[:n_t], place[2], held)
    inputs_t[...] = blocks_of(held, place[1], n_z).T.astype(BF16)
    copies = []
    ff, slots = gate_grad.shape[1], out.shape[0]
    for grad, hbm in ((gate_grad, gate_hbm), (up_grad, up_hbm)):
        for at, size in pieces(ff, 512):
            cols, slot = slice(at, at + size), len(copies) % slots
            if len(copies) >= slots:
                copies[len(copies) - slots].wait()
            out[slot, :, :size] = jnp.dot(
                inputs_t[...], grad[:, cols], preferred_element_type=F32
            ).astype(BF16)
            copy = pltpu.make_async_copy(out.at[slot, :, :size], hbm.at[:, cols], sems.at[slot])
            copy.start()
            copies.append(copy)
    for copy in copies[-slots:]:
        copy.wait()


def weight_grads(place, parts, gate_grad, up_grad, n_z):
    n_t, chans, tokens = len(parts), parts[0].shape[1], gate_grad.shape[0]
    ff = gate_grad.shape[1]
    slots = min(8, 2 * len(pieces(ff, 512)))
    return pl.pallas_call(
        functools.partial(weight_kernel, n_z, n_t),
        out_shape=(shape((chans, ff), BF16),) * 2,
        in_specs=[whole(SMEM)] + [whole()] * (n_t + 2),
        out_specs=(whole(pltpu.HBM),) * 2,
        scratch_shapes=[
            VMEM((slots, chans, 512), BF16),
            VMEM((tokens, chans), F32),
            VMEM((chans, tokens), BF16),
            pltpu.SemaphoreType.DMA((slots,)),
        ],
        compiler_params=params(16),
        cost_estimate=cost(4 * tokens * chans * ff, 4 * chans * ff + 4 * tokens * ff),
    )(place, *parts, gate_grad, up_grad)


def on_device(n_z, n_t, xq, xs, xo, xc, gq, gs, go, gc, gate_pre, up_pre, w_gate, w_up, w_down):
    place = jnp.stack([lax.axis_index(name) for name in ("core", "z", "tensor")]).astype(jnp.int32)
    ff = gate_pre.shape[1]
    width = -(-ff // 256) * 128

    def from_tensor(own):
        return [own] + [
            lax.ppermute(own, "tensor", [(a, a ^ s) for a in range(n_t)]) for s in range(1, n_t)
        ]

    cuts = (ff - width, width)
    grads, inputs, *halves = prep(cuts, xq, xs, xo, xc, gq, gs, go, gc, gate_pre, up_pre)
    bit = n_z // 2
    grads = from_tensor(grads)
    a, b = {0: halves[0]}, {0: halves[1]}
    a |= {bit: to_chip(a[0], bit, n_z), 1: to_chip(a[0], 1, n_z)}
    grads, grads_t, send = first_half(place, grads, w_down, n_z, width, a[bit])
    got = to_core(send)
    a[bit | 1] = to_chip(a[bit], 1, n_z)
    mine = second_half(place, grads_t, w_down, n_z, width, a[1], a[bit | 1])
    b |= {bit: to_chip(b[0], bit, n_z), 1: to_chip(b[0], 1, n_z)}
    terms = pair_sum(place, mine, got, b[bit], b[1])
    gate_up = [part for held in (a, b) for part in complete_z(held, n_z)]
    gate_up_other = [to_core(part) for part in gate_up]
    hidden = {0: reduce_z(terms, gate_up_other)}
    hidden |= {bit: to_chip(hidden[0], bit, n_z), 1: to_chip(hidden[0], 1, n_z)}
    grad_down, gate_factor, up_factor = down_grad(place, gate_up, gate_up_other, grads)
    inputs = from_tensor(inputs)
    hidden[bit] = add_all([hidden[bit]], [gate_factor, hidden[1], *inputs[1:]])
    hidden_grad = complete_z(hidden, n_z)
    gate_grad, up_grad, sends = input_grad(
        place, hidden_grad, [to_core(part) for part in hidden_grad],
        gate_factor, up_factor, w_gate, w_up, n_t,
    )
    terms = lax.all_to_all(sends, "tensor", 0, 0, tiled=True)
    grad_gate, grad_up = weight_grads(place, inputs, gate_grad, up_grad, n_z)
    return sum_parts(terms), grad_gate, grad_up, grad_down


def solution(mesh):
    n_dp, n_t = mesh.shape["dp"], mesh.shape["tensor"]
    fine = Mesh(mesh.devices.reshape(n_dp // 2, 2, n_t), ("z", "core", "tensor"))
    by_token, by_dp = P("tensor", ("z", "core")), P(("z", "core"), "tensor")
    return jax.shard_map(
        functools.partial(on_device, n_dp // 2, n_t),
        mesh=fine,
        in_specs=(by_token,) * 8 + (by_dp,) * 4 + (by_token,),
        out_specs=(by_token, by_dp, by_dp, by_token),
        check_vma=False,
    )
```

```python
import functools
import math

import jax
import jax.numpy as jnp
from jax import lax
from jax.experimental import pallas as pl
from jax.experimental.pallas import tpu as pltpu
from jax.sharding import Mesh
from jax.sharding import PartitionSpec as P

BLK_C = 128
F32 = jnp.float32
BF16 = jnp.bfloat16
VMEM = pltpu.VMEM
SMEM = pltpu.SMEM


def after(arrays):
    return [pl.BlockSpec(memory_space=pl.ANY)] * len(arrays)


def whole(space=VMEM):
    return pl.BlockSpec(memory_space=space)


def shape(dims, dtype):
    return jax.ShapeDtypeStruct(dims, dtype)


def params(mib):
    return pltpu.CompilerParams(vmem_limit_bytes=mib * 1024 * 1024)


def cost(flops, nbytes):
    return pl.CostEstimate(flops=int(flops), bytes_accessed=int(nbytes), transcendentals=0)


def pieces(extent, step, first=0):
    cuts = [0] + list(range(first or step, extent, step)) + [extent]
    return [(a, b - a) for a, b in zip(cuts[:-1], cuts[1:])]


def prep_kernel(xq, xs, xo, xc, gq, gs, go, gc, gate, up, grads, inputs, *halves):
    for out, quant, scale, flag, corr in ((grads, gq, gs, go, gc), (inputs, xq, xs, xo, xc)):
        for b in range(scale.shape[1]):
            cols = slice(b * BLK_C, (b + 1) * BLK_C)
            value = scale[0, b] * quant[:, cols].astype(F32) + flag[0, b].astype(F32) * corr[
                :, cols
            ].astype(F32)
            out[:, cols] = value.astype(BF16)
    at = 0
    for half in halves:
        cols = slice(at, at + half.shape[1])
        at += half.shape[1]
        half[...] = jnp.concatenate(
            [gate[:, cols].astype(F32), up[:, cols].astype(F32)], 0
        ).astype(BF16)


def prep(cuts, xq, xs, xo, xc, gq, gs, go, gc, gate, up):
    rows, width = xq.shape
    tok, ff = gate.shape
    return pl.pallas_call(
        prep_kernel,
        out_shape=(shape((rows, width), BF16),) * 2
        + tuple(shape((2 * tok, size), BF16) for size in cuts),
        in_specs=[whole(), whole(SMEM), whole(SMEM), whole()] * 2 + [whole()] * 2,
        out_specs=(whole(),) * (2 + len(cuts)),
        compiler_params=params(56),
        cost_estimate=cost(0, 4 * xq.size * 2 + gate.size * 8),
    )(xq, xs, xo, xc, gq, gs, go, gc, gate, up)


def load_down(start, width, w_hbm, w_vmem, sems):
    copies = []
    for k, (at, size) in enumerate(pieces(width, 1024, 256)):
        first = pl.multiple_of(start + at, 16)
        copy = pltpu.make_async_copy(
            w_hbm.at[pl.ds(first, size)], w_vmem.at[pl.ds(at, size)], sems.at[k]
        )
        copy.start()
        copies.append(copy)
    return copies


def hidden_half(copies, grads_t, width, w_vmem, out):
    groups, rows = out.shape[0], out.shape[1]
    for copy, (at, size) in zip(copies, pieces(width, 1024, 256)):
        copy.wait()
        total = jnp.dot(w_vmem[at : at + size, :], grads_t, preferred_element_type=F32).T
        for q in range(groups):
            out[q, :, at : at + size] = total[q * rows : (q + 1) * rows, :].astype(out.dtype)


def blocks_of(held, z, n_z):
    block = held.shape[0] // n_z
    return jnp.concatenate(
        [
            held[pl.ds(pl.multiple_of((z ^ m) * block, math.gcd(block, 8)), block), :]
            for m in range(n_z)
        ],
        0,
    )


def hold(parts, me, held):
    rows = parts[0].shape[0]
    for s, part in enumerate(parts):
        start = pl.multiple_of((me ^ s) * rows, math.gcd(rows, 8))
        held[pl.ds(start, rows), :] = part[...].astype(F32)


def first_half_kernel(n_t, offset, place, *refs):
    parts, w_hbm = refs[:n_t], refs[n_t]
    grads_out, grads_t, out, w_vmem, held, sems = refs[-6:]
    width = out.shape[2]
    copies = load_down((1 - place[0]) * offset, width, w_hbm, w_vmem, sems)
    hold(parts, place[2], held)
    grads_t[...] = held[...].T.astype(BF16)
    grads_out[...] = blocks_of(held, place[1], out.shape[0]).astype(BF16)
    hidden_half(copies, grads_t[...], width, w_vmem, out)


def second_half_kernel(offset, place, grads_t, w_hbm, *refs):
    out, w_vmem, sems = refs[-3:]
    width = out.shape[2]
    copies = load_down(place[0] * offset, width, w_hbm, w_vmem, sems)
    hidden_half(copies, grads_t[...], width, w_vmem, out)


def first_half(place, parts, w_down, n_z, width, *done):
    n_t, (rows, chans) = len(parts), parts[0].shape
    tokens = n_t * rows
    n_copies = len(pieces(width, 1024, 256))
    return pl.pallas_call(
        functools.partial(first_half_kernel, n_t, w_down.shape[0] - width),
        out_shape=(
            shape((tokens, chans), BF16),
            shape((chans, tokens), BF16),
            shape((n_z, tokens // n_z, width), BF16),
        ),
        in_specs=[whole(SMEM)] + [whole()] * n_t + [whole(pltpu.HBM)] + after(done),
        out_specs=(whole(),) * 3,
        scratch_shapes=[
            VMEM((width, chans), BF16),
            VMEM((tokens, chans), F32),
            pltpu.SemaphoreType.DMA((n_copies,)),
        ],
        compiler_params=params(52),
        cost_estimate=cost(2 * tokens * chans * width, 2 * chans * width),
    )(place, *parts, w_down, *done)


def second_half(place, grads_t, w_down, n_z, width, *done):
    chans, tokens = grads_t.shape
    n_copies = len(pieces(width, 1024, 256))
    return pl.pallas_call(
        functools.partial(second_half_kernel, w_down.shape[0] - width),
        out_shape=shape((n_z, tokens // n_z, width), F32),
        in_specs=[whole(SMEM), whole(), whole(pltpu.HBM)] + after(done),
        out_specs=whole(),
        scratch_shapes=[VMEM((width, chans), BF16), pltpu.SemaphoreType.DMA((n_copies,))],
        compiler_params=params(52),
        cost_estimate=cost(8 * tokens * chans * width, 8 * chans * width),
    )(place, grads_t, w_down, *done)


def pair_kernel(place, mine, theirs, *refs):
    n_z = mine.shape[0]
    outs = refs[-1 - n_z // 2 :]
    for m in range(n_z):
        at = place[1] ^ m
        total = mine[at] + theirs[at].astype(F32)
        if m % 2:
            outs[-1][m // 2] = total.astype(BF16)
        else:
            outs[m // 2][...] = total


def pair_sum(place, mine, theirs, *done):
    n_z, rows, width = mine.shape
    return pl.pallas_call(
        pair_kernel,
        out_shape=(shape((rows, width), F32),) * (n_z // 2)
        + (shape((n_z // 2, rows, width), BF16),),
        in_specs=[whole(SMEM), whole(), whole()] + after(done),
        out_specs=(whole(),) * (n_z // 2 + 1),
        compiler_params=params(5),
        cost_estimate=cost(0, mine.size * 9),
    )(place, mine, theirs, *done)


def add_kernel(picks, n_refs, *refs):
    outs = refs[-len(picks) :]
    for pick, out in zip(picks, outs):
        total = None
        for ref, row in pick:
            term = (refs[ref][...] if row is None else refs[ref][row]).astype(F32)
            total = term if total is None else total + term
        out[...] = total.astype(out.dtype)


def add_all(lists, dtypes, done=()):
    arrays, picks = [], []
    for terms in lists:
        pick = []
        for array, row in terms:
            at = next((k for k, known in enumerate(arrays) if known is array), len(arrays))
            if at == len(arrays):
                arrays.append(array)
            pick.append((at, row))
        picks.append(pick)
    dims = lists[0][0][0].shape[-2:]
    return pl.pallas_call(
        functools.partial(add_kernel, picks, len(arrays)),
        out_shape=tuple(shape(dims, dtype) for dtype in dtypes),
        in_specs=[whole()] * len(arrays) + after(done),
        out_specs=(whole(),) * len(lists),
        compiler_params=params(6),
        cost_estimate=cost(0, dims[0] * dims[1] * 6 * sum(map(len, lists))),
    )(*arrays, *done)


def stack_kernel(*refs):
    for k, ref in enumerate(refs[:-1]):
        refs[-1][k] = ref[...]


def stack(parts):
    return pl.pallas_call(
        stack_kernel,
        out_shape=shape((len(parts),) + parts[0].shape, parts[0].dtype),
        in_specs=[whole()] * len(parts),
        out_specs=whole(),
        compiler_params=params(4),
        cost_estimate=cost(0, parts[0].size * 4 * len(parts)),
    )(*parts)


def sum_kernel(parts, out):
    total = parts[0].astype(F32)
    for p in range(1, parts.shape[0]):
        total = total + parts[p].astype(F32)
    out[...] = total.astype(BF16)


def sum_parts(parts):
    return pl.pallas_call(
        sum_kernel,
        out_shape=shape(parts.shape[1:], BF16),
        in_specs=[whole()],
        out_specs=whole(),
        compiler_params=params(3),
        cost_estimate=cost(0, parts.size * 3),
    )(parts)


def to_chip(value, bit, n_z):
    return lax.ppermute(value, "z", [(a, a ^ bit) for a in range(n_z)])


def to_core(value):
    return lax.ppermute(value, "core", [(0, 1), (1, 0)])


def complete_z(held, n_z):
    bit = n_z // 2
    while bit:
        for m in range(0, n_z, 2 * bit):
            if m in held and m | bit not in held:
                held[m | bit] = to_chip(held[m], bit, n_z)
        bit //= 2
    return [held[m] for m in range(n_z)]


def reduce_z(evens, odds, n_z, done):
    got = to_chip(odds, 1, n_z)
    held = {2 * k: [(even, None), (got, k)] for k, even in enumerate(evens)}
    bit = 2
    while bit < n_z:
        for m in [m for m in held if m & bit]:
            (term,) = add_all([held.pop(m)], [BF16], done[0])
            held[m ^ bit].append((to_chip(term, bit, n_z), None))
        bit *= 2
    return add_all([held[0]], [BF16], done[1])[0]


def down_kernel(base, place, mine, theirs, grads, *refs):
    out_hbm, gate_hbm, up_hbm, out, gate_factor, up_factor, sems, factor_sems = refs[-8:]
    core0 = place[0] == 0
    n_z, double, ff = mine.shape
    tok, slots = double // 2, out.shape[0]
    copies, factor_copies = [], []
    for k, (at, size) in enumerate(pieces(ff, 512)):
        cols, slot = slice(at, at + size), k % slots
        gate, up = [], []
        for m in range(n_z):
            x, y = mine[m, :, cols].astype(F32), theirs[m, :, cols].astype(F32)
            first, second = jnp.where(core0, x, y), jnp.where(core0, y, x)
            gate += [first[:tok], second[:tok]]
            up += [first[tok:], second[tok:]]
        gate, up = jnp.concatenate(gate, 0), jnp.concatenate(up, 0)
        sig = 1.0 / (1.0 + jnp.exp(-gate))
        silu = gate * sig
        hidden = silu * up
        gate_factor[:, cols] = up * sig * (1.0 + gate * (1.0 - sig))
        up_factor[:, cols] = silu
        for n, (vmem, hbm) in enumerate(((gate_factor, gate_hbm), (up_factor, up_hbm))):
            copy = pltpu.make_async_copy(vmem.at[:, cols], hbm.at[:, cols], factor_sems.at[n, k])
            copy.start()
            factor_copies.append(copy)
        if k >= slots:
            copies[k - slots].wait()
        out[slot, :size, :] = jnp.dot(
            hidden.T.astype(BF16), grads[...], preferred_element_type=F32
        ).astype(BF16)
        copy = pltpu.make_async_copy(
            out.at[slot, :size], out_hbm.at[base + at : base + at + size], sems.at[slot]
        )
        copy.start()
        copies.append(copy)
    for copy in copies[-slots:] + factor_copies:
        copy.wait()


def down_grad(place, mine, theirs, grads, base, total, into=None):
    n_z, _, ff = mine.shape
    tokens, chans = grads.shape
    steps = len(pieces(ff, 512))
    slots = min(4, steps)
    held = [] if into is None else [into]
    return pl.pallas_call(
        functools.partial(down_kernel, base),
        out_shape=(shape((total, chans), BF16),) + (shape((tokens, ff), F32),) * 2,
        in_specs=[whole(SMEM)] + [whole()] * 3 + after(held),
        out_specs=(whole(pltpu.HBM),) * 3,
        scratch_shapes=[VMEM((slots, 512, chans), BF16)]
        + [VMEM((tokens, ff), F32)] * 2
        + [pltpu.SemaphoreType.DMA((slots,)), pltpu.SemaphoreType.DMA((2, steps))],
        input_output_aliases={4: 0} if held else {},
        compiler_params=params(14),
        cost_estimate=cost(2 * tokens * chans * ff, 2 * chans * ff + 8 * tokens * ff),
    )(place, mine, theirs, grads, *held)


def input_kernel(n_z, place, *refs):
    mine, theirs = refs[:n_z], refs[n_z : 2 * n_z]
    factors = (refs[2 * n_z : 2 * n_z + 2], refs[2 * n_z + 2 : 2 * n_z + 4])
    gate_hbm, up_hbm = refs[2 * n_z + 4 : 2 * n_z + 6]
    gate_grad, up_grad, out, w_gate, w_up, gate_factor, up_factor = refs[2 * n_z + 6 : 2 * n_z + 13]
    total, held, sems, factor_sems = refs[2 * n_z + 13 :]
    core0, z = place[0] == 0, place[1]
    rows, width = mine[0].shape
    ff = gate_grad.shape[1]
    low = ff - width
    slots = w_gate.shape[0]
    parts = [(0, at, size) for at, size in pieces(low, 1024, 256)]
    parts += [(low, at, size) for at, size in pieces(width, 1024)]

    def copies(k):
        base, at, size = parts[k]
        return [
            pltpu.make_async_copy(
                hbm.at[:, base + at : base + at + size],
                vmem.at[k % slots, :, :size],
                sems.at[n, k % slots],
            )
            for n, (hbm, vmem) in enumerate(((gate_hbm, w_gate), (up_hbm, w_up)))
        ]

    def factor_copies(k):
        base, at, size = parts[k]
        return [
            pltpu.make_async_copy(
                hbm.at[:, at : at + size],
                vmem.at[:, base + at : base + at + size],
                factor_sems.at[n, k],
            )
            for n, (hbm, vmem) in enumerate(
                zip(factors[0 if base == 0 else 1], (gate_factor, up_factor))
            )
        ]

    for k in range(len(parts)):
        for copy in factor_copies(k) + (copies(k) if k < slots else []):
            copy.start()
    dims = (((1,), (1,)), ((), ()))
    for k, (base, at, size) in enumerate(parts):
        cols = slice(base + at, base + at + size)
        first = core0 if base == 0 else ~core0
        hidden = jnp.concatenate(
            [
                jnp.where(first, mine[m][:, at : at + size], theirs[m][:, at : at + size]).astype(F32)
                for m in range(n_z)
            ],
            0,
        )
        for copy in factor_copies(k):
            copy.wait()
        gate = (hidden * gate_factor[:, cols]).astype(BF16)
        up = (hidden * up_factor[:, cols]).astype(BF16)
        gate_grad[:, cols] = gate
        up_grad[:, cols] = up
        for copy in copies(k):
            copy.wait()
        slot = k % slots
        term = lax.dot_general(w_gate[slot, :, :size], gate, dims, preferred_element_type=F32)
        term += lax.dot_general(w_up[slot, :, :size], up, dims, preferred_element_type=F32)
        total[...] = term if k == 0 else total[...] + term
        if k + slots < len(parts):
            for copy in copies(k + slots):
                copy.start()
    turned = total[...].T
    for m in range(n_z):
        held[pl.ds(pl.multiple_of((z ^ m) * rows, math.gcd(rows, 8)), rows), :] = turned[m * rows : (m + 1) * rows]
    n_t = out.shape[0]
    step = held.shape[0] // n_t
    for p in range(n_t):
        out[p] = held[p * step : (p + 1) * step, :].astype(BF16)


def input_grad(place, mine, theirs, factors, w_gate, w_up, n_t):
    tokens = factors[0].shape[0]
    chans, ff = w_gate.shape
    low, width = factors[0].shape[1], factors[2].shape[1]
    steps = len(pieces(low, 1024, 256)) + len(pieces(width, 1024))
    n_z, slots = len(mine), 3
    return pl.pallas_call(
        functools.partial(input_kernel, n_z),
        out_shape=(shape((tokens, ff), BF16),) * 2 + (shape((n_t, tokens // n_t, chans), BF16),),
        in_specs=[whole(SMEM)] + [whole()] * (2 * n_z) + [whole(pltpu.HBM)] * 6,
        out_specs=(whole(),) * 3,
        scratch_shapes=[
            VMEM((slots, chans, min(ff, 1024)), BF16),
            VMEM((slots, chans, min(ff, 1024)), BF16),
            VMEM((tokens, ff), F32),
            VMEM((tokens, ff), F32),
            VMEM((chans, tokens), F32),
            VMEM((tokens, chans), F32),
            pltpu.SemaphoreType.DMA((2, slots)),
            pltpu.SemaphoreType.DMA((2, steps)),
        ],
        compiler_params=params(50),
        cost_estimate=cost(4 * tokens * chans * ff, 4 * chans * ff + 12 * tokens * ff),
    )(place, *mine, *theirs, *factors, w_gate, w_up)


def weight_kernel(n_z, n_t, place, *refs):
    gate_grad, up_grad, gate_hbm, up_hbm, out, held, inputs_t, sems = refs[n_t:]
    hold(refs[:n_t], place[2], held)
    inputs_t[...] = blocks_of(held, place[1], n_z).T.astype(BF16)
    copies = []
    ff, slots = gate_grad.shape[1], out.shape[0]
    for grad, hbm in ((gate_grad, gate_hbm), (up_grad, up_hbm)):
        for at, size in pieces(ff, 512):
            cols, slot = slice(at, at + size), len(copies) % slots
            if len(copies) >= slots:
                copies[len(copies) - slots].wait()
            out[slot, :, :size] = jnp.dot(
                inputs_t[...], grad[:, cols], preferred_element_type=F32
            ).astype(BF16)
            copy = pltpu.make_async_copy(out.at[slot, :, :size], hbm.at[:, cols], sems.at[slot])
            copy.start()
            copies.append(copy)
    for copy in copies[-slots:]:
        copy.wait()


def weight_grads(place, parts, gate_grad, up_grad, n_z):
    n_t, chans, tokens = len(parts), parts[0].shape[1], gate_grad.shape[0]
    ff = gate_grad.shape[1]
    slots = min(8, 2 * len(pieces(ff, 512)))
    return pl.pallas_call(
        functools.partial(weight_kernel, n_z, n_t),
        out_shape=(shape((chans, ff), BF16),) * 2,
        in_specs=[whole(SMEM)] + [whole()] * (n_t + 2),
        out_specs=(whole(pltpu.HBM),) * 2,
        scratch_shapes=[
            VMEM((slots, chans, 512), BF16),
            VMEM((tokens, chans), F32),
            VMEM((chans, tokens), BF16),
            pltpu.SemaphoreType.DMA((slots,)),
        ],
        compiler_params=params(16),
        cost_estimate=cost(4 * tokens * chans * ff, 4 * chans * ff + 4 * tokens * ff),
    )(place, *parts, gate_grad, up_grad)


def on_device(n_z, n_t, xq, xs, xo, xc, gq, gs, go, gc, gate_pre, up_pre, w_gate, w_up, w_down):
    place = jnp.stack([lax.axis_index(name) for name in ("core", "z", "tensor")]).astype(jnp.int32)
    ff = gate_pre.shape[1]
    width = -(-ff // 256) * 128

    def from_tensor(own):
        return [own] + [
            lax.ppermute(own, "tensor", [(a, a ^ s) for a in range(n_t)]) for s in range(1, n_t)
        ]

    cuts = (ff - width, width)
    grads, inputs, *halves = prep(cuts, xq, xs, xo, xc, gq, gs, go, gc, gate_pre, up_pre)
    bit = n_z // 2
    grads = from_tensor(grads)
    a, b = {0: halves[0]}, {0: halves[1]}
    a |= {bit: to_chip(a[0], bit, n_z), 1: to_chip(a[0], 1, n_z)}
    grads, grads_t, send = first_half(place, grads, w_down, n_z, width, a[bit], a[1])
    got = to_core(send)
    a[bit | 1] = to_chip(a[bit], 1, n_z)
    b[bit] = to_chip(b[0], bit, n_z)
    mine = second_half(place, grads_t, w_down, n_z, width, a[bit | 1], b[bit])
    b |= {1: to_chip(b[0], 1, n_z), bit | 1: to_chip(b[bit], 1, n_z)}
    *evens, odds = pair_sum(place, mine, got, b[1], b[bit | 1])
    a, b = stack(complete_z(a, n_z)), stack(complete_z(b, n_z))
    a_other, b_other = to_core(a), to_core(b)
    inputs = from_tensor(inputs)
    grad_down, *factors = down_grad(place, a, a_other, grads, 0, ff)
    hidden = {0: reduce_z(evens, odds, n_z, (inputs[1:], (factors[0], b_other)))}
    hidden |= {bit: to_chip(hidden[0], bit, n_z), 1: to_chip(hidden[0], 1, n_z)}
    grad_down, *more = down_grad(place, b, b_other, grads, ff - width, ff, grad_down)
    (hidden[bit],) = add_all([[(hidden[bit], None)]], [BF16], [more[0], hidden[1]])
    hidden_grad = complete_z(hidden, n_z)
    gate_grad, up_grad, sends = input_grad(
        place, hidden_grad, [to_core(part) for part in hidden_grad], factors + more, w_gate, w_up, n_t
    )
    terms = lax.all_to_all(sends, "tensor", 0, 0, tiled=True)
    grad_gate, grad_up = weight_grads(place, inputs, gate_grad, up_grad, n_z)
    return sum_parts(terms), grad_gate, grad_up, grad_down


def solution(mesh):
    n_dp, n_t = mesh.shape["dp"], mesh.shape["tensor"]
    fine = Mesh(mesh.devices.reshape(n_dp // 2, 2, n_t), ("z", "core", "tensor"))
    by_token, by_dp = P("tensor", ("z", "core")), P(("z", "core"), "tensor")
    return jax.shard_map(
        functools.partial(on_device, n_dp // 2, n_t),
        mesh=fine,
        in_specs=(by_token,) * 8 + (by_dp,) * 4 + (by_token,),
        out_specs=(by_token, by_dp, by_dp, by_token),
        check_vma=False,
    )
```

```python
import functools
import math

import jax
import jax.numpy as jnp
from jax import lax
from jax.experimental import pallas as pl
from jax.experimental.pallas import tpu as pltpu
from jax.sharding import Mesh
from jax.sharding import PartitionSpec as P

BLK_C = 128
F32 = jnp.float32
BF16 = jnp.bfloat16
VMEM = pltpu.VMEM
SMEM = pltpu.SMEM


def after(arrays):
    return [pl.BlockSpec(memory_space=pl.ANY)] * len(arrays)


def whole(space=VMEM):
    return pl.BlockSpec(memory_space=space)


def shape(dims, dtype):
    return jax.ShapeDtypeStruct(dims, dtype)


def params(mib):
    return pltpu.CompilerParams(vmem_limit_bytes=mib * 1024 * 1024)


def cost(flops, nbytes):
    return pl.CostEstimate(flops=int(flops), bytes_accessed=int(nbytes), transcendentals=0)


def pieces(extent, step, first=0):
    cuts = [0] + list(range(first or step, extent, step)) + [extent]
    return [(a, b - a) for a, b in zip(cuts[:-1], cuts[1:])]


def prep_kernel(xq, xs, xo, xc, gq, gs, go, gc, gate, up, grads, inputs, *halves):
    for out, quant, scale, flag, corr in ((grads, gq, gs, go, gc), (inputs, xq, xs, xo, xc)):
        for b in range(scale.shape[1]):
            cols = slice(b * BLK_C, (b + 1) * BLK_C)
            value = scale[0, b] * quant[:, cols].astype(F32) + flag[0, b].astype(F32) * corr[
                :, cols
            ].astype(F32)
            out[:, cols] = value.astype(BF16)
    at = 0
    for half in halves:
        cols = slice(at, at + half.shape[1])
        at += half.shape[1]
        half[...] = jnp.concatenate(
            [gate[:, cols].astype(F32), up[:, cols].astype(F32)], 0
        ).astype(BF16)


def prep(cuts, xq, xs, xo, xc, gq, gs, go, gc, gate, up):
    rows, width = xq.shape
    tok, ff = gate.shape
    return pl.pallas_call(
        prep_kernel,
        out_shape=(shape((rows, width), BF16),) * 2
        + tuple(shape((2 * tok, size), BF16) for size in cuts),
        in_specs=[whole(), whole(SMEM), whole(SMEM), whole()] * 2 + [whole()] * 2,
        out_specs=(whole(),) * (2 + len(cuts)),
        compiler_params=params(56),
        cost_estimate=cost(0, 4 * xq.size * 2 + gate.size * 8),
    )(xq, xs, xo, xc, gq, gs, go, gc, gate, up)


def load_down(start, width, w_hbm, w_vmem, sems):
    copies = []
    for k, (at, size) in enumerate(pieces(width, 1024, 256)):
        first = pl.multiple_of(start + at, 16)
        copy = pltpu.make_async_copy(
            w_hbm.at[pl.ds(first, size)], w_vmem.at[pl.ds(at, size)], sems.at[k]
        )
        copy.start()
        copies.append(copy)
    return copies


def hidden_half(copies, grads_t, width, w_vmem, outs):
    rows = outs[0].shape[0]
    for copy, (at, size) in zip(copies, pieces(width, 1024, 256)):
        copy.wait()
        total = jnp.dot(w_vmem[at : at + size, :], grads_t, preferred_element_type=F32).T
        for q, out in enumerate(outs):
            out[:, at : at + size] = total[q * rows : (q + 1) * rows, :].astype(out.dtype)


def blocks_of(held, z, n_z):
    block = held.shape[0] // n_z
    return jnp.concatenate(
        [
            held[pl.ds(pl.multiple_of((z ^ m) * block, math.gcd(block, 8)), block), :]
            for m in range(n_z)
        ],
        0,
    )


def hold(parts, me, held):
    rows = parts[0].shape[0]
    for s, part in enumerate(parts):
        start = pl.multiple_of((me ^ s) * rows, math.gcd(rows, 8))
        held[pl.ds(start, rows), :] = part[...].astype(F32)


def first_half_kernel(n_t, n_z, offset, place, *refs):
    parts, w_hbm = refs[:n_t], refs[n_t]
    grads_out, grads_t, *outs = refs[-5 - n_z : -3]
    w_vmem, held, sems = refs[-3:]
    width = outs[0].shape[1]
    copies = load_down((1 - place[0]) * offset, width, w_hbm, w_vmem, sems)
    hold(parts, place[2], held)
    grads_t[...] = held[...].T.astype(BF16)
    grads_out[...] = blocks_of(held, place[1], n_z).astype(BF16)
    hidden_half(copies, grads_t[...], width, w_vmem, outs)


def second_half_kernel(offset, place, grads_t, w_hbm, *refs):
    out, w_vmem, sems = refs[-3:]
    width = out.shape[2]
    outs = [out.at[q] for q in range(out.shape[0])]
    copies = load_down(place[0] * offset, width, w_hbm, w_vmem, sems)
    hidden_half(copies, grads_t[...], width, w_vmem, outs)


def first_half(place, parts, w_down, n_z, width, *done):
    n_t, (rows, chans) = len(parts), parts[0].shape
    tokens = n_t * rows
    n_copies = len(pieces(width, 1024, 256))
    return pl.pallas_call(
        functools.partial(first_half_kernel, n_t, n_z, w_down.shape[0] - width),
        out_shape=(
            shape((tokens, chans), BF16),
            shape((chans, tokens), BF16),
        )
        + (shape((tokens // n_z, width), BF16),) * n_z,
        in_specs=[whole(SMEM)] + [whole()] * n_t + [whole(pltpu.HBM)] + after(done),
        out_specs=(whole(),) * (2 + n_z),
        scratch_shapes=[
            VMEM((width, chans), BF16),
            VMEM((tokens, chans), F32),
            pltpu.SemaphoreType.DMA((n_copies,)),
        ],
        compiler_params=params(52),
        cost_estimate=cost(2 * tokens * chans * width, 2 * chans * width),
    )(place, *parts, w_down, *done)


def second_half(place, grads_t, w_down, n_z, width, *done):
    chans, tokens = grads_t.shape
    n_copies = len(pieces(width, 1024, 256))
    return pl.pallas_call(
        functools.partial(second_half_kernel, w_down.shape[0] - width),
        out_shape=shape((n_z, tokens // n_z, width), F32),
        in_specs=[whole(SMEM), whole(), whole(pltpu.HBM)] + after(done),
        out_specs=whole(),
        scratch_shapes=[VMEM((width, chans), BF16), pltpu.SemaphoreType.DMA((n_copies,))],
        compiler_params=params(52),
        cost_estimate=cost(8 * tokens * chans * width, 8 * chans * width),
    )(place, grads_t, w_down, *done)


def pair_kernel(place, mine, *refs):
    n_z = mine.shape[0]
    theirs, outs, total_ref = refs[:n_z], refs[-2 - n_z // 2 : -1], refs[-1]
    for q in range(n_z):
        total_ref[q] = mine[q] + theirs[q][...].astype(F32)
    for m in range(n_z):
        total = total_ref[place[1] ^ m]
        if m % 2:
            outs[-1][m // 2] = total.astype(BF16)
        else:
            outs[m // 2][...] = total


def pair_sum(place, mine, theirs, *done):
    n_z, rows, width = mine.shape
    return pl.pallas_call(
        pair_kernel,
        out_shape=(shape((rows, width), F32),) * (n_z // 2)
        + (shape((n_z // 2, rows, width), BF16),),
        in_specs=[whole(SMEM)] + [whole()] * (1 + n_z) + after(done),
        out_specs=(whole(),) * (n_z // 2 + 1),
        scratch_shapes=[VMEM(mine.shape, F32)],
        compiler_params=params(6),
        cost_estimate=cost(0, mine.size * 9),
    )(place, mine, *theirs, *done)


def add_kernel(picks, n_refs, *refs):
    outs = refs[-len(picks) :]
    for pick, out in zip(picks, outs):
        total = None
        for ref, row in pick:
            term = (refs[ref][...] if row is None else refs[ref][row]).astype(F32)
            total = term if total is None else total + term
        out[...] = total.astype(out.dtype)


def add_all(lists, dtypes, done=()):
    arrays, picks = [], []
    for terms in lists:
        pick = []
        for array, row in terms:
            at = next((k for k, known in enumerate(arrays) if known is array), len(arrays))
            if at == len(arrays):
                arrays.append(array)
            pick.append((at, row))
        picks.append(pick)
    dims = lists[0][0][0].shape[-2:]
    return pl.pallas_call(
        functools.partial(add_kernel, picks, len(arrays)),
        out_shape=tuple(shape(dims, dtype) for dtype in dtypes),
        in_specs=[whole()] * len(arrays) + after(done),
        out_specs=(whole(),) * len(lists),
        compiler_params=params(6),
        cost_estimate=cost(0, dims[0] * dims[1] * 6 * sum(map(len, lists))),
    )(*arrays, *done)


def sum_kernel(parts, out):
    total = parts[0].astype(F32)
    for p in range(1, parts.shape[0]):
        total = total + parts[p].astype(F32)
    out[...] = total.astype(BF16)


def sum_parts(parts):
    return pl.pallas_call(
        sum_kernel,
        out_shape=shape(parts.shape[1:], BF16),
        in_specs=[whole()],
        out_specs=whole(),
        compiler_params=params(3),
        cost_estimate=cost(0, parts.size * 3),
    )(parts)


def to_chip(value, bit, n_z):
    return lax.ppermute(value, "z", [(a, a ^ bit) for a in range(n_z)])


def to_core(value):
    return lax.ppermute(value, "core", [(0, 1), (1, 0)])


def complete_z(held, n_z):
    bit = n_z // 2
    while bit:
        for m in range(0, n_z, 2 * bit):
            if m in held and m | bit not in held:
                held[m | bit] = to_chip(held[m], bit, n_z)
        bit //= 2
    return [held[m] for m in range(n_z)]


def reduce_z(evens, odds, n_z, done):
    got = to_chip(odds, 1, n_z)
    held = {2 * k: [(even, None), (got, k)] for k, even in enumerate(evens)}
    bit = 2
    while bit < n_z:
        for m in [m for m in held if m & bit]:
            (term,) = add_all([held.pop(m)], [BF16], done[0])
            held[m ^ bit].append((to_chip(term, bit, n_z), None))
        bit *= 2
    return add_all([held[0]], [BF16], done[1])[0]


def gate_up_rows(core0, mine, theirs, cols):
    tok = mine[0].shape[0] // 2
    gate, up = [], []
    for own, other in zip(mine, theirs):
        x, y = own[:, cols].astype(F32), other[:, cols].astype(F32)
        first, second = jnp.where(core0, x, y), jnp.where(core0, y, x)
        gate += [first[:tok], second[:tok]]
        up += [first[tok:], second[tok:]]
    return jnp.concatenate(gate, 0), jnp.concatenate(up, 0)


def down_kernel(base, n_z, place, *refs):
    mine, theirs, grads = refs[:n_z], refs[n_z : 2 * n_z], refs[2 * n_z]
    out_hbm, token, out, sems = refs[-4:]
    token[...] = jnp.zeros_like(token)
    slots, copies = out.shape[0], []
    for k, (at, size) in enumerate(pieces(mine[0].shape[1], 512)):
        slot = k % slots
        gate, up = gate_up_rows(place[0] == 0, mine, theirs, slice(at, at + size))
        hidden = gate * (1.0 / (1.0 + jnp.exp(-gate))) * up
        if k >= slots:
            copies[k - slots].wait()
        out[slot, :size, :] = jnp.dot(
            hidden.T.astype(BF16), grads[...], preferred_element_type=F32
        ).astype(BF16)
        copy = pltpu.make_async_copy(
            out.at[slot, :size], out_hbm.at[base + at : base + at + size], sems.at[slot]
        )
        copy.start()
        copies.append(copy)
    for copy in copies[-slots:]:
        copy.wait()


def down_grad(place, mine, theirs, grads, base, total, into=None):
    n_z, ff = len(mine), mine[0].shape[1]
    tokens, chans = grads.shape
    slots = min(4, len(pieces(ff, 512)))
    held = [] if into is None else [into]
    return pl.pallas_call(
        functools.partial(down_kernel, base, n_z),
        out_shape=(shape((total, chans), BF16), shape((8, 128), F32)),
        in_specs=[whole(SMEM)] + [whole()] * (2 * n_z + 1) + after(held),
        out_specs=(whole(pltpu.HBM), whole()),
        scratch_shapes=[VMEM((slots, 512, chans), BF16), pltpu.SemaphoreType.DMA((slots,))],
        input_output_aliases={2 * n_z + 2: 0} if held else {},
        compiler_params=params(12),
        cost_estimate=cost(2 * tokens * chans * ff, 2 * chans * ff),
    )(place, *mine, *theirs, grads, *held)


def input_kernel(n_z, place, *refs):
    hidden, rows_a, rows_b = [
        (refs[2 * k * n_z : (2 * k + 1) * n_z], refs[(2 * k + 1) * n_z : (2 * k + 2) * n_z])
        for k in range(3)
    ]
    gate_hbm, up_hbm, gate_grad, up_grad, out, w_gate, w_up, total, held, sems = refs[6 * n_z :]
    core0, z = place[0] == 0, place[1]
    rows, width = hidden[0][0].shape
    ff = gate_grad.shape[1]
    low = ff - width
    slots = w_gate.shape[0]
    parts = [(0, at, size) for at, size in pieces(low, 1024, 256)]
    parts += [(low, at, size) for at, size in pieces(width, 1024)]

    def copies(k):
        base, at, size = parts[k]
        return [
            pltpu.make_async_copy(
                hbm.at[:, base + at : base + at + size],
                vmem.at[k % slots, :, :size],
                sems.at[n, k % slots],
            )
            for n, (hbm, vmem) in enumerate(((gate_hbm, w_gate), (up_hbm, w_up)))
        ]

    def gradients(k):
        base, at, size = parts[k]
        cols, span = slice(base + at, base + at + size), slice(at, at + size)
        first = core0 if base == 0 else ~core0
        grad = jnp.concatenate(
            [
                jnp.where(first, own[:, span], other[:, span]).astype(F32)
                for own, other in zip(*hidden)
            ],
            0,
        )
        gate, up = gate_up_rows(core0, *(rows_a if base == 0 else rows_b), span)
        sig = 1.0 / (1.0 + jnp.exp(-gate))
        gate_grad[:, cols] = (grad * up * sig * (1.0 + gate * (1.0 - sig))).astype(BF16)
        up_grad[:, cols] = (grad * (gate * sig)).astype(BF16)

    for k in range(min(slots, len(parts))):
        for copy in copies(k):
            copy.start()
    gradients(0)
    dims = (((1,), (1,)), ((), ()))
    for k, (base, at, size) in enumerate(parts):
        for copy in copies(k):
            copy.wait()
        cols, slot = slice(base + at, base + at + size), k % slots
        term = lax.dot_general(
            w_gate[slot, :, :size], gate_grad[:, cols], dims, preferred_element_type=F32
        )
        term += lax.dot_general(
            w_up[slot, :, :size], up_grad[:, cols], dims, preferred_element_type=F32
        )
        total[...] = term if k == 0 else total[...] + term
        if k + 1 < len(parts):
            gradients(k + 1)
        if k + slots < len(parts):
            for copy in copies(k + slots):
                copy.start()
    turned = total[...].T
    for m in range(n_z):
        start = pl.multiple_of((z ^ m) * rows, math.gcd(rows, 8))
        held[pl.ds(start, rows), :] = turned[m * rows : (m + 1) * rows]
    n_t = out.shape[0]
    step = held.shape[0] // n_t
    for p in range(n_t):
        out[p] = held[p * step : (p + 1) * step, :].astype(BF16)


def input_grad(place, hidden, rows_a, rows_b, w_gate, w_up, n_t):
    n_z, slots = len(hidden[0]), 3
    tokens = n_z * hidden[0][0].shape[0]
    chans, ff = w_gate.shape
    return pl.pallas_call(
        functools.partial(input_kernel, n_z),
        out_shape=(shape((tokens, ff), BF16),) * 2 + (shape((n_t, tokens // n_t, chans), BF16),),
        in_specs=[whole(SMEM)] + [whole()] * (6 * n_z) + [whole(pltpu.HBM)] * 2,
        out_specs=(whole(),) * 3,
        scratch_shapes=[
            VMEM((slots, chans, min(ff, 1024)), BF16),
            VMEM((slots, chans, min(ff, 1024)), BF16),
            VMEM((chans, tokens), F32),
            VMEM((tokens, chans), F32),
            pltpu.SemaphoreType.DMA((2, slots)),
        ],
        compiler_params=params(42),
        cost_estimate=cost(4 * tokens * chans * ff, 4 * chans * ff + 12 * tokens * ff),
    )(place, *hidden[0], *hidden[1], *rows_a[0], *rows_a[1], *rows_b[0], *rows_b[1], w_gate, w_up)


def weight_kernel(n_z, n_t, place, *refs):
    gate_grad, up_grad, gate_hbm, up_hbm, out, held, inputs_t, sems = refs[n_t:]
    hold(refs[:n_t], place[2], held)
    inputs_t[...] = blocks_of(held, place[1], n_z).T.astype(BF16)
    copies = []
    ff, slots = gate_grad.shape[1], out.shape[0]
    for grad, hbm in ((gate_grad, gate_hbm), (up_grad, up_hbm)):
        for at, size in pieces(ff, 512):
            cols, slot = slice(at, at + size), len(copies) % slots
            if len(copies) >= slots:
                copies[len(copies) - slots].wait()
            out[slot, :, :size] = jnp.dot(
                inputs_t[...], grad[:, cols], preferred_element_type=F32
            ).astype(BF16)
            copy = pltpu.make_async_copy(out.at[slot, :, :size], hbm.at[:, cols], sems.at[slot])
            copy.start()
            copies.append(copy)
    for copy in copies[-slots:]:
        copy.wait()


def weight_grads(place, parts, gate_grad, up_grad, n_z):
    n_t, chans, tokens = len(parts), parts[0].shape[1], gate_grad.shape[0]
    ff = gate_grad.shape[1]
    slots = min(8, 2 * len(pieces(ff, 512)))
    return pl.pallas_call(
        functools.partial(weight_kernel, n_z, n_t),
        out_shape=(shape((chans, ff), BF16),) * 2,
        in_specs=[whole(SMEM)] + [whole()] * (n_t + 2),
        out_specs=(whole(pltpu.HBM),) * 2,
        scratch_shapes=[
            VMEM((slots, chans, 512), BF16),
            VMEM((tokens, chans), F32),
            VMEM((chans, tokens), BF16),
            pltpu.SemaphoreType.DMA((slots,)),
        ],
        compiler_params=params(16),
        cost_estimate=cost(4 * tokens * chans * ff, 4 * chans * ff + 4 * tokens * ff),
    )(place, *parts, gate_grad, up_grad)


def on_device(n_z, n_t, xq, xs, xo, xc, gq, gs, go, gc, gate_pre, up_pre, w_gate, w_up, w_down):
    place = jnp.stack([lax.axis_index(name) for name in ("core", "z", "tensor")]).astype(jnp.int32)
    ff = gate_pre.shape[1]
    width = -(-ff // 256) * 128

    def from_tensor(own):
        return [own] + [
            lax.ppermute(own, "tensor", [(a, a ^ s) for a in range(n_t)]) for s in range(1, n_t)
        ]

    cuts = (ff - width, width)
    grads, inputs, *halves = prep(cuts, xq, xs, xo, xc, gq, gs, go, gc, gate_pre, up_pre)
    bit = n_z // 2
    grads = from_tensor(grads)
    a, b = {0: halves[0]}, {0: halves[1]}
    a |= {bit: to_chip(a[0], bit, n_z), 1: to_chip(a[0], 1, n_z)}
    grads, grads_t, *send = first_half(place, grads, w_down, n_z, width, a[bit], a[1])
    got = [to_core(part) for part in send]
    a[bit | 1] = to_chip(a[bit], 1, n_z)
    b[bit] = to_chip(b[0], bit, n_z)
    mine = second_half(place, grads_t, w_down, n_z, width, a[bit | 1], b[bit])
    b |= {1: to_chip(b[0], 1, n_z), bit | 1: to_chip(b[bit], 1, n_z)}
    *evens, odds = pair_sum(place, mine, got, b[1], b[bit | 1])
    a, b = complete_z(a, n_z), complete_z(b, n_z)
    rows_a, rows_b = [(held, [to_core(part) for part in held]) for held in (a, b)]
    inputs = from_tensor(inputs)
    grad_down, token = down_grad(place, *rows_a, grads, 0, ff)
    hidden = {0: reduce_z(evens, odds, n_z, (inputs[1:], (token, *rows_b[1])))}
    hidden |= {bit: to_chip(hidden[0], bit, n_z), 1: to_chip(hidden[0], 1, n_z)}
    grad_down, token = down_grad(place, *rows_b, grads, ff - width, ff, grad_down)
    (hidden[bit],) = add_all([[(hidden[bit], None)]], [BF16], [token, hidden[1]])
    hidden = complete_z(hidden, n_z)
    gate_grad, up_grad, sends = input_grad(
        place, (hidden, [to_core(part) for part in hidden]), rows_a, rows_b, w_gate, w_up, n_t
    )
    terms = lax.all_to_all(sends, "tensor", 0, 0, tiled=True)
    grad_gate, grad_up = weight_grads(place, inputs, gate_grad, up_grad, n_z)
    return sum_parts(terms), grad_gate, grad_up, grad_down


def solution(mesh):
    n_dp, n_t = mesh.shape["dp"], mesh.shape["tensor"]
    fine = Mesh(mesh.devices.reshape(n_dp // 2, 2, n_t), ("z", "core", "tensor"))
    by_token, by_dp = P("tensor", ("z", "core")), P(("z", "core"), "tensor")
    return jax.shard_map(
        functools.partial(on_device, n_dp // 2, n_t),
        mesh=fine,
        in_specs=(by_token,) * 8 + (by_dp,) * 4 + (by_token,),
        out_specs=(by_token, by_dp, by_dp, by_token),
        check_vma=False,
    )
```

```python
import functools
import math

import jax
import jax.numpy as jnp
from jax import lax
from jax.experimental import pallas as pl
from jax.experimental.pallas import tpu as pltpu
from jax.sharding import Mesh
from jax.sharding import PartitionSpec as P

BLK_C = 128
F32 = jnp.float32
BF16 = jnp.bfloat16
VMEM = pltpu.VMEM
SMEM = pltpu.SMEM


def after(arrays):
    return [pl.BlockSpec(memory_space=pl.ANY)] * len(arrays)


def whole(space=VMEM):
    return pl.BlockSpec(memory_space=space)


def shape(dims, dtype):
    return jax.ShapeDtypeStruct(dims, dtype)


def params(mib):
    return pltpu.CompilerParams(vmem_limit_bytes=mib * 1024 * 1024)


def cost(flops, nbytes):
    return pl.CostEstimate(flops=int(flops), bytes_accessed=int(nbytes), transcendentals=0)


def pieces(extent, step, first=0):
    cuts = [0] + list(range(first or step, extent, step)) + [extent]
    return [(a, b - a) for a, b in zip(cuts[:-1], cuts[1:])]


def prep_kernel(xq, xs, xo, xc, gq, gs, go, gc, gate, up, grads, inputs, *halves):
    for out, quant, scale, flag, corr in ((grads, gq, gs, go, gc), (inputs, xq, xs, xo, xc)):
        for b in range(scale.shape[1]):
            cols = slice(b * BLK_C, (b + 1) * BLK_C)
            value = scale[0, b] * quant[:, cols].astype(F32) + flag[0, b].astype(F32) * corr[
                :, cols
            ].astype(F32)
            out[:, cols] = value.astype(BF16)
    at = 0
    for half in halves:
        cols = slice(at, at + half.shape[1])
        at += half.shape[1]
        half[...] = jnp.concatenate(
            [gate[:, cols].astype(F32), up[:, cols].astype(F32)], 0
        ).astype(BF16)


def prep(cuts, xq, xs, xo, xc, gq, gs, go, gc, gate, up):
    rows, width = xq.shape
    tok, ff = gate.shape
    return pl.pallas_call(
        prep_kernel,
        out_shape=(shape((rows, width), BF16),) * 2
        + tuple(shape((2 * tok, size), BF16) for size in cuts),
        in_specs=[whole(), whole(SMEM), whole(SMEM), whole()] * 2 + [whole()] * 2,
        out_specs=(whole(),) * (2 + len(cuts)),
        compiler_params=params(56),
        cost_estimate=cost(0, 4 * xq.size * 2 + gate.size * 8),
    )(xq, xs, xo, xc, gq, gs, go, gc, gate, up)


def load_down(start, width, w_hbm, w_vmem, sems):
    copies = []
    for k, (at, size) in enumerate(pieces(width, 1024, 256)):
        first = pl.multiple_of(start + at, 16)
        copy = pltpu.make_async_copy(
            w_hbm.at[pl.ds(first, size)], w_vmem.at[pl.ds(at, size)], sems.at[k]
        )
        copy.start()
        copies.append(copy)
    return copies


def hidden_half(copies, grads_t, width, w_vmem, outs):
    rows = outs[0].shape[0]
    for copy, (at, size) in zip(copies, pieces(width, 1024, 256)):
        copy.wait()
        total = jnp.dot(w_vmem[at : at + size, :], grads_t, preferred_element_type=F32).T
        for q, out in enumerate(outs):
            out[:, at : at + size] = total[q * rows : (q + 1) * rows, :].astype(out.dtype)


def blocks_of(held, z, n_z):
    block = held.shape[0] // n_z
    return jnp.concatenate(
        [
            held[pl.ds(pl.multiple_of((z ^ m) * block, math.gcd(block, 8)), block), :]
            for m in range(n_z)
        ],
        0,
    )


def hold(parts, me, held):
    rows = parts[0].shape[0]
    for s, part in enumerate(parts):
        start = pl.multiple_of((me ^ s) * rows, math.gcd(rows, 8))
        held[pl.ds(start, rows), :] = part[...].astype(F32)


def first_half_kernel(n_t, n_z, offset, place, *refs):
    parts, w_hbm = refs[:n_t], refs[n_t]
    grads_out, grads_t, *outs = refs[-5 - n_z : -3]
    w_vmem, held, sems = refs[-3:]
    width = outs[0].shape[1]
    copies = load_down((1 - place[0]) * offset, width, w_hbm, w_vmem, sems)
    hold(parts, place[2], held)
    grads_t[...] = held[...].T.astype(BF16)
    grads_out[...] = blocks_of(held, place[1], n_z).astype(BF16)
    hidden_half(copies, grads_t[...], width, w_vmem, outs)


def second_half_kernel(offset, place, grads_t, w_hbm, *refs):
    out, w_vmem, sems = refs[-3:]
    width = out.shape[2]
    outs = [out.at[q] for q in range(out.shape[0])]
    copies = load_down(place[0] * offset, width, w_hbm, w_vmem, sems)
    hidden_half(copies, grads_t[...], width, w_vmem, outs)


def first_half(place, parts, w_down, n_z, width, *done):
    n_t, (rows, chans) = len(parts), parts[0].shape
    tokens = n_t * rows
    n_copies = len(pieces(width, 1024, 256))
    return pl.pallas_call(
        functools.partial(first_half_kernel, n_t, n_z, w_down.shape[0] - width),
        out_shape=(
            shape((tokens, chans), BF16),
            shape((chans, tokens), BF16),
        )
        + (shape((tokens // n_z, width), BF16),) * n_z,
        in_specs=[whole(SMEM)] + [whole()] * n_t + [whole(pltpu.HBM)] + after(done),
        out_specs=(whole(),) * (2 + n_z),
        scratch_shapes=[
            VMEM((width, chans), BF16),
            VMEM((tokens, chans), F32),
            pltpu.SemaphoreType.DMA((n_copies,)),
        ],
        compiler_params=params(52),
        cost_estimate=cost(2 * tokens * chans * width, 2 * chans * width),
    )(place, *parts, w_down, *done)


def second_half(place, grads_t, w_down, n_z, width, *done):
    chans, tokens = grads_t.shape
    n_copies = len(pieces(width, 1024, 256))
    return pl.pallas_call(
        functools.partial(second_half_kernel, w_down.shape[0] - width),
        out_shape=shape((n_z, tokens // n_z, width), F32),
        in_specs=[whole(SMEM), whole(), whole(pltpu.HBM)] + after(done),
        out_specs=whole(),
        scratch_shapes=[VMEM((width, chans), BF16), pltpu.SemaphoreType.DMA((n_copies,))],
        compiler_params=params(52),
        cost_estimate=cost(8 * tokens * chans * width, 8 * chans * width),
    )(place, grads_t, w_down, *done)


def pair_kernel(place, mine, *refs):
    n_z = mine.shape[0]
    theirs, outs, total_ref = refs[:n_z], refs[-2 - n_z // 2 : -1], refs[-1]
    for q in range(n_z):
        total_ref[q] = mine[q] + theirs[q][...].astype(F32)
    for m in range(n_z):
        total = total_ref[place[1] ^ m]
        if m % 2:
            outs[-1][m // 2] = total.astype(BF16)
        else:
            outs[m // 2][...] = total


def pair_sum(place, mine, theirs, *done):
    n_z, rows, width = mine.shape
    return pl.pallas_call(
        pair_kernel,
        out_shape=(shape((rows, width), F32),) * (n_z // 2)
        + (shape((n_z // 2, rows, width), BF16),),
        in_specs=[whole(SMEM)] + [whole()] * (1 + n_z) + after(done),
        out_specs=(whole(),) * (n_z // 2 + 1),
        scratch_shapes=[VMEM(mine.shape, F32)],
        compiler_params=params(6),
        cost_estimate=cost(0, mine.size * 9),
    )(place, mine, *theirs, *done)


def add_kernel(picks, n_refs, *refs):
    outs = refs[-len(picks) :]
    for pick, out in zip(picks, outs):
        total = None
        for ref, row in pick:
            term = (refs[ref][...] if row is None else refs[ref][row]).astype(F32)
            total = term if total is None else total + term
        out[...] = total.astype(out.dtype)


def add_all(lists, dtypes, done=()):
    arrays, picks = [], []
    for terms in lists:
        pick = []
        for array, row in terms:
            at = next((k for k, known in enumerate(arrays) if known is array), len(arrays))
            if at == len(arrays):
                arrays.append(array)
            pick.append((at, row))
        picks.append(pick)
    dims = lists[0][0][0].shape[-2:]
    return pl.pallas_call(
        functools.partial(add_kernel, picks, len(arrays)),
        out_shape=tuple(shape(dims, dtype) for dtype in dtypes),
        in_specs=[whole()] * len(arrays) + after(done),
        out_specs=(whole(),) * len(lists),
        compiler_params=params(6),
        cost_estimate=cost(0, dims[0] * dims[1] * 6 * sum(map(len, lists))),
    )(*arrays, *done)


def sum_kernel(parts, out):
    total = parts[0].astype(F32)
    for p in range(1, parts.shape[0]):
        total = total + parts[p].astype(F32)
    out[...] = total.astype(BF16)


def sum_parts(parts):
    return pl.pallas_call(
        sum_kernel,
        out_shape=shape(parts.shape[1:], BF16),
        in_specs=[whole()],
        out_specs=whole(),
        compiler_params=params(3),
        cost_estimate=cost(0, parts.size * 3),
    )(parts)


def to_chip(value, bit, n_z):
    return lax.ppermute(value, "z", [(a, a ^ bit) for a in range(n_z)])


def to_core(value):
    return lax.ppermute(value, "core", [(0, 1), (1, 0)])


def complete_z(held, n_z):
    bit = n_z // 2
    while bit:
        for m in range(0, n_z, 2 * bit):
            if m in held and m | bit not in held:
                held[m | bit] = to_chip(held[m], bit, n_z)
        bit //= 2
    return [held[m] for m in range(n_z)]


def reduce_z(evens, odds, n_z, done):
    got = to_chip(odds, 1, n_z)
    held = {2 * k: [(even, None), (got, k)] for k, even in enumerate(evens)}
    bit = 2
    while bit < n_z:
        for m in [m for m in held if m & bit]:
            (term,) = add_all([held.pop(m)], [BF16], done[0])
            held[m ^ bit].append((to_chip(term, bit, n_z), None))
        bit *= 2
    return add_all([held[0]], [BF16], done[1])[0]


def gate_up_rows(core0, mine, theirs, cols):
    tok = mine[0].shape[0] // 2
    gate, up = [], []
    for own, other in zip(mine, theirs):
        x, y = own[:, cols].astype(F32), other[:, cols].astype(F32)
        first, second = jnp.where(core0, x, y), jnp.where(core0, y, x)
        gate += [first[:tok], second[:tok]]
        up += [first[tok:], second[tok:]]
    return jnp.concatenate(gate, 0), jnp.concatenate(up, 0)


def down_kernel(base, n_z, place, *refs):
    mine, theirs, grads = refs[:n_z], refs[n_z : 2 * n_z], refs[2 * n_z]
    out_hbm, token, out, sems = refs[-4:]
    token[...] = jnp.zeros_like(token)
    slots, copies = out.shape[0], []
    for k, (at, size) in enumerate(pieces(mine[0].shape[1], 512)):
        slot = k % slots
        gate, up = gate_up_rows(place[0] == 0, mine, theirs, slice(at, at + size))
        hidden = gate * (1.0 / (1.0 + jnp.exp(-gate))) * up
        if k >= slots:
            copies[k - slots].wait()
        out[slot, :size, :] = jnp.dot(
            hidden.T.astype(BF16), grads[...], preferred_element_type=F32
        ).astype(BF16)
        copy = pltpu.make_async_copy(
            out.at[slot, :size], out_hbm.at[base + at : base + at + size], sems.at[slot]
        )
        copy.start()
        copies.append(copy)
    for copy in copies[-slots:]:
        copy.wait()


def down_grad(place, mine, theirs, grads, base, total, into=None):
    n_z, ff = len(mine), mine[0].shape[1]
    tokens, chans = grads.shape
    slots = min(4, len(pieces(ff, 512)))
    held = [] if into is None else [into]
    return pl.pallas_call(
        functools.partial(down_kernel, base, n_z),
        out_shape=(shape((total, chans), BF16), shape((8, 128), F32)),
        in_specs=[whole(SMEM)] + [whole()] * (2 * n_z + 1) + after(held),
        out_specs=(whole(pltpu.HBM), whole()),
        scratch_shapes=[VMEM((slots, 512, chans), BF16), pltpu.SemaphoreType.DMA((slots,))],
        input_output_aliases={2 * n_z + 2: 0} if held else {},
        compiler_params=params(12),
        cost_estimate=cost(2 * tokens * chans * ff, 2 * chans * ff),
    )(place, *mine, *theirs, grads, *held)


def input_kernel(n_z, place, *refs):
    hidden, rows_a, rows_b = [
        (refs[2 * k * n_z : (2 * k + 1) * n_z], refs[(2 * k + 1) * n_z : (2 * k + 2) * n_z])
        for k in range(3)
    ]
    gate_hbm, up_hbm, gate_grad, up_grad, out, w_gate, w_up, total, held, sems = refs[6 * n_z :]
    core0, z = place[0] == 0, place[1]
    rows, width = hidden[0][0].shape
    ff = gate_grad.shape[1]
    low = ff - width
    slots = w_gate.shape[0]
    parts = [(0, at, size) for at, size in pieces(low, 1024, 256)]
    parts += [(low, at, size) for at, size in pieces(width, 1024)]

    def copies(k):
        base, at, size = parts[k]
        return [
            pltpu.make_async_copy(
                hbm.at[:, base + at : base + at + size],
                vmem.at[k % slots, :, :size],
                sems.at[n, k % slots],
            )
            for n, (hbm, vmem) in enumerate(((gate_hbm, w_gate), (up_hbm, w_up)))
        ]

    def gradients(k):
        base, at, size = parts[k]
        cols, span = slice(base + at, base + at + size), slice(at, at + size)
        first = core0 if base == 0 else ~core0
        grad = jnp.concatenate(
            [
                jnp.where(first, own[:, span], other[:, span]).astype(F32)
                for own, other in zip(*hidden)
            ],
            0,
        )
        gate, up = gate_up_rows(core0, *(rows_a if base == 0 else rows_b), span)
        sig = 1.0 / (1.0 + jnp.exp(-gate))
        gate_grad[:, cols] = (grad * up * sig * (1.0 + gate * (1.0 - sig))).astype(BF16)
        up_grad[:, cols] = (grad * (gate * sig)).astype(BF16)

    for k in range(min(slots, len(parts))):
        for copy in copies(k):
            copy.start()
    gradients(0)
    dims = (((1,), (1,)), ((), ()))
    for k, (base, at, size) in enumerate(parts):
        for copy in copies(k):
            copy.wait()
        cols, slot = slice(base + at, base + at + size), k % slots
        term = lax.dot_general(
            w_gate[slot, :, :size], gate_grad[:, cols], dims, preferred_element_type=F32
        )
        term += lax.dot_general(
            w_up[slot, :, :size], up_grad[:, cols], dims, preferred_element_type=F32
        )
        total[...] = term if k == 0 else total[...] + term
        if k + 1 < len(parts):
            gradients(k + 1)
        if k + slots < len(parts):
            for copy in copies(k + slots):
                copy.start()
    turned = total[...].T
    for m in range(n_z):
        start = pl.multiple_of((z ^ m) * rows, math.gcd(rows, 8))
        held[pl.ds(start, rows), :] = turned[m * rows : (m + 1) * rows]
    n_t = out.shape[0]
    step = held.shape[0] // n_t
    for p in range(n_t):
        out[p] = held[p * step : (p + 1) * step, :].astype(BF16)


def input_grad(place, hidden, rows_a, rows_b, w_gate, w_up, n_t):
    n_z, slots = len(hidden[0]), 3
    tokens = n_z * hidden[0][0].shape[0]
    chans, ff = w_gate.shape
    return pl.pallas_call(
        functools.partial(input_kernel, n_z),
        out_shape=(shape((tokens, ff), BF16),) * 2 + (shape((n_t, tokens // n_t, chans), BF16),),
        in_specs=[whole(SMEM)] + [whole()] * (6 * n_z) + [whole(pltpu.HBM)] * 2,
        out_specs=(whole(),) * 3,
        scratch_shapes=[
            VMEM((slots, chans, min(ff, 1024)), BF16),
            VMEM((slots, chans, min(ff, 1024)), BF16),
            VMEM((chans, tokens), F32),
            VMEM((tokens, chans), F32),
            pltpu.SemaphoreType.DMA((2, slots)),
        ],
        compiler_params=params(42),
        cost_estimate=cost(4 * tokens * chans * ff, 4 * chans * ff + 12 * tokens * ff),
    )(place, *hidden[0], *hidden[1], *rows_a[0], *rows_a[1], *rows_b[0], *rows_b[1], w_gate, w_up)


def weight_kernel(n_z, n_t, place, *refs):
    gate_grad, up_grad, gate_hbm, up_hbm, out, held, inputs_t, sems = refs[n_t:]
    hold(refs[:n_t], place[2], held)
    inputs_t[...] = blocks_of(held, place[1], n_z).T.astype(BF16)
    copies = []
    ff, slots = gate_grad.shape[1], out.shape[0]
    for grad, hbm in ((gate_grad, gate_hbm), (up_grad, up_hbm)):
        for at, size in pieces(ff, 512):
            cols, slot = slice(at, at + size), len(copies) % slots
            if len(copies) >= slots:
                copies[len(copies) - slots].wait()
            out[slot, :, :size] = jnp.dot(
                inputs_t[...], grad[:, cols], preferred_element_type=F32
            ).astype(BF16)
            copy = pltpu.make_async_copy(out.at[slot, :, :size], hbm.at[:, cols], sems.at[slot])
            copy.start()
            copies.append(copy)
    for copy in copies[-slots:]:
        copy.wait()


def weight_grads(place, parts, gate_grad, up_grad, n_z):
    n_t, chans, tokens = len(parts), parts[0].shape[1], gate_grad.shape[0]
    ff = gate_grad.shape[1]
    slots = min(8, 2 * len(pieces(ff, 512)))
    return pl.pallas_call(
        functools.partial(weight_kernel, n_z, n_t),
        out_shape=(shape((chans, ff), BF16),) * 2,
        in_specs=[whole(SMEM)] + [whole()] * (n_t + 2),
        out_specs=(whole(pltpu.HBM),) * 2,
        scratch_shapes=[
            VMEM((slots, chans, 512), BF16),
            VMEM((tokens, chans), F32),
            VMEM((chans, tokens), BF16),
            pltpu.SemaphoreType.DMA((slots,)),
        ],
        compiler_params=params(16),
        cost_estimate=cost(4 * tokens * chans * ff, 4 * chans * ff + 4 * tokens * ff),
    )(place, *parts, gate_grad, up_grad)


def on_device(n_z, n_t, xq, xs, xo, xc, gq, gs, go, gc, gate_pre, up_pre, w_gate, w_up, w_down):
    place = jnp.stack([lax.axis_index(name) for name in ("core", "z", "tensor")]).astype(jnp.int32)
    ff = gate_pre.shape[1]
    width = -(-ff // 256) * 128

    def from_tensor(own):
        return [own] + [
            lax.ppermute(own, "tensor", [(a, a ^ s) for a in range(n_t)]) for s in range(1, n_t)
        ]

    cuts = (ff - width, width)
    grads, inputs, *halves = prep(cuts, xq, xs, xo, xc, gq, gs, go, gc, gate_pre, up_pre)
    bit = n_z // 2
    grads = from_tensor(grads)
    a, b = {0: halves[0]}, {0: halves[1]}
    a |= {bit: to_chip(a[0], bit, n_z), 1: to_chip(a[0], 1, n_z)}
    a_other, b_other = {0: to_core(a[0])}, {0: to_core(b[0])}
    grads, grads_t, *send = first_half(
        place, grads, w_down, n_z, width, a_other[0], b_other[0]
    )
    got = [to_core(part) for part in send]
    b[bit] = to_chip(b[0], bit, n_z)
    mine = second_half(place, grads_t, w_down, n_z, width, a[1], b[bit])
    a[bit | 1] = to_chip(a[bit], 1, n_z)
    b |= {1: to_chip(b[0], 1, n_z), bit | 1: to_chip(b[bit], 1, n_z)}
    *evens, odds = pair_sum(place, mine, got, a[bit | 1], b[1], b[bit | 1])
    rows_a, rows_b = [
        (held, [swapped[m] if m in swapped else to_core(part) for m, part in enumerate(held)])
        for held, swapped in ((complete_z(a, n_z), a_other), (complete_z(b, n_z), b_other))
    ]
    inputs = from_tensor(inputs)
    grad_down, token = down_grad(place, *rows_a, grads, 0, ff)
    hidden = {0: reduce_z(evens, odds, n_z, (inputs[1:] + rows_a[1] + rows_b[1], [token]))}
    hidden |= {bit: to_chip(hidden[0], bit, n_z), 1: to_chip(hidden[0], 1, n_z)}
    grad_down, token = down_grad(place, *rows_b, grads, ff - width, ff, grad_down)
    (hidden[bit],) = add_all([[(hidden[bit], None)]], [BF16], [token, hidden[1]])
    hidden = complete_z(hidden, n_z)
    gate_grad, up_grad, sends = input_grad(
        place, (hidden, [to_core(part) for part in hidden]), rows_a, rows_b, w_gate, w_up, n_t
    )
    terms = lax.all_to_all(sends, "tensor", 0, 0, tiled=True)
    grad_gate, grad_up = weight_grads(place, inputs, gate_grad, up_grad, n_z)
    return sum_parts(terms), grad_gate, grad_up, grad_down


def solution(mesh):
    n_dp, n_t = mesh.shape["dp"], mesh.shape["tensor"]
    fine = Mesh(mesh.devices.reshape(n_dp // 2, 2, n_t), ("z", "core", "tensor"))
    by_token, by_dp = P("tensor", ("z", "core")), P(("z", "core"), "tensor")
    return jax.shard_map(
        functools.partial(on_device, n_dp // 2, n_t),
        mesh=fine,
        in_specs=(by_token,) * 8 + (by_dp,) * 4 + (by_token,),
        out_specs=(by_token, by_dp, by_dp, by_token),
        check_vma=False,
    )
```

```python
import functools
import math

import jax
import jax.numpy as jnp
from jax import lax
from jax.experimental import pallas as pl
from jax.experimental.pallas import tpu as pltpu
from jax.sharding import Mesh
from jax.sharding import PartitionSpec as P

BLK_C = 128
F32 = jnp.float32
BF16 = jnp.bfloat16
VMEM = pltpu.VMEM
SMEM = pltpu.SMEM


def after(arrays):
    return [pl.BlockSpec(memory_space=pl.ANY)] * len(arrays)


def whole(space=VMEM):
    return pl.BlockSpec(memory_space=space)


def shape(dims, dtype):
    return jax.ShapeDtypeStruct(dims, dtype)


def params(mib):
    return pltpu.CompilerParams(vmem_limit_bytes=mib * 1024 * 1024)


def cost(flops, nbytes):
    return pl.CostEstimate(flops=int(flops), bytes_accessed=int(nbytes), transcendentals=0)


def pieces(extent, step, first=0):
    cuts = [0] + list(range(first or step, extent, step)) + [extent]
    return [(a, b - a) for a, b in zip(cuts[:-1], cuts[1:])]


def prep_kernel(xq, xs, xo, xc, gq, gs, go, gc, gate, up, both, rows):
    for k, (quant, scale, flag, corr) in enumerate(((gq, gs, go, gc), (xq, xs, xo, xc))):
        for b in range(scale.shape[1]):
            cols = slice(b * BLK_C, (b + 1) * BLK_C)
            value = scale[0, b] * quant[:, cols].astype(F32) + flag[0, b].astype(F32) * corr[
                :, cols
            ].astype(F32)
            both[k, :, cols] = value.astype(BF16)
    rows[...] = jnp.concatenate([gate[...].astype(F32), up[...].astype(F32)], 0).astype(BF16)


def prep(xq, xs, xo, xc, gq, gs, go, gc, gate, up):
    rows, width = xq.shape
    tok, ff = gate.shape
    return pl.pallas_call(
        prep_kernel,
        out_shape=(shape((2, rows, width), BF16), shape((2 * tok, ff), BF16)),
        in_specs=[whole(), whole(SMEM), whole(SMEM), whole()] * 2 + [whole()] * 2,
        out_specs=(whole(),) * 2,
        compiler_params=params(56),
        cost_estimate=cost(0, 4 * xq.size * 2 + gate.size * 8),
    )(xq, xs, xo, xc, gq, gs, go, gc, gate, up)


def load_down(start, width, w_hbm, w_vmem, sems):
    copies = []
    for k, (at, size) in enumerate(pieces(width, 1024, 256)):
        first = pl.multiple_of(start + at, 16)
        copy = pltpu.make_async_copy(
            w_hbm.at[pl.ds(first, size)], w_vmem.at[pl.ds(at, size)], sems.at[k]
        )
        copy.start()
        copies.append(copy)
    return copies


def hidden_half(copies, grads_t, width, w_vmem, outs):
    rows = outs[0].shape[0]
    for copy, (at, size) in zip(copies, pieces(width, 1024, 256)):
        copy.wait()
        total = jnp.dot(w_vmem[at : at + size, :], grads_t, preferred_element_type=F32).T
        for q, out in enumerate(outs):
            out[:, at : at + size] = total[q * rows : (q + 1) * rows, :].astype(out.dtype)


def blocks_of(held, z, n_z):
    block = held.shape[0] // n_z
    return jnp.concatenate(
        [
            held[pl.ds(pl.multiple_of((z ^ m) * block, math.gcd(block, 8)), block), :]
            for m in range(n_z)
        ],
        0,
    )


def hold(parts, which, me, held):
    rows = parts[0].shape[1]
    for s, part in enumerate(parts):
        start = pl.multiple_of((me ^ s) * rows, math.gcd(rows, 8))
        held[pl.ds(start, rows), :] = part[which].astype(F32)


def first_half_kernel(n_t, n_z, offset, place, *refs):
    parts, w_hbm = refs[:n_t], refs[n_t]
    grads_out, grads_t, *outs = refs[-5 - n_z : -3]
    w_vmem, held, sems = refs[-3:]
    width = outs[0].shape[1]
    copies = load_down((1 - place[0]) * offset, width, w_hbm, w_vmem, sems)
    hold(parts, 0, place[2], held)
    grads_t[...] = held[...].T.astype(BF16)
    grads_out[...] = blocks_of(held, place[1], n_z).astype(BF16)
    hidden_half(copies, grads_t[...], width, w_vmem, outs)


def second_half_kernel(offset, place, grads_t, w_hbm, *refs):
    out, w_vmem, sems = refs[-3:]
    width = out.shape[2]
    outs = [out.at[q] for q in range(out.shape[0])]
    copies = load_down(place[0] * offset, width, w_hbm, w_vmem, sems)
    hidden_half(copies, grads_t[...], width, w_vmem, outs)


def first_half(place, parts, w_down, n_z, width, *done):
    n_t, (_, rows, chans) = len(parts), parts[0].shape
    tokens = n_t * rows
    n_copies = len(pieces(width, 1024, 256))
    return pl.pallas_call(
        functools.partial(first_half_kernel, n_t, n_z, w_down.shape[0] - width),
        out_shape=(
            shape((tokens, chans), BF16),
            shape((chans, tokens), BF16),
        )
        + (shape((tokens // n_z, width), BF16),) * n_z,
        in_specs=[whole(SMEM)] + [whole()] * n_t + [whole(pltpu.HBM)] + after(done),
        out_specs=(whole(),) * (2 + n_z),
        scratch_shapes=[
            VMEM((width, chans), BF16),
            VMEM((tokens, chans), F32),
            pltpu.SemaphoreType.DMA((n_copies,)),
        ],
        compiler_params=params(44),
        cost_estimate=cost(2 * tokens * chans * width, 2 * chans * width),
    )(place, *parts, w_down, *done)


def second_half(place, grads_t, w_down, n_z, width, *done):
    chans, tokens = grads_t.shape
    n_copies = len(pieces(width, 1024, 256))
    return pl.pallas_call(
        functools.partial(second_half_kernel, w_down.shape[0] - width),
        out_shape=shape((n_z, tokens // n_z, width), F32),
        in_specs=[whole(SMEM), whole(), whole(pltpu.HBM)] + after(done),
        out_specs=whole(),
        scratch_shapes=[VMEM((width, chans), BF16), pltpu.SemaphoreType.DMA((n_copies,))],
        compiler_params=params(44),
        cost_estimate=cost(24 * tokens * chans * width, 24 * chans * width),
    )(place, grads_t, w_down, *done)


def pair_kernel(place, mine, *refs):
    n_z = mine.shape[0]
    theirs, outs, total_ref = refs[:n_z], refs[-2 - n_z // 2 : -1], refs[-1]
    for q in range(n_z):
        total_ref[q] = mine[q] + theirs[q][...].astype(F32)
    for m in range(n_z):
        total = total_ref[place[1] ^ m]
        if m % 2:
            outs[-1][m // 2] = total.astype(BF16)
        else:
            outs[m // 2][...] = total


def pair_sum(place, mine, theirs, *done):
    n_z, rows, width = mine.shape
    return pl.pallas_call(
        pair_kernel,
        out_shape=(shape((rows, width), F32),) * (n_z // 2)
        + (shape((n_z // 2, rows, width), BF16),),
        in_specs=[whole(SMEM)] + [whole()] * (1 + n_z) + after(done),
        out_specs=(whole(),) * (n_z // 2 + 1),
        scratch_shapes=[VMEM(mine.shape, F32)],
        compiler_params=params(6),
        cost_estimate=cost(0, mine.size * 9),
    )(place, mine, *theirs, *done)


def add_kernel(picks, n_refs, *refs):
    outs = refs[-len(picks) :]
    for pick, out in zip(picks, outs):
        total = None
        for ref, row in pick:
            term = (refs[ref][...] if row is None else refs[ref][row]).astype(F32)
            total = term if total is None else total + term
        out[...] = total.astype(out.dtype)


def add_all(lists, dtypes, done=()):
    arrays, picks = [], []
    for terms in lists:
        pick = []
        for array, row in terms:
            at = next((k for k, known in enumerate(arrays) if known is array), len(arrays))
            if at == len(arrays):
                arrays.append(array)
            pick.append((at, row))
        picks.append(pick)
    dims = lists[0][0][0].shape[-2:]
    return pl.pallas_call(
        functools.partial(add_kernel, picks, len(arrays)),
        out_shape=tuple(shape(dims, dtype) for dtype in dtypes),
        in_specs=[whole()] * len(arrays) + after(done),
        out_specs=(whole(),) * len(lists),
        compiler_params=params(6),
        cost_estimate=cost(0, dims[0] * dims[1] * 6 * sum(map(len, lists))),
    )(*arrays, *done)


def sum_kernel(parts, out):
    total = parts[0].astype(F32)
    for p in range(1, parts.shape[0]):
        total = total + parts[p].astype(F32)
    out[...] = total.astype(BF16)


def sum_parts(parts):
    return pl.pallas_call(
        sum_kernel,
        out_shape=shape(parts.shape[1:], BF16),
        in_specs=[whole()],
        out_specs=whole(),
        compiler_params=params(3),
        cost_estimate=cost(0, parts.size * 3),
    )(parts)


def to_chip(value, bit, n_z):
    return lax.ppermute(value, "z", [(a, a ^ bit) for a in range(n_z)])


def to_core(value):
    return lax.ppermute(value, "core", [(0, 1), (1, 0)])


def complete_z(held, n_z):
    bit = n_z // 2
    while bit:
        for m in range(0, n_z, 2 * bit):
            if m in held and m | bit not in held:
                held[m | bit] = to_chip(held[m], bit, n_z)
        bit //= 2
    return [held[m] for m in range(n_z)]


def reduce_z(evens, odds, n_z, done):
    got = to_chip(odds, 1, n_z)
    held = {2 * k: [(even, None), (got, k)] for k, even in enumerate(evens)}
    bit = 2
    while bit < n_z:
        for m in [m for m in held if m & bit]:
            (term,) = add_all([held.pop(m)], [BF16], done[0])
            held[m ^ bit].append((to_chip(term, bit, n_z), None))
        bit *= 2
    return add_all([held[0]], [BF16], done[1])[0]


def gate_up_rows(core0, mine, theirs, cols):
    tok = mine[0].shape[0] // 2
    gate, up = [], []
    for own, other in zip(mine, theirs):
        x, y = own[:, cols].astype(F32), other[:, cols].astype(F32)
        first, second = jnp.where(core0, x, y), jnp.where(core0, y, x)
        gate += [first[:tok], second[:tok]]
        up += [first[tok:], second[tok:]]
    return jnp.concatenate(gate, 0), jnp.concatenate(up, 0)


def down_kernel(base, width, n_z, place, *refs):
    mine, theirs, grads = refs[:n_z], refs[n_z : 2 * n_z], refs[2 * n_z]
    out_hbm, token, out, sems = refs[-4:]
    token[...] = jnp.zeros_like(token)
    slots, copies = out.shape[0], []
    for k, (at, size) in enumerate(pieces(width, 512)):
        slot, cols = k % slots, slice(base + at, base + at + size)
        gate, up = gate_up_rows(place[0] == 0, mine, theirs, cols)
        hidden = gate * (1.0 / (1.0 + jnp.exp(-gate))) * up
        if k >= slots:
            copies[k - slots].wait()
        out[slot, :size, :] = jnp.dot(
            hidden.T.astype(BF16), grads[...], preferred_element_type=F32
        ).astype(BF16)
        copy = pltpu.make_async_copy(out.at[slot, :size], out_hbm.at[cols], sems.at[slot])
        copy.start()
        copies.append(copy)
    for copy in copies[-slots:]:
        copy.wait()


def down_grad(place, mine, theirs, grads, base, ff, into=None):
    n_z, total = len(mine), mine[0].shape[1]
    tokens, chans = grads.shape
    slots = min(4, len(pieces(ff, 512)))
    held = [] if into is None else [into]
    return pl.pallas_call(
        functools.partial(down_kernel, base, ff, n_z),
        out_shape=(shape((total, chans), BF16), shape((8, 128), F32)),
        in_specs=[whole(SMEM)] + [whole()] * (2 * n_z + 1) + after(held),
        out_specs=(whole(pltpu.HBM), whole()),
        scratch_shapes=[VMEM((slots, 512, chans), BF16), pltpu.SemaphoreType.DMA((slots,))],
        input_output_aliases={2 * n_z + 2: 0} if held else {},
        compiler_params=params(12),
        cost_estimate=cost(2 * tokens * chans * ff, 2 * chans * ff),
    )(place, *mine, *theirs, grads, *held)


def input_kernel(n_z, place, *refs):
    hidden, gate_up = [
        (refs[2 * k * n_z : (2 * k + 1) * n_z], refs[(2 * k + 1) * n_z : (2 * k + 2) * n_z])
        for k in range(2)
    ]
    gate_hbm, up_hbm, gate_grad, up_grad, out, w_gate, w_up, total, held, sems = refs[4 * n_z :]
    core0, z = place[0] == 0, place[1]
    rows, width = hidden[0][0].shape
    ff = gate_grad.shape[1]
    low = ff - width
    slots = w_gate.shape[0]
    parts = [(0, at, size) for at, size in pieces(low, 1024, 256)]
    parts += [(low, at, size) for at, size in pieces(width, 1024)]

    def copies(k):
        base, at, size = parts[k]
        return [
            pltpu.make_async_copy(
                hbm.at[:, base + at : base + at + size],
                vmem.at[k % slots, :, :size],
                sems.at[n, k % slots],
            )
            for n, (hbm, vmem) in enumerate(((gate_hbm, w_gate), (up_hbm, w_up)))
        ]

    def gradients(k):
        base, at, size = parts[k]
        cols, span = slice(base + at, base + at + size), slice(at, at + size)
        first = core0 if base == 0 else ~core0
        grad = jnp.concatenate(
            [
                jnp.where(first, own[:, span], other[:, span]).astype(F32)
                for own, other in zip(*hidden)
            ],
            0,
        )
        gate, up = gate_up_rows(core0, *gate_up, cols)
        sig = 1.0 / (1.0 + jnp.exp(-gate))
        gate_grad[:, cols] = (grad * up * sig * (1.0 + gate * (1.0 - sig))).astype(BF16)
        up_grad[:, cols] = (grad * (gate * sig)).astype(BF16)

    for k in range(min(slots, len(parts))):
        for copy in copies(k):
            copy.start()
    gradients(0)
    dims = (((1,), (1,)), ((), ()))
    for k, (base, at, size) in enumerate(parts):
        for copy in copies(k):
            copy.wait()
        cols, slot = slice(base + at, base + at + size), k % slots
        term = lax.dot_general(
            w_gate[slot, :, :size], gate_grad[:, cols], dims, preferred_element_type=F32
        )
        term += lax.dot_general(
            w_up[slot, :, :size], up_grad[:, cols], dims, preferred_element_type=F32
        )
        total[...] = term if k == 0 else total[...] + term
        if k + 1 < len(parts):
            gradients(k + 1)
        if k + slots < len(parts):
            for copy in copies(k + slots):
                copy.start()
    turned = total[...].T
    for m in range(n_z):
        start = pl.multiple_of((z ^ m) * rows, math.gcd(rows, 8))
        held[pl.ds(start, rows), :] = turned[m * rows : (m + 1) * rows]
    n_t = out.shape[0]
    step = held.shape[0] // n_t
    for p in range(n_t):
        out[p] = held[p * step : (p + 1) * step, :].astype(BF16)


def input_grad(place, hidden, gate_up, w_gate, w_up, n_t):
    n_z, slots = len(hidden[0]), 3
    tokens = n_z * hidden[0][0].shape[0]
    chans, ff = w_gate.shape
    return pl.pallas_call(
        functools.partial(input_kernel, n_z),
        out_shape=(shape((tokens, ff), BF16),) * 2 + (shape((n_t, tokens // n_t, chans), BF16),),
        in_specs=[whole(SMEM)] + [whole()] * (4 * n_z) + [whole(pltpu.HBM)] * 2,
        out_specs=(whole(),) * 3,
        scratch_shapes=[
            VMEM((slots, chans, min(ff, 1024)), BF16),
            VMEM((slots, chans, min(ff, 1024)), BF16),
            VMEM((chans, tokens), F32),
            VMEM((tokens, chans), F32),
            pltpu.SemaphoreType.DMA((2, slots)),
        ],
        compiler_params=params(42),
        cost_estimate=cost(4 * tokens * chans * ff, 4 * chans * ff + 12 * tokens * ff),
    )(place, *hidden[0], *hidden[1], *gate_up[0], *gate_up[1], w_gate, w_up)


def weight_kernel(n_z, n_t, place, *refs):
    gate_grad, up_grad, gate_hbm, up_hbm, out, held, inputs_t, sems = refs[n_t:]
    hold(refs[:n_t], 1, place[2], held)
    inputs_t[...] = blocks_of(held, place[1], n_z).T.astype(BF16)
    copies = []
    ff, slots = gate_grad.shape[1], out.shape[0]
    for grad, hbm in ((gate_grad, gate_hbm), (up_grad, up_hbm)):
        for at, size in pieces(ff, 512):
            cols, slot = slice(at, at + size), len(copies) % slots
            if len(copies) >= slots:
                copies[len(copies) - slots].wait()
            out[slot, :, :size] = jnp.dot(
                inputs_t[...], grad[:, cols], preferred_element_type=F32
            ).astype(BF16)
            copy = pltpu.make_async_copy(out.at[slot, :, :size], hbm.at[:, cols], sems.at[slot])
            copy.start()
            copies.append(copy)
    for copy in copies[-slots:]:
        copy.wait()


def weight_grads(place, parts, gate_grad, up_grad, n_z):
    n_t, chans, tokens = len(parts), parts[0].shape[2], gate_grad.shape[0]
    ff = gate_grad.shape[1]
    slots = min(8, 2 * len(pieces(ff, 512)))
    return pl.pallas_call(
        functools.partial(weight_kernel, n_z, n_t),
        out_shape=(shape((chans, ff), BF16),) * 2,
        in_specs=[whole(SMEM)] + [whole()] * (n_t + 2),
        out_specs=(whole(pltpu.HBM),) * 2,
        scratch_shapes=[
            VMEM((slots, chans, 512), BF16),
            VMEM((tokens, chans), F32),
            VMEM((chans, tokens), BF16),
            pltpu.SemaphoreType.DMA((slots,)),
        ],
        compiler_params=params(16),
        cost_estimate=cost(4 * tokens * chans * ff, 4 * chans * ff + 4 * tokens * ff),
    )(place, *parts, gate_grad, up_grad)


def on_device(n_z, n_t, xq, xs, xo, xc, gq, gs, go, gc, gate_pre, up_pre, w_gate, w_up, w_down):
    place = jnp.stack([lax.axis_index(name) for name in ("core", "z", "tensor")]).astype(jnp.int32)
    ff = gate_pre.shape[1]
    width = -(-ff // 256) * 128

    def from_tensor(own):
        return [own] + [
            lax.ppermute(own, "tensor", [(a, a ^ s) for a in range(n_t)]) for s in range(1, n_t)
        ]

    both, rows = prep(xq, xs, xo, xc, gq, gs, go, gc, gate_pre, up_pre)
    both = from_tensor(both)
    bit = n_z // 2
    rows = {0: rows, bit: to_chip(rows, bit, n_z), 1: to_chip(rows, 1, n_z)}
    grads, grads_t, *send = first_half(place, both, w_down, n_z, width)
    got = [to_core(part) for part in send]
    mine = second_half(place, grads_t, w_down, n_z, width, rows[1], rows[bit])
    rows[bit | 1] = to_chip(rows[bit], 1, n_z)
    *evens, odds = pair_sum(place, mine, got, rows[bit | 1])
    rows = complete_z(rows, n_z)
    gate_up = (rows, [to_core(part) for part in rows])
    grad_down, token = down_grad(place, *gate_up, grads, 0, ff - width)
    hidden = {0: reduce_z(evens, odds, n_z, (gate_up[1], [token]))}
    hidden |= {bit: to_chip(hidden[0], bit, n_z), 1: to_chip(hidden[0], 1, n_z)}
    grad_down, token = down_grad(place, *gate_up, grads, ff - width, width, grad_down)
    (hidden[bit],) = add_all([[(hidden[bit], None)]], [BF16], [token, hidden[1]])
    hidden = complete_z(hidden, n_z)
    gate_grad, up_grad, sends = input_grad(
        place, (hidden, [to_core(part) for part in hidden]), gate_up, w_gate, w_up, n_t
    )
    terms = lax.all_to_all(sends, "tensor", 0, 0, tiled=True)
    grad_gate, grad_up = weight_grads(place, both, gate_grad, up_grad, n_z)
    return sum_parts(terms), grad_gate, grad_up, grad_down


def solution(mesh):
    n_dp, n_t = mesh.shape["dp"], mesh.shape["tensor"]
    fine = Mesh(mesh.devices.reshape(n_dp // 2, 2, n_t), ("z", "core", "tensor"))
    by_token, by_dp = P("tensor", ("z", "core")), P(("z", "core"), "tensor")
    return jax.shard_map(
        functools.partial(on_device, n_dp // 2, n_t),
        mesh=fine,
        in_specs=(by_token,) * 8 + (by_dp,) * 4 + (by_token,),
        out_specs=(by_token, by_dp, by_dp, by_token),
        check_vma=False,
    )
```

```python
import functools
import math

import jax
import jax.numpy as jnp
from jax import lax
from jax.experimental import pallas as pl
from jax.experimental.pallas import tpu as pltpu
from jax.sharding import Mesh
from jax.sharding import PartitionSpec as P

BLK_C = 128
F32 = jnp.float32
BF16 = jnp.bfloat16
VMEM = pltpu.VMEM
SMEM = pltpu.SMEM


def after(arrays):
    return [pl.BlockSpec(memory_space=pl.ANY)] * len(arrays)


def whole(space=VMEM):
    return pl.BlockSpec(memory_space=space)


def shape(dims, dtype):
    return jax.ShapeDtypeStruct(dims, dtype)


def params(mib):
    return pltpu.CompilerParams(vmem_limit_bytes=mib * 1024 * 1024)


def cost(flops, nbytes):
    return pl.CostEstimate(flops=int(flops), bytes_accessed=int(nbytes), transcendentals=0)


def pieces(extent, step, first=0):
    cuts = [0] + list(range(first or step, extent, step)) + [extent]
    return [(a, b - a) for a, b in zip(cuts[:-1], cuts[1:])]


def prep_kernel(xq, xs, xo, xc, gq, gs, go, gc, gate, up, both, rows):
    for k, (quant, scale, flag, corr) in enumerate(((gq, gs, go, gc), (xq, xs, xo, xc))):
        for b in range(scale.shape[1]):
            cols = slice(b * BLK_C, (b + 1) * BLK_C)
            value = scale[0, b] * quant[:, cols].astype(F32) + flag[0, b].astype(F32) * corr[
                :, cols
            ].astype(F32)
            both[k, :, cols] = value.astype(BF16)
    rows[...] = jnp.concatenate([gate[...].astype(F32), up[...].astype(F32)], 0).astype(BF16)


def prep(xq, xs, xo, xc, gq, gs, go, gc, gate, up):
    rows, width = xq.shape
    tok, ff = gate.shape
    return pl.pallas_call(
        prep_kernel,
        out_shape=(shape((2, rows, width), BF16), shape((2 * tok, ff), BF16)),
        in_specs=[whole(), whole(SMEM), whole(SMEM), whole()] * 2 + [whole()] * 2,
        out_specs=(whole(),) * 2,
        compiler_params=params(56),
        cost_estimate=cost(0, 4 * xq.size * 2 + gate.size * 8),
    )(xq, xs, xo, xc, gq, gs, go, gc, gate, up)


def load_down(start, width, w_hbm, w_vmem, sems):
    copies = []
    for k, (at, size) in enumerate(pieces(width, 1024, 256)):
        first = pl.multiple_of(start + at, 16)
        copy = pltpu.make_async_copy(
            w_hbm.at[pl.ds(first, size)], w_vmem.at[pl.ds(at, size)], sems.at[k]
        )
        copy.start()
        copies.append(copy)
    return copies


def hidden_half(copies, grads_t, width, w_vmem, outs, turned):
    rows, depth = outs[0].shape[0], grads_t.shape[0] // 2

    def put(k, at, size):
        total = turned[k % 2, :size, :].T
        for q, out in enumerate(outs):
            out[:, at : at + size] = total[q * rows : (q + 1) * rows, :].astype(out.dtype)

    spans = pieces(width, 1024, 256)
    for k, (copy, (at, size)) in enumerate(zip(copies, spans)):
        copy.wait()
        total = jnp.dot(
            w_vmem[at : at + size, :depth], grads_t[:depth], preferred_element_type=F32
        )
        total += jnp.dot(
            w_vmem[at : at + size, depth:], grads_t[depth:], preferred_element_type=F32
        )
        turned[k % 2, :size, :] = total
        if k:
            put(k - 1, *spans[k - 1])
    put(len(spans) - 1, *spans[-1])


def blocks_of(held, z, n_z):
    block = held.shape[0] // n_z
    return jnp.concatenate(
        [
            held[pl.ds(pl.multiple_of((z ^ m) * block, math.gcd(block, 8)), block), :]
            for m in range(n_z)
        ],
        0,
    )


def hold(parts, which, me, held):
    rows = parts[0].shape[1]
    for s, part in enumerate(parts):
        start = pl.multiple_of((me ^ s) * rows, math.gcd(rows, 8))
        held[pl.ds(start, rows), :] = part[which].astype(F32)


def first_half_kernel(n_t, n_z, offset, place, *refs):
    parts, w_hbm = refs[:n_t], refs[n_t]
    grads_out, grads_t, *outs = refs[-6 - n_z : -4]
    w_vmem, turned, held, sems = refs[-4:]
    width = outs[0].shape[1]
    copies = load_down((1 - place[0]) * offset, width, w_hbm, w_vmem, sems)
    hold(parts, 0, place[2], held)
    grads_t[...] = held[...].T.astype(BF16)
    grads_out[...] = blocks_of(held, place[1], n_z).astype(BF16)
    hidden_half(copies, grads_t[...], width, w_vmem, outs, turned)


def second_half_kernel(offset, base, place, grads_t, w_hbm, *refs):
    out, w_vmem, turned, sems = refs[-4:]
    width = out.shape[2]
    outs = [out.at[q] for q in range(out.shape[0])]
    copies = load_down(place[0] * offset + base, width, w_hbm, w_vmem, sems)
    hidden_half(copies, grads_t[...], width, w_vmem, outs, turned)


def first_half(place, parts, w_down, n_z, width, *done):
    n_t, (_, rows, chans) = len(parts), parts[0].shape
    tokens = n_t * rows
    n_copies = len(pieces(width, 1024, 256))
    return pl.pallas_call(
        functools.partial(first_half_kernel, n_t, n_z, w_down.shape[0] - width),
        out_shape=(
            shape((tokens, chans), BF16),
            shape((chans, tokens), BF16),
        )
        + (shape((tokens // n_z, width), BF16),) * n_z,
        in_specs=[whole(SMEM)] + [whole()] * n_t + [whole(pltpu.HBM)] + after(done),
        out_specs=(whole(),) * (2 + n_z),
        scratch_shapes=[
            VMEM((width, chans), BF16),
            VMEM((2, min(width, 1024), tokens), F32),
            VMEM((tokens, chans), F32),
            pltpu.SemaphoreType.DMA((n_copies,)),
        ],
        compiler_params=params(44),
        cost_estimate=cost(2 * tokens * chans * width, 2 * chans * width),
    )(place, *parts, w_down, *done)


def second_half(place, grads_t, w_down, n_z, offset, base, width, *done):
    chans, tokens = grads_t.shape
    n_copies = len(pieces(width, 1024, 256))
    return pl.pallas_call(
        functools.partial(second_half_kernel, offset, base),
        out_shape=shape((n_z, tokens // n_z, width), F32),
        in_specs=[whole(SMEM), whole(), whole(pltpu.HBM)] + after(done),
        out_specs=whole(),
        scratch_shapes=[
            VMEM((width, chans), BF16),
            VMEM((2, min(width, 1024), tokens), F32),
            pltpu.SemaphoreType.DMA((n_copies,)),
        ],
        compiler_params=params(44),
        cost_estimate=cost(24 * tokens * chans * width, 24 * chans * width),
    )(place, grads_t, w_down, *done)


def pair_kernel(base, place, mine, *refs):
    n_z, _, width = mine.shape
    theirs, outs, total_ref = refs[:n_z], refs[-2 - n_z // 2 : -1], refs[-1]
    for q in range(n_z):
        total_ref[q] = mine[q] + theirs[q][:, base : base + width].astype(F32)
    for m in range(n_z):
        total = total_ref[place[1] ^ m]
        if m % 2:
            outs[-1][m // 2] = total.astype(BF16)
        else:
            outs[m // 2][...] = total


def pair_sum(place, mine, theirs, base, *done):
    n_z, rows, width = mine.shape
    return pl.pallas_call(
        functools.partial(pair_kernel, base),
        out_shape=(shape((rows, width), F32),) * (n_z // 2)
        + (shape((n_z // 2, rows, width), BF16),),
        in_specs=[whole(SMEM)] + [whole()] * (1 + n_z) + after(done),
        out_specs=(whole(),) * (n_z // 2 + 1),
        scratch_shapes=[VMEM(mine.shape, F32)],
        compiler_params=params(6),
        cost_estimate=cost(0, mine.size * 9),
    )(place, mine, *theirs, *done)


def add_kernel(picks, *refs):
    out = refs[-1]
    for at, size, pick in picks:
        total = None
        for ref, row, col in pick:
            cols = slice(col, col + size)
            term = (refs[ref][:, cols] if row is None else refs[ref][row, :, cols]).astype(F32)
            total = term if total is None else total + term
        out[:, at : at + size] = total.astype(out.dtype)


def add_all(spans, done):
    arrays, picks = [], []
    for at, size, terms in spans:
        pick = []
        for array, row, col in terms:
            k = next((k for k, known in enumerate(arrays) if known is array), len(arrays))
            if k == len(arrays):
                arrays.append(array)
            pick.append((k, row, col))
        picks.append((at, size, pick))
    dims = (spans[0][2][0][0].shape[-2], sum(size for _, size, _ in spans))
    return pl.pallas_call(
        functools.partial(add_kernel, picks),
        out_shape=shape(dims, BF16),
        in_specs=[whole()] * len(arrays) + after(done),
        out_specs=whole(),
        compiler_params=params(6),
        cost_estimate=cost(0, dims[0] * dims[1] * 6 * len(spans[0][2])),
    )(*arrays, *done)


def sum_kernel(parts, out):
    total = parts[0].astype(F32)
    for p in range(1, parts.shape[0]):
        total = total + parts[p].astype(F32)
    out[...] = total.astype(BF16)


def sum_parts(parts):
    return pl.pallas_call(
        sum_kernel,
        out_shape=shape(parts.shape[1:], BF16),
        in_specs=[whole()],
        out_specs=whole(),
        compiler_params=params(3),
        cost_estimate=cost(0, parts.size * 3),
    )(parts)


def to_chip(value, bit, n_z):
    return lax.ppermute(value, "z", [(a, a ^ bit) for a in range(n_z)])


def to_core(value):
    return lax.ppermute(value, "core", [(0, 1), (1, 0)])


def complete_z(held, n_z):
    bit = n_z // 2
    while bit:
        for m in range(0, n_z, 2 * bit):
            if m in held and m | bit not in held:
                held[m | bit] = to_chip(held[m], bit, n_z)
        bit //= 2
    return [held[m] for m in range(n_z)]


def reduce_z(spans, n_z, done):
    held = {m: [] for m in range(0, n_z, 2)}
    for at, size, evens, odds in spans:
        got = to_chip(odds, 1, n_z)
        for k, even in enumerate(evens):
            held[2 * k].append((at, size, [(even, None, 0), (got, k, 0)]))
    bit = 2
    while bit < n_z:
        for m in [m for m in held if m & bit]:
            term = to_chip(add_all(held.pop(m), done[0]), bit, n_z)
            for at, _, terms in held[m ^ bit]:
                terms.append((term, None, at))
        bit *= 2
    return add_all(held[0], done[1])


def gate_up_rows(core0, mine, theirs, cols):
    tok = mine[0].shape[0] // 2
    gate, up = [], []
    for own, other in zip(mine, theirs):
        x, y = own[:, cols].astype(F32), other[:, cols].astype(F32)
        first, second = jnp.where(core0, x, y), jnp.where(core0, y, x)
        gate += [first[:tok], second[:tok]]
        up += [first[tok:], second[tok:]]
    return jnp.concatenate(gate, 0), jnp.concatenate(up, 0)


def down_kernel(base, width, n_z, place, *refs):
    mine, theirs, grads = refs[:n_z], refs[n_z : 2 * n_z], refs[2 * n_z]
    out_hbm, token, out, sems = refs[-4:]
    token[...] = jnp.zeros_like(token)
    slots, copies = out.shape[0], []
    for k, (at, size) in enumerate(pieces(width, 512)):
        slot, cols = k % slots, slice(base + at, base + at + size)
        gate, up = gate_up_rows(place[0] == 0, mine, theirs, cols)
        hidden = gate * (1.0 / (1.0 + jnp.exp(-gate))) * up
        if k >= slots:
            copies[k - slots].wait()
        out[slot, :size, :] = jnp.dot(
            hidden.T.astype(BF16), grads[...], preferred_element_type=F32
        ).astype(BF16)
        copy = pltpu.make_async_copy(out.at[slot, :size], out_hbm.at[cols], sems.at[slot])
        copy.start()
        copies.append(copy)
    for copy in copies[-slots:]:
        copy.wait()


def down_grad(place, mine, theirs, grads, base, ff, into=None):
    n_z, total = len(mine), mine[0].shape[1]
    tokens, chans = grads.shape
    slots = min(4, len(pieces(ff, 512)))
    held = [] if into is None else [into]
    return pl.pallas_call(
        functools.partial(down_kernel, base, ff, n_z),
        out_shape=(shape((total, chans), BF16), shape((8, 128), F32)),
        in_specs=[whole(SMEM)] + [whole()] * (2 * n_z + 1) + after(held),
        out_specs=(whole(pltpu.HBM), whole()),
        scratch_shapes=[VMEM((slots, 512, chans), BF16), pltpu.SemaphoreType.DMA((slots,))],
        input_output_aliases={2 * n_z + 2: 0} if held else {},
        compiler_params=params(12),
        cost_estimate=cost(2 * tokens * chans * ff, 2 * chans * ff),
    )(place, *mine, *theirs, grads, *held)


def input_kernel(n_z, place, *refs):
    hidden, gate_up = [
        (refs[2 * k * n_z : (2 * k + 1) * n_z], refs[(2 * k + 1) * n_z : (2 * k + 2) * n_z])
        for k in range(2)
    ]
    gate_hbm, up_hbm, gate_grad, up_grad, out, w_gate, w_up, total, held, sems = refs[4 * n_z :]
    core0, z = place[0] == 0, place[1]
    rows, width = hidden[0][0].shape
    ff = gate_grad.shape[1]
    low = ff - width
    slots = w_gate.shape[0]
    parts = [(0, at, size) for at, size in pieces(low, 1024, 256)]
    parts += [(low, at, size) for at, size in pieces(width, 1024)]

    def copies(k):
        base, at, size = parts[k]
        return [
            pltpu.make_async_copy(
                hbm.at[:, base + at : base + at + size],
                vmem.at[k % slots, :, :size],
                sems.at[n, k % slots],
            )
            for n, (hbm, vmem) in enumerate(((gate_hbm, w_gate), (up_hbm, w_up)))
        ]

    def gradients(k):
        base, at, size = parts[k]
        cols, span = slice(base + at, base + at + size), slice(at, at + size)
        first = core0 if base == 0 else ~core0
        grad = jnp.concatenate(
            [
                jnp.where(first, own[:, span], other[:, span]).astype(F32)
                for own, other in zip(*hidden)
            ],
            0,
        )
        gate, up = gate_up_rows(core0, *gate_up, cols)
        sig = 1.0 / (1.0 + jnp.exp(-gate))
        gate_grad[:, cols] = (grad * up * sig * (1.0 + gate * (1.0 - sig))).astype(BF16)
        up_grad[:, cols] = (grad * (gate * sig)).astype(BF16)

    for k in range(min(slots, len(parts))):
        for copy in copies(k):
            copy.start()
    gradients(0)
    dims = (((1,), (1,)), ((), ()))
    for k, (base, at, size) in enumerate(parts):
        for copy in copies(k):
            copy.wait()
        cols, slot = slice(base + at, base + at + size), k % slots
        term = lax.dot_general(
            w_gate[slot, :, :size], gate_grad[:, cols], dims, preferred_element_type=F32
        )
        term += lax.dot_general(
            w_up[slot, :, :size], up_grad[:, cols], dims, preferred_element_type=F32
        )
        total[...] = term if k == 0 else total[...] + term
        if k + 1 < len(parts):
            gradients(k + 1)
        if k + slots < len(parts):
            for copy in copies(k + slots):
                copy.start()
    turned = total[...].T
    for m in range(n_z):
        start = pl.multiple_of((z ^ m) * rows, math.gcd(rows, 8))
        held[pl.ds(start, rows), :] = turned[m * rows : (m + 1) * rows]
    n_t = out.shape[0]
    step = held.shape[0] // n_t
    for p in range(n_t):
        out[p] = held[p * step : (p + 1) * step, :].astype(BF16)


def input_grad(place, hidden, gate_up, w_gate, w_up, n_t):
    n_z, slots = len(hidden[0]), 3
    tokens = n_z * hidden[0][0].shape[0]
    chans, ff = w_gate.shape
    return pl.pallas_call(
        functools.partial(input_kernel, n_z),
        out_shape=(shape((tokens, ff), BF16),) * 2 + (shape((n_t, tokens // n_t, chans), BF16),),
        in_specs=[whole(SMEM)] + [whole()] * (4 * n_z) + [whole(pltpu.HBM)] * 2,
        out_specs=(whole(),) * 3,
        scratch_shapes=[
            VMEM((slots, chans, min(ff, 1024)), BF16),
            VMEM((slots, chans, min(ff, 1024)), BF16),
            VMEM((chans, tokens), F32),
            VMEM((tokens, chans), F32),
            pltpu.SemaphoreType.DMA((2, slots)),
        ],
        compiler_params=params(38),
        cost_estimate=cost(4 * tokens * chans * ff, 4 * chans * ff + 12 * tokens * ff),
    )(place, *hidden[0], *hidden[1], *gate_up[0], *gate_up[1], w_gate, w_up)


def weight_kernel(n_z, n_t, place, *refs):
    gate_grad, up_grad, gate_hbm, up_hbm, out, held, inputs_t, sems = refs[n_t:]
    hold(refs[:n_t], 1, place[2], held)
    inputs_t[...] = blocks_of(held, place[1], n_z).T.astype(BF16)
    copies = []
    ff, slots = gate_grad.shape[1], out.shape[0]
    for grad, hbm in ((gate_grad, gate_hbm), (up_grad, up_hbm)):
        for at, size in pieces(ff, 512):
            cols, slot = slice(at, at + size), len(copies) % slots
            if len(copies) >= slots:
                copies[len(copies) - slots].wait()
            out[slot, :, :size] = jnp.dot(
                inputs_t[...], grad[:, cols], preferred_element_type=F32
            ).astype(BF16)
            copy = pltpu.make_async_copy(out.at[slot, :, :size], hbm.at[:, cols], sems.at[slot])
            copy.start()
            copies.append(copy)
    for copy in copies[-slots:]:
        copy.wait()


def weight_grads(place, parts, gate_grad, up_grad, n_z):
    n_t, chans, tokens = len(parts), parts[0].shape[2], gate_grad.shape[0]
    ff = gate_grad.shape[1]
    slots = min(8, 2 * len(pieces(ff, 512)))
    return pl.pallas_call(
        functools.partial(weight_kernel, n_z, n_t),
        out_shape=(shape((chans, ff), BF16),) * 2,
        in_specs=[whole(SMEM)] + [whole()] * (n_t + 2),
        out_specs=(whole(pltpu.HBM),) * 2,
        scratch_shapes=[
            VMEM((slots, chans, 512), BF16),
            VMEM((tokens, chans), F32),
            VMEM((chans, tokens), BF16),
            pltpu.SemaphoreType.DMA((slots,)),
        ],
        compiler_params=params(16),
        cost_estimate=cost(4 * tokens * chans * ff, 4 * chans * ff + 4 * tokens * ff),
    )(place, *parts, gate_grad, up_grad)


def on_device(n_z, n_t, xq, xs, xo, xc, gq, gs, go, gc, gate_pre, up_pre, w_gate, w_up, w_down):
    place = jnp.stack([lax.axis_index(name) for name in ("core", "z", "tensor")]).astype(jnp.int32)
    ff = gate_pre.shape[1]
    width = -(-ff // 256) * 128

    def from_tensor(own):
        return [own] + [
            lax.ppermute(own, "tensor", [(a, a ^ s) for a in range(n_t)]) for s in range(1, n_t)
        ]

    both, rows = prep(xq, xs, xo, xc, gq, gs, go, gc, gate_pre, up_pre)
    both = from_tensor(both)
    bit = n_z // 2
    rows = {0: rows, bit: to_chip(rows, bit, n_z), 1: to_chip(rows, 1, n_z)}
    grads, grads_t, *send = first_half(place, both, w_down, n_z, width)
    got = [to_core(part) for part in send]
    mine = second_half(place, grads_t, w_down, n_z, ff - width, 0, width, rows[1], rows[bit])
    rows[bit | 1] = to_chip(rows[bit], 1, n_z)
    *evens, odds = pair_sum(place, mine, got, 0)
    spans = [(0, width, evens, odds)]
    rows = complete_z(rows, n_z)
    gate_up = (rows, [to_core(part) for part in rows])
    grad_down, token = down_grad(place, *gate_up, grads, 0, ff - width)
    early = [part for m, part in enumerate(gate_up[1]) if m != bit | 1]
    hidden = {0: reduce_z(spans, n_z, (early, [token]))}
    hidden |= {bit: to_chip(hidden[0], bit, n_z), 1: to_chip(hidden[0], 1, n_z)}
    grad_down, token = down_grad(place, *gate_up, grads, ff - width, width, grad_down)
    hidden[bit] = add_all([(0, width, [(hidden[bit], None, 0)])], [token, hidden[1]])
    hidden = complete_z(hidden, n_z)
    gate_grad, up_grad, sends = input_grad(
        place, (hidden, [to_core(part) for part in hidden]), gate_up, w_gate, w_up, n_t
    )
    terms = lax.all_to_all(sends, "tensor", 0, 0, tiled=True)
    grad_gate, grad_up = weight_grads(place, both, gate_grad, up_grad, n_z)
    return sum_parts(terms), grad_gate, grad_up, grad_down


def solution(mesh):
    n_dp, n_t = mesh.shape["dp"], mesh.shape["tensor"]
    fine = Mesh(mesh.devices.reshape(n_dp // 2, 2, n_t), ("z", "core", "tensor"))
    by_token, by_dp = P("tensor", ("z", "core")), P(("z", "core"), "tensor")
    return jax.shard_map(
        functools.partial(on_device, n_dp // 2, n_t),
        mesh=fine,
        in_specs=(by_token,) * 8 + (by_dp,) * 4 + (by_token,),
        out_specs=(by_token, by_dp, by_dp, by_token),
        check_vma=False,
    )
```

```python
import functools
import math

import jax
import jax.numpy as jnp
from jax import lax
from jax.experimental import pallas as pl
from jax.experimental.pallas import tpu as pltpu
from jax.sharding import Mesh
from jax.sharding import PartitionSpec as P

BLK_C = 128
F32 = jnp.float32
BF16 = jnp.bfloat16
VMEM = pltpu.VMEM
SMEM = pltpu.SMEM


def after(arrays):
    return [pl.BlockSpec(memory_space=pl.ANY)] * len(arrays)


def whole(space=VMEM):
    return pl.BlockSpec(memory_space=space)


def shape(dims, dtype):
    return jax.ShapeDtypeStruct(dims, dtype)


def params(mib):
    return pltpu.CompilerParams(vmem_limit_bytes=mib * 1024 * 1024)


def cost(flops, nbytes):
    return pl.CostEstimate(flops=int(flops), bytes_accessed=int(nbytes), transcendentals=0)


def pieces(extent, step, first=0):
    cuts = [0] + list(range(first or step, extent, step)) + [extent]
    return [(a, b - a) for a, b in zip(cuts[:-1], cuts[1:])]


def prep_kernel(xq, xs, xo, xc, gq, gs, go, gc, gate, up, both, rows):
    for k, (quant, scale, flag, corr) in enumerate(((gq, gs, go, gc), (xq, xs, xo, xc))):
        for b in range(scale.shape[1]):
            cols = slice(b * BLK_C, (b + 1) * BLK_C)
            value = scale[0, b] * quant[:, cols].astype(F32) + flag[0, b].astype(F32) * corr[
                :, cols
            ].astype(F32)
            both[k, :, cols] = value.astype(BF16)
    rows[...] = jnp.concatenate([gate[...].astype(F32), up[...].astype(F32)], 0).astype(BF16)


def prep(xq, xs, xo, xc, gq, gs, go, gc, gate, up):
    rows, width = xq.shape
    tok, ff = gate.shape
    return pl.pallas_call(
        prep_kernel,
        out_shape=(shape((2, rows, width), BF16), shape((2 * tok, ff), BF16)),
        in_specs=[whole(), whole(SMEM), whole(SMEM), whole()] * 2 + [whole()] * 2,
        out_specs=(whole(),) * 2,
        compiler_params=params(56),
        cost_estimate=cost(0, 4 * xq.size * 2 + gate.size * 8),
    )(xq, xs, xo, xc, gq, gs, go, gc, gate, up)


def load_down(start, width, w_hbm, w_vmem, sems):
    copies = []
    for k, (at, size) in enumerate(pieces(width, 1024, 256)):
        first = pl.multiple_of(start + at, 16)
        copy = pltpu.make_async_copy(
            w_hbm.at[pl.ds(first, size)], w_vmem.at[pl.ds(at, size)], sems.at[k]
        )
        copy.start()
        copies.append(copy)
    return copies


def hidden_half(copies, grads_t, width, w_vmem, outs, turned):
    rows, depth = outs[0].shape[0], grads_t.shape[0] // 2

    def put(k, at, size):
        total = turned[k % 2, :size, :].T
        for q, out in enumerate(outs):
            out[:, at : at + size] = total[q * rows : (q + 1) * rows, :].astype(out.dtype)

    spans = pieces(width, 1024, 256)
    for k, (copy, (at, size)) in enumerate(zip(copies, spans)):
        copy.wait()
        total = jnp.dot(
            w_vmem[at : at + size, :depth], grads_t[:depth], preferred_element_type=F32
        )
        total += jnp.dot(
            w_vmem[at : at + size, depth:], grads_t[depth:], preferred_element_type=F32
        )
        turned[k % 2, :size, :] = total
        if k:
            put(k - 1, *spans[k - 1])
    put(len(spans) - 1, *spans[-1])


def blocks_of(held, z, n_z):
    block = held.shape[0] // n_z
    return jnp.concatenate(
        [
            held[pl.ds(pl.multiple_of((z ^ m) * block, math.gcd(block, 8)), block), :]
            for m in range(n_z)
        ],
        0,
    )


def hold(parts, which, me, held):
    rows = parts[0].shape[1]
    for s, part in enumerate(parts):
        start = pl.multiple_of((me ^ s) * rows, math.gcd(rows, 8))
        held[pl.ds(start, rows), :] = part[which].astype(F32)


def first_half_kernel(n_t, n_z, offset, place, *refs):
    parts, w_hbm = refs[:n_t], refs[n_t]
    grads_out, grads_t, *outs = refs[-6 - n_z : -4]
    w_vmem, turned, held, sems = refs[-4:]
    width = outs[0].shape[1]
    copies = load_down((1 - place[0]) * offset, width, w_hbm, w_vmem, sems)
    hold(parts, 0, place[2], held)
    grads_t[...] = held[...].T.astype(BF16)
    grads_out[...] = blocks_of(held, place[1], n_z).astype(BF16)
    hidden_half(copies, grads_t[...], width, w_vmem, outs, turned)


def second_half_kernel(offset, base, place, grads_t, w_hbm, *refs):
    out, w_vmem, turned, sems = refs[-4:]
    width = out.shape[2]
    outs = [out.at[q] for q in range(out.shape[0])]
    copies = load_down(place[0] * offset + base, width, w_hbm, w_vmem, sems)
    hidden_half(copies, grads_t[...], width, w_vmem, outs, turned)


def first_half(place, parts, w_down, n_z, width, *done):
    n_t, (_, rows, chans) = len(parts), parts[0].shape
    tokens = n_t * rows
    n_copies = len(pieces(width, 1024, 256))
    return pl.pallas_call(
        functools.partial(first_half_kernel, n_t, n_z, w_down.shape[0] - width),
        out_shape=(
            shape((tokens, chans), BF16),
            shape((chans, tokens), BF16),
        )
        + (shape((tokens // n_z, width), BF16),) * n_z,
        in_specs=[whole(SMEM)] + [whole()] * n_t + [whole(pltpu.HBM)] + after(done),
        out_specs=(whole(),) * (2 + n_z),
        scratch_shapes=[
            VMEM((width, chans), BF16),
            VMEM((2, min(width, 1024), tokens), F32),
            VMEM((tokens, chans), F32),
            pltpu.SemaphoreType.DMA((n_copies,)),
        ],
        compiler_params=params(44),
        cost_estimate=cost(2 * tokens * chans * width, 2 * chans * width),
    )(place, *parts, w_down, *done)


def second_half(place, grads_t, w_down, n_z, offset, base, width, *done):
    chans, tokens = grads_t.shape
    n_copies = len(pieces(width, 1024, 256))
    return pl.pallas_call(
        functools.partial(second_half_kernel, offset, base),
        out_shape=shape((n_z, tokens // n_z, width), F32),
        in_specs=[whole(SMEM), whole(), whole(pltpu.HBM)] + after(done),
        out_specs=whole(),
        scratch_shapes=[
            VMEM((width, chans), BF16),
            VMEM((2, min(width, 1024), tokens), F32),
            pltpu.SemaphoreType.DMA((n_copies,)),
        ],
        compiler_params=params(44),
        cost_estimate=cost(24 * tokens * chans * width, 24 * chans * width),
    )(place, grads_t, w_down, *done)


def pair_kernel(base, place, mine, *refs):
    n_z, _, width = mine.shape
    theirs, outs, total_ref = refs[:n_z], refs[-2 - n_z // 2 : -1], refs[-1]
    for q in range(n_z):
        total_ref[q] = mine[q] + theirs[q][:, base : base + width].astype(F32)
    for m in range(n_z):
        total = total_ref[place[1] ^ m]
        if m % 2:
            outs[-1][m // 2] = total.astype(BF16)
        else:
            outs[m // 2][...] = total


def pair_sum(place, mine, theirs, base, *done):
    n_z, rows, width = mine.shape
    return pl.pallas_call(
        functools.partial(pair_kernel, base),
        out_shape=(shape((rows, width), F32),) * (n_z // 2)
        + (shape((n_z // 2, rows, width), BF16),),
        in_specs=[whole(SMEM)] + [whole()] * (1 + n_z) + after(done),
        out_specs=(whole(),) * (n_z // 2 + 1),
        scratch_shapes=[VMEM(mine.shape, F32)],
        compiler_params=params(6),
        cost_estimate=cost(0, mine.size * 9),
    )(place, mine, *theirs, *done)


def add_kernel(picks, *refs):
    out = refs[-1]
    for at, size, pick in picks:
        total = None
        for ref, row, col in pick:
            cols = slice(col, col + size)
            term = (refs[ref][:, cols] if row is None else refs[ref][row, :, cols]).astype(F32)
            total = term if total is None else total + term
        out[:, at : at + size] = total.astype(out.dtype)


def add_all(spans, done):
    arrays, picks = [], []
    for at, size, terms in spans:
        pick = []
        for array, row, col in terms:
            k = next((k for k, known in enumerate(arrays) if known is array), len(arrays))
            if k == len(arrays):
                arrays.append(array)
            pick.append((k, row, col))
        picks.append((at, size, pick))
    dims = (spans[0][2][0][0].shape[-2], sum(size for _, size, _ in spans))
    return pl.pallas_call(
        functools.partial(add_kernel, picks),
        out_shape=shape(dims, BF16),
        in_specs=[whole()] * len(arrays) + after(done),
        out_specs=whole(),
        compiler_params=params(6),
        cost_estimate=cost(0, dims[0] * dims[1] * 6 * len(spans[0][2])),
    )(*arrays, *done)


def to_chip(value, bit, n_z):
    return lax.ppermute(value, "z", [(a, a ^ bit) for a in range(n_z)])


def to_core(value):
    return lax.ppermute(value, "core", [(0, 1), (1, 0)])


def complete_z(held, n_z):
    bit = n_z // 2
    while bit:
        for m in range(0, n_z, 2 * bit):
            if m in held and m | bit not in held:
                held[m | bit] = to_chip(held[m], bit, n_z)
        bit //= 2
    return [held[m] for m in range(n_z)]


def reduce_z(spans, n_z, done):
    held = {m: [] for m in range(0, n_z, 2)}
    for at, size, evens, odds in spans:
        got = to_chip(odds, 1, n_z)
        for k, even in enumerate(evens):
            held[2 * k].append((at, size, [(even, None, 0), (got, k, 0)]))
    bit = 2
    while bit < n_z:
        for m in [m for m in held if m & bit]:
            term = to_chip(add_all(held.pop(m), done[0]), bit, n_z)
            for at, _, terms in held[m ^ bit]:
                terms.append((term, None, at))
        bit *= 2
    return add_all(held[0], done[1])


def gate_up_rows(core0, mine, theirs, cols):
    tok = mine[0].shape[0] // 2
    gate, up = [], []
    for own, other in zip(mine, theirs):
        x, y = own[:, cols].astype(F32), other[:, cols].astype(F32)
        first, second = jnp.where(core0, x, y), jnp.where(core0, y, x)
        gate += [first[:tok], second[:tok]]
        up += [first[tok:], second[tok:]]
    return jnp.concatenate(gate, 0), jnp.concatenate(up, 0)


def down_kernel(base, width, n_z, place, *refs):
    mine, theirs, grads = refs[:n_z], refs[n_z : 2 * n_z], refs[2 * n_z]
    out_hbm, token, out, sems = refs[-4:]
    token[...] = jnp.zeros_like(token)
    slots, copies = out.shape[0], []
    for k, (at, size) in enumerate(pieces(width, 512)):
        slot, cols = k % slots, slice(base + at, base + at + size)
        gate, up = gate_up_rows(place[0] == 0, mine, theirs, cols)
        hidden = gate * (1.0 / (1.0 + jnp.exp(-gate))) * up
        if k >= slots:
            copies[k - slots].wait()
        out[slot, :size, :] = jnp.dot(
            hidden.T.astype(BF16), grads[...], preferred_element_type=F32
        ).astype(BF16)
        copy = pltpu.make_async_copy(out.at[slot, :size], out_hbm.at[cols], sems.at[slot])
        copy.start()
        copies.append(copy)
    for copy in copies[-slots:]:
        copy.wait()


def down_grad(place, mine, theirs, grads, base, ff, into=None):
    n_z, total = len(mine), mine[0].shape[1]
    tokens, chans = grads.shape
    slots = min(4, len(pieces(ff, 512)))
    held = [] if into is None else [into]
    return pl.pallas_call(
        functools.partial(down_kernel, base, ff, n_z),
        out_shape=(shape((total, chans), BF16), shape((8, 128), F32)),
        in_specs=[whole(SMEM)] + [whole()] * (2 * n_z + 1) + after(held),
        out_specs=(whole(pltpu.HBM), whole()),
        scratch_shapes=[VMEM((slots, 512, chans), BF16), pltpu.SemaphoreType.DMA((slots,))],
        input_output_aliases={2 * n_z + 2: 0} if held else {},
        compiler_params=params(12),
        cost_estimate=cost(2 * tokens * chans * ff, 2 * chans * ff),
    )(place, *mine, *theirs, grads, *held)


def input_kernel(n_z, place, *refs):
    hidden, gate_up = [
        (refs[2 * k * n_z : (2 * k + 1) * n_z], refs[(2 * k + 1) * n_z : (2 * k + 2) * n_z])
        for k in range(2)
    ]
    gate_hbm, up_hbm, gate_grad, up_grad, *outs = refs[4 * n_z : -5]
    w_gate, w_up, total, held, sems = refs[-5:]
    core0, z = place[0] == 0, place[1]
    rows, width = hidden[0][0].shape
    ff = gate_grad.shape[1]
    low = ff - width
    slots = w_gate.shape[0]
    parts = [(0, at, size) for at, size in pieces(low, 1024, 256)]
    parts += [(low, at, size) for at, size in pieces(width, 1024)]

    def copies(k):
        base, at, size = parts[k]
        return [
            pltpu.make_async_copy(
                hbm.at[:, base + at : base + at + size],
                vmem.at[k % slots, :, :size],
                sems.at[n, k % slots],
            )
            for n, (hbm, vmem) in enumerate(((gate_hbm, w_gate), (up_hbm, w_up)))
        ]

    def gradients(k):
        base, at, size = parts[k]
        cols, span = slice(base + at, base + at + size), slice(at, at + size)
        first = core0 if base == 0 else ~core0
        grad = jnp.concatenate(
            [
                jnp.where(first, own[:, span], other[:, span]).astype(F32)
                for own, other in zip(*hidden)
            ],
            0,
        )
        gate, up = gate_up_rows(core0, *gate_up, cols)
        sig = 1.0 / (1.0 + jnp.exp(-gate))
        gate_grad[:, cols] = (grad * up * sig * (1.0 + gate * (1.0 - sig))).astype(BF16)
        up_grad[:, cols] = (grad * (gate * sig)).astype(BF16)

    for k in range(min(slots, len(parts))):
        for copy in copies(k):
            copy.start()
    gradients(0)
    dims = (((1,), (1,)), ((), ()))
    for k, (base, at, size) in enumerate(parts):
        for copy in copies(k):
            copy.wait()
        cols, slot = slice(base + at, base + at + size), k % slots
        term = lax.dot_general(
            w_gate[slot, :, :size], gate_grad[:, cols], dims, preferred_element_type=F32
        )
        term += lax.dot_general(
            w_up[slot, :, :size], up_grad[:, cols], dims, preferred_element_type=F32
        )
        total[...] = term if k == 0 else total[...] + term
        if k + 1 < len(parts):
            gradients(k + 1)
        if k + slots < len(parts):
            for copy in copies(k + slots):
                copy.start()
    turned = total[...].T
    for m in range(n_z):
        start = pl.multiple_of((z ^ m) * rows, math.gcd(rows, 8))
        held[pl.ds(start, rows), :] = turned[m * rows : (m + 1) * rows]
    for s, out in enumerate(outs):
        step = out.shape[0]
        start = pl.multiple_of((place[2] ^ s) * step, math.gcd(step, 8))
        out[...] = held[pl.ds(start, step), :].astype(out.dtype)


def input_grad(place, hidden, gate_up, w_gate, w_up, n_t):
    n_z, slots = len(hidden[0]), 3
    tokens = n_z * hidden[0][0].shape[0]
    chans, ff = w_gate.shape
    return pl.pallas_call(
        functools.partial(input_kernel, n_z),
        out_shape=(shape((tokens, ff), BF16),) * 2
        + (shape((tokens // n_t, chans), F32),)
        + (shape((tokens // n_t, chans), BF16),) * (n_t - 1),
        in_specs=[whole(SMEM)] + [whole()] * (4 * n_z) + [whole(pltpu.HBM)] * 2,
        out_specs=(whole(),) * (2 + n_t),
        scratch_shapes=[
            VMEM((slots, chans, min(ff, 1024)), BF16),
            VMEM((slots, chans, min(ff, 1024)), BF16),
            VMEM((chans, tokens), F32),
            VMEM((tokens, chans), F32),
            pltpu.SemaphoreType.DMA((2, slots)),
        ],
        compiler_params=params(38),
        cost_estimate=cost(4 * tokens * chans * ff, 4 * chans * ff + 12 * tokens * ff),
    )(place, *hidden[0], *hidden[1], *gate_up[0], *gate_up[1], w_gate, w_up)


def weight_kernel(n_z, n_t, place, *refs):
    gate_grad, up_grad, gate_hbm, up_hbm, out, held, inputs_t, sems = refs[n_t:]
    hold(refs[:n_t], 1, place[2], held)
    inputs_t[...] = blocks_of(held, place[1], n_z).T.astype(BF16)
    copies = []
    ff, slots = gate_grad.shape[1], out.shape[0]
    for grad, hbm in ((gate_grad, gate_hbm), (up_grad, up_hbm)):
        for at, size in pieces(ff, 512):
            cols, slot = slice(at, at + size), len(copies) % slots
            if len(copies) >= slots:
                copies[len(copies) - slots].wait()
            out[slot, :, :size] = jnp.dot(
                inputs_t[...], grad[:, cols], preferred_element_type=F32
            ).astype(BF16)
            copy = pltpu.make_async_copy(out.at[slot, :, :size], hbm.at[:, cols], sems.at[slot])
            copy.start()
            copies.append(copy)
    for copy in copies[-slots:]:
        copy.wait()


def weight_grads(place, parts, gate_grad, up_grad, n_z):
    n_t, chans, tokens = len(parts), parts[0].shape[2], gate_grad.shape[0]
    ff = gate_grad.shape[1]
    slots = min(8, 2 * len(pieces(ff, 512)))
    return pl.pallas_call(
        functools.partial(weight_kernel, n_z, n_t),
        out_shape=(shape((chans, ff), BF16),) * 2,
        in_specs=[whole(SMEM)] + [whole()] * (n_t + 2),
        out_specs=(whole(pltpu.HBM),) * 2,
        scratch_shapes=[
            VMEM((slots, chans, 512), BF16),
            VMEM((tokens, chans), F32),
            VMEM((chans, tokens), BF16),
            pltpu.SemaphoreType.DMA((slots,)),
        ],
        compiler_params=params(16),
        cost_estimate=cost(4 * tokens * chans * ff, 4 * chans * ff + 4 * tokens * ff),
    )(place, *parts, gate_grad, up_grad)


def on_device(n_z, n_t, xq, xs, xo, xc, gq, gs, go, gc, gate_pre, up_pre, w_gate, w_up, w_down):
    place = jnp.stack([lax.axis_index(name) for name in ("core", "z", "tensor")]).astype(jnp.int32)
    ff = gate_pre.shape[1]
    width = -(-ff // 256) * 128

    def to_tensor(value, s):
        return lax.ppermute(value, "tensor", [(p, p ^ s) for p in range(n_t)])

    both, rows = prep(xq, xs, xo, xc, gq, gs, go, gc, gate_pre, up_pre)
    both = [both] + [to_tensor(both, s) for s in range(1, n_t)]
    bit = n_z // 2
    rows = {0: rows, bit: to_chip(rows, bit, n_z), 1: to_chip(rows, 1, n_z)}
    grads, grads_t, *send = first_half(place, both, w_down, n_z, width)
    got = [to_core(part) for part in send]
    mine = second_half(place, grads_t, w_down, n_z, ff - width, 0, width, rows[1], rows[bit])
    rows[bit | 1] = to_chip(rows[bit], 1, n_z)
    *evens, odds = pair_sum(place, mine, got, 0)
    spans = [(0, width, evens, odds)]
    rows = complete_z(rows, n_z)
    gate_up = (rows, [to_core(part) for part in rows])
    grad_down, token = down_grad(place, *gate_up, grads, 0, ff - width)
    early = [part for m, part in enumerate(gate_up[1]) if m != bit | 1]
    hidden = {0: reduce_z(spans, n_z, (early, [token]))}
    hidden |= {bit: to_chip(hidden[0], bit, n_z), 1: to_chip(hidden[0], 1, n_z)}
    grad_down, token = down_grad(place, *gate_up, grads, ff - width, width, grad_down)
    hidden[bit] = add_all([(0, width, [(hidden[bit], None, 0)])], [token, hidden[1]])
    hidden = complete_z(hidden, n_z)
    gate_grad, up_grad, kept, *sends = input_grad(
        place, (hidden, [to_core(part) for part in hidden]), gate_up, w_gate, w_up, n_t
    )
    terms = [kept] + [to_tensor(part, s) for s, part in enumerate(sends, 1)]
    grad_gate, grad_up = weight_grads(place, both, gate_grad, up_grad, n_z)
    grad_input = add_all([(0, kept.shape[1], [(term, None, 0) for term in terms])], [])
    return grad_input, grad_gate, grad_up, grad_down


def solution(mesh):
    n_dp, n_t = mesh.shape["dp"], mesh.shape["tensor"]
    fine = Mesh(mesh.devices.reshape(n_dp // 2, 2, n_t), ("z", "core", "tensor"))
    by_token, by_dp = P("tensor", ("z", "core")), P(("z", "core"), "tensor")
    return jax.shard_map(
        functools.partial(on_device, n_dp // 2, n_t),
        mesh=fine,
        in_specs=(by_token,) * 8 + (by_dp,) * 4 + (by_token,),
        out_specs=(by_token, by_dp, by_dp, by_token),
        check_vma=False,
    )
```

```python
import functools
import math

import jax
import jax.numpy as jnp
from jax import lax
from jax.experimental import pallas as pl
from jax.experimental.pallas import tpu as pltpu
from jax.sharding import Mesh
from jax.sharding import PartitionSpec as P

BLK_C = 128
F32 = jnp.float32
BF16 = jnp.bfloat16
VMEM = pltpu.VMEM
SMEM = pltpu.SMEM


def after(arrays):
    return [pl.BlockSpec(memory_space=pl.ANY)] * len(arrays)


def whole(space=VMEM):
    return pl.BlockSpec(memory_space=space)


def shape(dims, dtype):
    return jax.ShapeDtypeStruct(dims, dtype)


def params(mib):
    return pltpu.CompilerParams(vmem_limit_bytes=mib * 1024 * 1024)


def cost(flops, nbytes):
    return pl.CostEstimate(flops=int(flops), bytes_accessed=int(nbytes), transcendentals=0)


def pieces(extent, step, first=0):
    cuts = [0] + list(range(first or step, extent, step)) + [extent]
    return [(a, b - a) for a, b in zip(cuts[:-1], cuts[1:])]


def prep_kernel(xq, xs, xo, xc, gq, gs, go, gc, gate, up, both, rows):
    for k, (quant, scale, flag, corr) in enumerate(((gq, gs, go, gc), (xq, xs, xo, xc))):
        for b in range(scale.shape[1]):
            cols = slice(b * BLK_C, (b + 1) * BLK_C)
            value = scale[0, b] * quant[:, cols].astype(F32) + flag[0, b].astype(F32) * corr[
                :, cols
            ].astype(F32)
            both[k, :, cols] = value.astype(BF16)
    rows[...] = jnp.concatenate([gate[...].astype(F32), up[...].astype(F32)], 0).astype(BF16)


def prep(xq, xs, xo, xc, gq, gs, go, gc, gate, up):
    rows, width = xq.shape
    tok, ff = gate.shape
    return pl.pallas_call(
        prep_kernel,
        out_shape=(shape((2, rows, width), BF16), shape((2 * tok, ff), BF16)),
        in_specs=[whole(), whole(SMEM), whole(SMEM), whole()] * 2 + [whole()] * 2,
        out_specs=(whole(),) * 2,
        compiler_params=params(56),
        cost_estimate=cost(0, 4 * xq.size * 2 + gate.size * 8),
    )(xq, xs, xo, xc, gq, gs, go, gc, gate, up)


def load_down(start, width, w_hbm, w_vmem, sems):
    copies = []
    for k, (at, size) in enumerate(pieces(width, 1024, 256)):
        first = pl.multiple_of(start + at, 16)
        copy = pltpu.make_async_copy(
            w_hbm.at[pl.ds(first, size)], w_vmem.at[pl.ds(at, size)], sems.at[k]
        )
        copy.start()
        copies.append(copy)
    return copies


def hidden_half(copies, grads_t, width, w_vmem, outs, turned):
    rows, depth = outs[0].shape[0], grads_t.shape[0] // 2

    def put(k, at, size):
        total = turned[k % 2, :size, :].T
        for q, out in enumerate(outs):
            out[:, at : at + size] = total[q * rows : (q + 1) * rows, :].astype(out.dtype)

    spans = pieces(width, 1024, 256)
    for k, (copy, (at, size)) in enumerate(zip(copies, spans)):
        copy.wait()
        total = jnp.dot(
            w_vmem[at : at + size, :depth], grads_t[:depth], preferred_element_type=F32
        )
        total += jnp.dot(
            w_vmem[at : at + size, depth:], grads_t[depth:], preferred_element_type=F32
        )
        turned[k % 2, :size, :] = total
        if k:
            put(k - 1, *spans[k - 1])
    put(len(spans) - 1, *spans[-1])


def blocks_of(held, z, n_z):
    block = held.shape[0] // n_z
    return jnp.concatenate(
        [
            held[pl.ds(pl.multiple_of((z ^ m) * block, math.gcd(block, 8)), block), :]
            for m in range(n_z)
        ],
        0,
    )


def hold(parts, which, me, held):
    rows = parts[0].shape[1]
    for s, part in enumerate(parts):
        start = pl.multiple_of((me ^ s) * rows, math.gcd(rows, 8))
        held[pl.ds(start, rows), :] = part[which].astype(F32)


def first_half_kernel(n_t, n_z, offset, place, *refs):
    parts, w_hbm = refs[:n_t], refs[n_t]
    grads_out, grads_t, *outs = refs[-6 - n_z : -4]
    w_vmem, turned, held, sems = refs[-4:]
    width = outs[0].shape[1]
    copies = load_down((1 - place[0]) * offset, width, w_hbm, w_vmem, sems)
    hold(parts, 0, place[2], held)
    grads_t[...] = held[...].T.astype(BF16)
    grads_out[...] = blocks_of(held, place[1], n_z).astype(BF16)
    hidden_half(copies, grads_t[...], width, w_vmem, outs, turned)


def second_half_kernel(offset, base, place, grads_t, w_hbm, *refs):
    out, w_vmem, turned, sems = refs[-4:]
    width = out.shape[2]
    outs = [out.at[q] for q in range(out.shape[0])]
    copies = load_down(place[0] * offset + base, width, w_hbm, w_vmem, sems)
    hidden_half(copies, grads_t[...], width, w_vmem, outs, turned)


def first_half(place, parts, w_down, n_z, width, *done):
    n_t, (_, rows, chans) = len(parts), parts[0].shape
    tokens = n_t * rows
    n_copies = len(pieces(width, 1024, 256))
    return pl.pallas_call(
        functools.partial(first_half_kernel, n_t, n_z, w_down.shape[0] - width),
        out_shape=(
            shape((tokens, chans), BF16),
            shape((chans, tokens), BF16),
        )
        + (shape((tokens // n_z, width), BF16),) * n_z,
        in_specs=[whole(SMEM)] + [whole()] * n_t + [whole(pltpu.HBM)] + after(done),
        out_specs=(whole(),) * (2 + n_z),
        scratch_shapes=[
            VMEM((width, chans), BF16),
            VMEM((2, min(width, 1024), tokens), F32),
            VMEM((tokens, chans), F32),
            pltpu.SemaphoreType.DMA((n_copies,)),
        ],
        compiler_params=params(44),
        cost_estimate=cost(12 * tokens * chans * width, 12 * chans * width),
    )(place, *parts, w_down, *done)


def second_half(place, grads_t, w_down, n_z, offset, base, width, *done):
    chans, tokens = grads_t.shape
    n_copies = len(pieces(width, 1024, 256))
    return pl.pallas_call(
        functools.partial(second_half_kernel, offset, base),
        out_shape=shape((n_z, tokens // n_z, width), F32),
        in_specs=[whole(SMEM), whole(), whole(pltpu.HBM)] + after(done),
        out_specs=whole(),
        scratch_shapes=[
            VMEM((width, chans), BF16),
            VMEM((2, min(width, 1024), tokens), F32),
            pltpu.SemaphoreType.DMA((n_copies,)),
        ],
        compiler_params=params(44),
        cost_estimate=cost(24 * tokens * chans * width, 24 * chans * width),
    )(place, grads_t, w_down, *done)


def pair_kernel(base, place, mine, *refs):
    n_z, _, width = mine.shape
    theirs, outs, total_ref = refs[:n_z], refs[-2 - n_z // 2 : -1], refs[-1]
    for q in range(n_z):
        total_ref[q] = mine[q] + theirs[q][:, base : base + width].astype(F32)
    for m in range(n_z):
        total = total_ref[place[1] ^ m]
        if m % 2:
            outs[-1][m // 2] = total.astype(BF16)
        else:
            outs[m // 2][...] = total


def pair_sum(place, mine, theirs, base, *done):
    n_z, rows, width = mine.shape
    return pl.pallas_call(
        functools.partial(pair_kernel, base),
        out_shape=(shape((rows, width), F32),) * (n_z // 2)
        + (shape((n_z // 2, rows, width), BF16),),
        in_specs=[whole(SMEM)] + [whole()] * (1 + n_z) + after(done),
        out_specs=(whole(),) * (n_z // 2 + 1),
        scratch_shapes=[VMEM(mine.shape, F32)],
        compiler_params=params(6),
        cost_estimate=cost(0, mine.size * 9),
    )(place, mine, *theirs, *done)


def add_kernel(picks, *refs):
    out = refs[-1]
    for at, size, pick in picks:
        total = None
        for ref, row, col in pick:
            cols = slice(col, col + size)
            term = (refs[ref][:, cols] if row is None else refs[ref][row, :, cols]).astype(F32)
            total = term if total is None else total + term
        out[:, at : at + size] = total.astype(out.dtype)


def add_all(spans, done):
    arrays, picks = [], []
    for at, size, terms in spans:
        pick = []
        for array, row, col in terms:
            k = next((k for k, known in enumerate(arrays) if known is array), len(arrays))
            if k == len(arrays):
                arrays.append(array)
            pick.append((k, row, col))
        picks.append((at, size, pick))
    dims = (spans[0][2][0][0].shape[-2], sum(size for _, size, _ in spans))
    return pl.pallas_call(
        functools.partial(add_kernel, picks),
        out_shape=shape(dims, BF16),
        in_specs=[whole()] * len(arrays) + after(done),
        out_specs=whole(),
        compiler_params=params(6),
        cost_estimate=cost(0, dims[0] * dims[1] * 6 * len(spans[0][2])),
    )(*arrays, *done)


def to_chip(value, bit, n_z):
    return lax.ppermute(value, "z", [(a, a ^ bit) for a in range(n_z)])


def to_core(value):
    return lax.ppermute(value, "core", [(0, 1), (1, 0)])


def complete_z(held, n_z):
    bit = n_z // 2
    while bit:
        for m in range(0, n_z, 2 * bit):
            if m in held and m | bit not in held:
                held[m | bit] = to_chip(held[m], bit, n_z)
        bit //= 2
    return [held[m] for m in range(n_z)]


def reduce_z(spans, n_z, done):
    held = {m: [] for m in range(0, n_z, 2)}
    for at, size, evens, odds in spans:
        got = to_chip(odds, 1, n_z)
        for k, even in enumerate(evens):
            held[2 * k].append((at, size, [(even, None, 0), (got, k, 0)]))
    bit = 2
    while bit < n_z:
        for m in [m for m in held if m & bit]:
            term = to_chip(add_all(held.pop(m), done[0]), bit, n_z)
            for at, _, terms in held[m ^ bit]:
                terms.append((term, None, at))
        bit *= 2
    return add_all(held[0], done[1])


def gate_up_rows(core0, mine, theirs, cols):
    tok = mine[0].shape[0] // 2
    gate, up = [], []
    for own, other in zip(mine, theirs):
        x, y = own[:, cols].astype(F32), other[:, cols].astype(F32)
        first, second = jnp.where(core0, x, y), jnp.where(core0, y, x)
        gate += [first[:tok], second[:tok]]
        up += [first[tok:], second[tok:]]
    return jnp.concatenate(gate, 0), jnp.concatenate(up, 0)


def down_kernel(base, width, n_z, place, *refs):
    mine, theirs, grads = refs[:n_z], refs[n_z : 2 * n_z], refs[2 * n_z]
    out_hbm, token, out, sems = refs[-4:]
    token[...] = jnp.zeros_like(token)
    slots, copies = out.shape[0], []
    for k, (at, size) in enumerate(pieces(width, 512)):
        slot, cols = k % slots, slice(base + at, base + at + size)
        gate, up = gate_up_rows(place[0] == 0, mine, theirs, cols)
        hidden = gate * (1.0 / (1.0 + jnp.exp(-gate))) * up
        if k >= slots:
            copies[k - slots].wait()
        out[slot, :size, :] = jnp.dot(
            hidden.T.astype(BF16), grads[...], preferred_element_type=F32
        ).astype(BF16)
        copy = pltpu.make_async_copy(out.at[slot, :size], out_hbm.at[cols], sems.at[slot])
        copy.start()
        copies.append(copy)
    for copy in copies[-slots:]:
        copy.wait()


def down_grad(place, mine, theirs, grads, base, ff, into=None):
    n_z, total = len(mine), mine[0].shape[1]
    tokens, chans = grads.shape
    slots = min(4, len(pieces(ff, 512)))
    held = [] if into is None else [into]
    return pl.pallas_call(
        functools.partial(down_kernel, base, ff, n_z),
        out_shape=(shape((total, chans), BF16), shape((8, 128), F32)),
        in_specs=[whole(SMEM)] + [whole()] * (2 * n_z + 1) + after(held),
        out_specs=(whole(pltpu.HBM), whole()),
        scratch_shapes=[VMEM((slots, 512, chans), BF16), pltpu.SemaphoreType.DMA((slots,))],
        input_output_aliases={2 * n_z + 2: 0} if held else {},
        compiler_params=params(12),
        cost_estimate=cost(2 * tokens * chans * ff, 2 * chans * ff),
    )(place, *mine, *theirs, grads, *held)


def input_kernel(n_z, place, *refs):
    hidden, gate_up = [
        (refs[2 * k * n_z : (2 * k + 1) * n_z], refs[(2 * k + 1) * n_z : (2 * k + 2) * n_z])
        for k in range(2)
    ]
    gate_hbm, up_hbm, gate_grad, up_grad, *outs = refs[4 * n_z : -5]
    w_gate, w_up, total, held, sems = refs[-5:]
    core0, z = place[0] == 0, place[1]
    rows, width = hidden[0][0].shape
    ff = gate_grad.shape[1]
    low = ff - width
    slots = w_gate.shape[0]
    parts = [(0, at, size) for at, size in pieces(low, 1024, 256)]
    parts += [(low, at, size) for at, size in pieces(width, 1024)]

    def copies(k):
        base, at, size = parts[k]
        return [
            pltpu.make_async_copy(
                hbm.at[:, base + at : base + at + size],
                vmem.at[k % slots, :, :size],
                sems.at[n, k % slots],
            )
            for n, (hbm, vmem) in enumerate(((gate_hbm, w_gate), (up_hbm, w_up)))
        ]

    def gradients(k):
        base, at, size = parts[k]
        cols, span = slice(base + at, base + at + size), slice(at, at + size)
        first = core0 if base == 0 else ~core0
        grad = jnp.concatenate(
            [
                jnp.where(first, own[:, span], other[:, span]).astype(F32)
                for own, other in zip(*hidden)
            ],
            0,
        )
        gate, up = gate_up_rows(core0, *gate_up, cols)
        sig = 1.0 / (1.0 + jnp.exp(-gate))
        gate_grad[:, cols] = (grad * up * sig * (1.0 + gate * (1.0 - sig))).astype(BF16)
        up_grad[:, cols] = (grad * (gate * sig)).astype(BF16)

    for k in range(min(slots, len(parts))):
        for copy in copies(k):
            copy.start()
    gradients(0)
    dims = (((1,), (1,)), ((), ()))
    for k, (base, at, size) in enumerate(parts):
        for copy in copies(k):
            copy.wait()
        cols, slot = slice(base + at, base + at + size), k % slots
        term = lax.dot_general(
            w_gate[slot, :, :size], gate_grad[:, cols], dims, preferred_element_type=F32
        )
        term += lax.dot_general(
            w_up[slot, :, :size], up_grad[:, cols], dims, preferred_element_type=F32
        )
        total[...] = term if k == 0 else total[...] + term
        if k + 1 < len(parts):
            gradients(k + 1)
        if k + slots < len(parts):
            for copy in copies(k + slots):
                copy.start()
    turned = total[...].T
    for m in range(n_z):
        start = pl.multiple_of((z ^ m) * rows, math.gcd(rows, 8))
        held[pl.ds(start, rows), :] = turned[m * rows : (m + 1) * rows]
    for s, out in enumerate(outs):
        step = out.shape[0]
        start = pl.multiple_of((place[2] ^ s) * step, math.gcd(step, 8))
        out[...] = held[pl.ds(start, step), :].astype(out.dtype)


def input_grad(place, hidden, gate_up, w_gate, w_up, n_t):
    n_z, slots = len(hidden[0]), 3
    tokens = n_z * hidden[0][0].shape[0]
    chans, ff = w_gate.shape
    return pl.pallas_call(
        functools.partial(input_kernel, n_z),
        out_shape=(shape((tokens, ff), BF16),) * 2
        + (shape((tokens // n_t, chans), F32),)
        + (shape((tokens // n_t, chans), BF16),) * (n_t - 1),
        in_specs=[whole(SMEM)] + [whole()] * (4 * n_z) + [whole(pltpu.HBM)] * 2,
        out_specs=(whole(),) * (2 + n_t),
        scratch_shapes=[
            VMEM((slots, chans, min(ff, 1024)), BF16),
            VMEM((slots, chans, min(ff, 1024)), BF16),
            VMEM((chans, tokens), F32),
            VMEM((tokens, chans), F32),
            pltpu.SemaphoreType.DMA((2, slots)),
        ],
        compiler_params=params(38),
        cost_estimate=cost(4 * tokens * chans * ff, 4 * chans * ff + 12 * tokens * ff),
    )(place, *hidden[0], *hidden[1], *gate_up[0], *gate_up[1], w_gate, w_up)


def turn_kernel(n_z, n_t, place, *refs):
    inputs_t, held = refs[-2:]
    hold(refs[:n_t], 1, place[2], held)
    inputs_t[...] = blocks_of(held, place[1], n_z).T.astype(BF16)


def turn_inputs(place, parts, n_z):
    n_t, (_, rows, chans) = len(parts), parts[0].shape
    return pl.pallas_call(
        functools.partial(turn_kernel, n_z, n_t),
        out_shape=shape((chans, n_t * rows), BF16),
        in_specs=[whole(SMEM)] + [whole()] * n_t,
        out_specs=whole(),
        scratch_shapes=[VMEM((n_t * rows, chans), F32)],
        compiler_params=params(4),
        cost_estimate=cost(0, n_t * rows * chans * 4),
    )(place, *parts)


def weight_kernel(inputs_t, gate_grad, up_grad, gate_hbm, up_hbm, out, sems):
    copies = []
    ff, slots = gate_grad.shape[1], out.shape[0]
    for grad, hbm in ((gate_grad, gate_hbm), (up_grad, up_hbm)):
        for at, size in pieces(ff, 512):
            cols, slot = slice(at, at + size), len(copies) % slots
            if len(copies) >= slots:
                copies[len(copies) - slots].wait()
            out[slot, :, :size] = jnp.dot(
                inputs_t[...], grad[:, cols], preferred_element_type=F32
            ).astype(BF16)
            copy = pltpu.make_async_copy(out.at[slot, :, :size], hbm.at[:, cols], sems.at[slot])
            copy.start()
            copies.append(copy)
    for copy in copies[-slots:]:
        copy.wait()


def weight_grads(inputs_t, gate_grad, up_grad):
    chans, tokens = inputs_t.shape
    ff = gate_grad.shape[1]
    slots = min(8, 2 * len(pieces(ff, 512)))
    return pl.pallas_call(
        weight_kernel,
        out_shape=(shape((chans, ff), BF16),) * 2,
        in_specs=[whole()] * 3,
        out_specs=(whole(pltpu.HBM),) * 2,
        scratch_shapes=[VMEM((slots, chans, 512), BF16), pltpu.SemaphoreType.DMA((slots,))],
        compiler_params=params(16),
        cost_estimate=cost(4 * tokens * chans * ff, 4 * chans * ff + 4 * tokens * ff),
    )(inputs_t, gate_grad, up_grad)


def on_device(n_z, n_t, xq, xs, xo, xc, gq, gs, go, gc, gate_pre, up_pre, w_gate, w_up, w_down):
    place = jnp.stack([lax.axis_index(name) for name in ("core", "z", "tensor")]).astype(jnp.int32)
    ff = gate_pre.shape[1]
    width = -(-ff // 256) * 128

    def to_tensor(value, s):
        return lax.ppermute(value, "tensor", [(p, p ^ s) for p in range(n_t)])

    both, rows = prep(xq, xs, xo, xc, gq, gs, go, gc, gate_pre, up_pre)
    both = [both] + [to_tensor(both, s) for s in range(1, n_t)]
    bit = n_z // 2
    rows = {0: rows, bit: to_chip(rows, bit, n_z), 1: to_chip(rows, 1, n_z)}
    grads, grads_t, *send = first_half(place, both, w_down, n_z, width)
    got = [to_core(part) for part in send]
    mine = second_half(place, grads_t, w_down, n_z, ff - width, 0, width, rows[1], rows[bit])
    rows[bit | 1] = to_chip(rows[bit], 1, n_z)
    *evens, odds = pair_sum(place, mine, got, 0)
    spans = [(0, width, evens, odds)]
    rows = complete_z(rows, n_z)
    gate_up = (rows, [to_core(part) for part in rows])
    grad_down, token = down_grad(place, *gate_up, grads, 0, ff - width)
    early = [part for m, part in enumerate(gate_up[1]) if m != bit | 1]
    inputs_t = turn_inputs(place, both, n_z)
    hidden = {0: reduce_z(spans, n_z, ([inputs_t, *early], [token]))}
    hidden |= {bit: to_chip(hidden[0], bit, n_z), 1: to_chip(hidden[0], 1, n_z)}
    grad_down, token = down_grad(place, *gate_up, grads, ff - width, width, grad_down)
    hidden[bit] = add_all([(0, width, [(hidden[bit], None, 0)])], [token, hidden[1]])
    hidden = complete_z(hidden, n_z)
    gate_grad, up_grad, kept, *sends = input_grad(
        place, (hidden, [to_core(part) for part in hidden]), gate_up, w_gate, w_up, n_t
    )
    terms = [kept] + [to_tensor(part, s) for s, part in enumerate(sends, 1)]
    grad_gate, grad_up = weight_grads(inputs_t, gate_grad, up_grad)
    grad_input = add_all([(0, kept.shape[1], [(term, None, 0) for term in terms])], [])
    return grad_input, grad_gate, grad_up, grad_down


def solution(mesh):
    n_dp, n_t = mesh.shape["dp"], mesh.shape["tensor"]
    fine = Mesh(mesh.devices.reshape(n_dp // 2, 2, n_t), ("z", "core", "tensor"))
    by_token, by_dp = P("tensor", ("z", "core")), P(("z", "core"), "tensor")
    return jax.shard_map(
        functools.partial(on_device, n_dp // 2, n_t),
        mesh=fine,
        in_specs=(by_token,) * 8 + (by_dp,) * 4 + (by_token,),
        out_specs=(by_token, by_dp, by_dp, by_token),
        check_vma=False,
    )
```

```python
import functools
import math

import jax
import jax.numpy as jnp
from jax import lax
from jax.experimental import pallas as pl
from jax.experimental.pallas import tpu as pltpu
from jax.sharding import Mesh
from jax.sharding import PartitionSpec as P

BLK_C = 128
F32 = jnp.float32
BF16 = jnp.bfloat16
VMEM = pltpu.VMEM
SMEM = pltpu.SMEM


def after(arrays):
    return [pl.BlockSpec(memory_space=pl.ANY)] * len(arrays)


def whole(space=VMEM):
    return pl.BlockSpec(memory_space=space)


def shape(dims, dtype):
    return jax.ShapeDtypeStruct(dims, dtype)


def params(mib):
    return pltpu.CompilerParams(vmem_limit_bytes=mib * 1024 * 1024)


def cost(flops, nbytes):
    return pl.CostEstimate(flops=int(flops), bytes_accessed=int(nbytes), transcendentals=0)


def pieces(extent, step, first=0):
    cuts = [0] + list(range(first or step, extent, step)) + [extent]
    return [(a, b - a) for a, b in zip(cuts[:-1], cuts[1:])]


def prep_kernel(xq, xs, xo, xc, gq, gs, go, gc, gate, up, both, rows):
    for k, (quant, scale, flag, corr) in enumerate(((gq, gs, go, gc), (xq, xs, xo, xc))):
        for b in range(scale.shape[1]):
            cols = slice(b * BLK_C, (b + 1) * BLK_C)
            value = scale[0, b] * quant[:, cols].astype(F32) + flag[0, b].astype(F32) * corr[
                :, cols
            ].astype(F32)
            both[k, :, cols] = value.astype(BF16)
    rows[...] = jnp.concatenate([gate[...].astype(F32), up[...].astype(F32)], 0).astype(BF16)


def prep(xq, xs, xo, xc, gq, gs, go, gc, gate, up):
    rows, width = xq.shape
    tok, ff = gate.shape
    return pl.pallas_call(
        prep_kernel,
        out_shape=(shape((2, rows, width), BF16), shape((2 * tok, ff), BF16)),
        in_specs=[whole(), whole(SMEM), whole(SMEM), whole()] * 2 + [whole()] * 2,
        out_specs=(whole(),) * 2,
        compiler_params=params(56),
        cost_estimate=cost(0, 4 * xq.size * 2 + gate.size * 8),
    )(xq, xs, xo, xc, gq, gs, go, gc, gate, up)


def load_down(start, width, w_hbm, w_vmem, sems):
    copies = []
    for k, (at, size) in enumerate(pieces(width, 1024, 256)):
        first = pl.multiple_of(start + at, 16)
        copy = pltpu.make_async_copy(
            w_hbm.at[pl.ds(first, size)], w_vmem.at[pl.ds(at, size)], sems.at[k]
        )
        copy.start()
        copies.append(copy)
    return copies


def hidden_half(copies, grads_t, width, w_vmem, outs, turned):
    rows, depth = outs[0].shape[0], grads_t.shape[0] // 2

    def put(k, at, size):
        total = turned[k % 2, :size, :].T
        for q, out in enumerate(outs):
            out[:, at : at + size] = total[q * rows : (q + 1) * rows, :].astype(out.dtype)

    spans = pieces(width, 1024, 256)
    for k, (copy, (at, size)) in enumerate(zip(copies, spans)):
        copy.wait()
        total = jnp.dot(
            w_vmem[at : at + size, :depth], grads_t[:depth], preferred_element_type=F32
        )
        total += jnp.dot(
            w_vmem[at : at + size, depth:], grads_t[depth:], preferred_element_type=F32
        )
        turned[k % 2, :size, :] = total
        if k:
            put(k - 1, *spans[k - 1])
    put(len(spans) - 1, *spans[-1])


def blocks_of(held, z, n_z):
    block = held.shape[0] // n_z
    return jnp.concatenate(
        [
            held[pl.ds(pl.multiple_of((z ^ m) * block, math.gcd(block, 8)), block), :]
            for m in range(n_z)
        ],
        0,
    )


def hold(parts, which, me, held):
    rows = parts[0].shape[1]
    for s, part in enumerate(parts):
        start = pl.multiple_of((me ^ s) * rows, math.gcd(rows, 8))
        held[pl.ds(start, rows), :] = part[which].astype(F32)


def first_half_kernel(n_t, n_z, offset, place, *refs):
    parts, w_hbm = refs[:n_t], refs[n_t]
    grads_out, grads_t, *outs = refs[-6 - n_z : -4]
    w_vmem, turned, held, sems = refs[-4:]
    width = outs[0].shape[1]
    copies = load_down((1 - place[0]) * offset, width, w_hbm, w_vmem, sems)
    hold(parts, 0, place[2], held)
    grads_t[...] = held[...].T.astype(BF16)
    grads_out[...] = blocks_of(held, place[1], n_z).astype(BF16)
    hidden_half(copies, grads_t[...], width, w_vmem, outs, turned)


def second_half_kernel(offset, base, place, grads_t, w_hbm, *refs):
    out, w_vmem, turned, sems = refs[-4:]
    width = out.shape[2]
    outs = [out.at[q] for q in range(out.shape[0])]
    copies = load_down(place[0] * offset + base, width, w_hbm, w_vmem, sems)
    hidden_half(copies, grads_t[...], width, w_vmem, outs, turned)


def first_half(place, parts, w_down, n_z, width, *done):
    n_t, (_, rows, chans) = len(parts), parts[0].shape
    tokens = n_t * rows
    n_copies = len(pieces(width, 1024, 256))
    return pl.pallas_call(
        functools.partial(first_half_kernel, n_t, n_z, w_down.shape[0] - width),
        out_shape=(
            shape((tokens, chans), BF16),
            shape((chans, tokens), BF16),
        )
        + (shape((tokens // n_z, width), BF16),) * n_z,
        in_specs=[whole(SMEM)] + [whole()] * n_t + [whole(pltpu.HBM)] + after(done),
        out_specs=(whole(),) * (2 + n_z),
        scratch_shapes=[
            VMEM((width, chans), BF16),
            VMEM((2, min(width, 1024), tokens), F32),
            VMEM((tokens, chans), F32),
            pltpu.SemaphoreType.DMA((n_copies,)),
        ],
        compiler_params=params(44),
        cost_estimate=cost(2 * tokens * chans * width, 2 * chans * width),
    )(place, *parts, w_down, *done)


def second_half(place, grads_t, w_down, n_z, offset, base, width, *done):
    chans, tokens = grads_t.shape
    n_copies = len(pieces(width, 1024, 256))
    return pl.pallas_call(
        functools.partial(second_half_kernel, offset, base),
        out_shape=shape((n_z, tokens // n_z, width), F32),
        in_specs=[whole(SMEM), whole(), whole(pltpu.HBM)] + after(done),
        out_specs=whole(),
        scratch_shapes=[
            VMEM((width, chans), BF16),
            VMEM((2, min(width, 1024), tokens), F32),
            pltpu.SemaphoreType.DMA((n_copies,)),
        ],
        compiler_params=params(44),
        cost_estimate=cost(24 * tokens * chans * width, 24 * chans * width),
    )(place, grads_t, w_down, *done)


def pair_kernel(base, place, mine, *refs):
    n_z, _, width = mine.shape
    theirs, outs, total_ref = refs[:n_z], refs[-2 - n_z // 2 : -1], refs[-1]
    for q in range(n_z):
        total_ref[q] = mine[q] + theirs[q][:, base : base + width].astype(F32)
    for m in range(n_z):
        total = total_ref[place[1] ^ m]
        if m % 2:
            outs[-1][m // 2] = total.astype(BF16)
        else:
            outs[m // 2][...] = total


def pair_sum(place, mine, theirs, base, *done):
    n_z, rows, width = mine.shape
    return pl.pallas_call(
        functools.partial(pair_kernel, base),
        out_shape=(shape((rows, width), F32),) * (n_z // 2)
        + (shape((n_z // 2, rows, width), BF16),),
        in_specs=[whole(SMEM)] + [whole()] * (1 + n_z) + after(done),
        out_specs=(whole(),) * (n_z // 2 + 1),
        scratch_shapes=[VMEM(mine.shape, F32)],
        compiler_params=params(6),
        cost_estimate=cost(0, mine.size * 9),
    )(place, mine, *theirs, *done)


def add_kernel(picks, *refs):
    out = refs[-1]
    for at, size, pick in picks:
        total = None
        for ref, row, col in pick:
            cols = slice(col, col + size)
            term = (refs[ref][:, cols] if row is None else refs[ref][row, :, cols]).astype(F32)
            total = term if total is None else total + term
        out[:, at : at + size] = total.astype(out.dtype)


def add_all(spans, done):
    arrays, picks = [], []
    for at, size, terms in spans:
        pick = []
        for array, row, col in terms:
            k = next((k for k, known in enumerate(arrays) if known is array), len(arrays))
            if k == len(arrays):
                arrays.append(array)
            pick.append((k, row, col))
        picks.append((at, size, pick))
    dims = (spans[0][2][0][0].shape[-2], sum(size for _, size, _ in spans))
    return pl.pallas_call(
        functools.partial(add_kernel, picks),
        out_shape=shape(dims, BF16),
        in_specs=[whole()] * len(arrays) + after(done),
        out_specs=whole(),
        compiler_params=params(6),
        cost_estimate=cost(0, dims[0] * dims[1] * 6 * len(spans[0][2])),
    )(*arrays, *done)


def to_chip(value, bit, n_z):
    return lax.ppermute(value, "z", [(a, a ^ bit) for a in range(n_z)])


def to_core(value):
    return lax.ppermute(value, "core", [(0, 1), (1, 0)])


def complete_z(held, n_z):
    bit = n_z // 2
    while bit:
        for m in range(0, n_z, 2 * bit):
            if m in held and m | bit not in held:
                held[m | bit] = to_chip(held[m], bit, n_z)
        bit //= 2
    return [held[m] for m in range(n_z)]


def reduce_z(spans, n_z, done):
    held = {m: [] for m in range(0, n_z, 2)}
    for at, size, evens, odds in spans:
        got = to_chip(odds, 1, n_z)
        for k, even in enumerate(evens):
            held[2 * k].append((at, size, [(even, None, 0), (got, k, 0)]))
    bit = 2
    while bit < n_z:
        for m in [m for m in held if m & bit]:
            term = to_chip(add_all(held.pop(m), done[0]), bit, n_z)
            for at, _, terms in held[m ^ bit]:
                terms.append((term, None, at))
        bit *= 2
    return add_all(held[0], done[1])


def gate_up_rows(core0, mine, theirs, cols):
    tok = mine[0].shape[0] // 2
    gate, up = [], []
    for own, other in zip(mine, theirs):
        x, y = own[:, cols].astype(F32), other[:, cols].astype(F32)
        first, second = jnp.where(core0, x, y), jnp.where(core0, y, x)
        gate += [first[:tok], second[:tok]]
        up += [first[tok:], second[tok:]]
    return jnp.concatenate(gate, 0), jnp.concatenate(up, 0)


def down_kernel(base, width, n_z, place, *refs):
    mine, theirs, grads = refs[:n_z], refs[n_z : 2 * n_z], refs[2 * n_z]
    out_hbm, token, out, sems = refs[-4:]
    token[...] = jnp.zeros_like(token)
    slots, copies = out.shape[0], []
    for k, (at, size) in enumerate(pieces(width, 512)):
        slot, cols = k % slots, slice(base + at, base + at + size)
        gate, up = gate_up_rows(place[0] == 0, mine, theirs, cols)
        hidden = gate * (1.0 / (1.0 + jnp.exp(-gate))) * up
        if k >= slots:
            copies[k - slots].wait()
        out[slot, :size, :] = jnp.dot(
            hidden.T.astype(BF16), grads[...], preferred_element_type=F32
        ).astype(BF16)
        copy = pltpu.make_async_copy(out.at[slot, :size], out_hbm.at[cols], sems.at[slot])
        copy.start()
        copies.append(copy)
    for copy in copies[-slots:]:
        copy.wait()


def down_grad(place, mine, theirs, grads, base, ff, into=None):
    n_z, total = len(mine), mine[0].shape[1]
    tokens, chans = grads.shape
    slots = min(4, len(pieces(ff, 512)))
    held = [] if into is None else [into]
    return pl.pallas_call(
        functools.partial(down_kernel, base, ff, n_z),
        out_shape=(shape((total, chans), BF16), shape((8, 128), F32)),
        in_specs=[whole(SMEM)] + [whole()] * (2 * n_z + 1) + after(held),
        out_specs=(whole(pltpu.HBM), whole()),
        scratch_shapes=[VMEM((slots, 512, chans), BF16), pltpu.SemaphoreType.DMA((slots,))],
        input_output_aliases={2 * n_z + 2: 0} if held else {},
        compiler_params=params(12),
        cost_estimate=cost(2 * tokens * chans * ff, 2 * chans * ff),
    )(place, *mine, *theirs, grads, *held)


def input_kernel(n_z, place, *refs):
    hidden, gate_up = [
        (refs[2 * k * n_z : (2 * k + 1) * n_z], refs[(2 * k + 1) * n_z : (2 * k + 2) * n_z])
        for k in range(2)
    ]
    gate_hbm, up_hbm, gate_grad, up_grad, *outs = refs[4 * n_z : -5]
    w_gate, w_up, total, held, sems = refs[-5:]
    core0, z = place[0] == 0, place[1]
    rows, width = hidden[0][0].shape
    ff = gate_grad.shape[1]
    low = ff - width
    slots = w_gate.shape[0]
    parts = [(0, at, size) for at, size in pieces(low, 1024, 256)]
    parts += [(low, at, size) for at, size in pieces(width, 1024)]

    def copies(k):
        base, at, size = parts[k]
        return [
            pltpu.make_async_copy(
                hbm.at[:, base + at : base + at + size],
                vmem.at[k % slots, :, :size],
                sems.at[n, k % slots],
            )
            for n, (hbm, vmem) in enumerate(((gate_hbm, w_gate), (up_hbm, w_up)))
        ]

    def gradients(k):
        base, at, size = parts[k]
        cols, span = slice(base + at, base + at + size), slice(at, at + size)
        first = core0 if base == 0 else ~core0
        grad = jnp.concatenate(
            [
                jnp.where(first, own[:, span], other[:, span]).astype(F32)
                for own, other in zip(*hidden)
            ],
            0,
        )
        gate, up = gate_up_rows(core0, *gate_up, cols)
        sig = 1.0 / (1.0 + jnp.exp(-gate))
        gate_grad[:, cols] = (grad * up * sig * (1.0 + gate * (1.0 - sig))).astype(BF16)
        up_grad[:, cols] = (grad * (gate * sig)).astype(BF16)

    for k in range(min(slots, len(parts))):
        for copy in copies(k):
            copy.start()
    gradients(0)
    dims = (((1,), (1,)), ((), ()))
    for k, (base, at, size) in enumerate(parts):
        for copy in copies(k):
            copy.wait()
        cols, slot = slice(base + at, base + at + size), k % slots
        term = lax.dot_general(
            w_gate[slot, :, :size], gate_grad[:, cols], dims, preferred_element_type=F32
        )
        term += lax.dot_general(
            w_up[slot, :, :size], up_grad[:, cols], dims, preferred_element_type=F32
        )
        total[...] = term if k == 0 else total[...] + term
        if k + 1 < len(parts):
            gradients(k + 1)
        if k + slots < len(parts):
            for copy in copies(k + slots):
                copy.start()
    turned = total[...].T
    for m in range(n_z):
        start = pl.multiple_of((z ^ m) * rows, math.gcd(rows, 8))
        held[pl.ds(start, rows), :] = turned[m * rows : (m + 1) * rows]
    for s, out in enumerate(outs):
        step = out.shape[0]
        start = pl.multiple_of((place[2] ^ s) * step, math.gcd(step, 8))
        out[...] = held[pl.ds(start, step), :].astype(out.dtype)


def input_grad(place, hidden, gate_up, w_gate, w_up, n_t):
    n_z, slots = len(hidden[0]), 3
    tokens = n_z * hidden[0][0].shape[0]
    chans, ff = w_gate.shape
    return pl.pallas_call(
        functools.partial(input_kernel, n_z),
        out_shape=(shape((tokens, ff), BF16),) * 2
        + (shape((tokens // n_t, chans), F32),)
        + (shape((tokens // n_t, chans), BF16),) * (n_t - 1),
        in_specs=[whole(SMEM)] + [whole()] * (4 * n_z) + [whole(pltpu.HBM)] * 2,
        out_specs=(whole(),) * (2 + n_t),
        scratch_shapes=[
            VMEM((slots, chans, min(ff, 1024)), BF16),
            VMEM((slots, chans, min(ff, 1024)), BF16),
            VMEM((chans, tokens), F32),
            VMEM((tokens, chans), F32),
            pltpu.SemaphoreType.DMA((2, slots)),
        ],
        compiler_params=params(38),
        cost_estimate=cost(4 * tokens * chans * ff, 4 * chans * ff + 12 * tokens * ff),
    )(place, *hidden[0], *hidden[1], *gate_up[0], *gate_up[1], w_gate, w_up)


def turn_kernel(n_z, n_t, place, *refs):
    inputs_t, held = refs[-2:]
    hold(refs[:n_t], 1, place[2], held)
    inputs_t[...] = blocks_of(held, place[1], n_z).T.astype(BF16)


def turn_inputs(place, parts, n_z):
    n_t, (_, rows, chans) = len(parts), parts[0].shape
    return pl.pallas_call(
        functools.partial(turn_kernel, n_z, n_t),
        out_shape=shape((chans, n_t * rows), BF16),
        in_specs=[whole(SMEM)] + [whole()] * n_t,
        out_specs=whole(),
        scratch_shapes=[VMEM((n_t * rows, chans), F32)],
        compiler_params=params(4),
        cost_estimate=cost(0, n_t * rows * chans * 4),
    )(place, *parts)


def weight_kernel(inputs_t, gate_grad, up_grad, gate_hbm, up_hbm, out, sems):
    copies = []
    ff, slots = gate_grad.shape[1], out.shape[0]
    for grad, hbm in ((gate_grad, gate_hbm), (up_grad, up_hbm)):
        for at, size in pieces(ff, 512, 256):
            cols, slot = slice(at, at + size), len(copies) % slots
            if len(copies) >= slots:
                copies[len(copies) - slots].wait()
            out[slot, :, :size] = jnp.dot(
                inputs_t[...], grad[:, cols], preferred_element_type=F32
            ).astype(BF16)
            copy = pltpu.make_async_copy(out.at[slot, :, :size], hbm.at[:, cols], sems.at[slot])
            copy.start()
            copies.append(copy)
    for copy in copies[-slots:]:
        copy.wait()


def weight_grads(inputs_t, gate_grad, up_grad):
    chans, tokens = inputs_t.shape
    ff = gate_grad.shape[1]
    slots = min(8, 2 * len(pieces(ff, 512, 256)))
    return pl.pallas_call(
        weight_kernel,
        out_shape=(shape((chans, ff), BF16),) * 2,
        in_specs=[whole()] * 3,
        out_specs=(whole(pltpu.HBM),) * 2,
        scratch_shapes=[VMEM((slots, chans, 512), BF16), pltpu.SemaphoreType.DMA((slots,))],
        compiler_params=params(16),
        cost_estimate=cost(4 * tokens * chans * ff, 4 * chans * ff + 4 * tokens * ff),
    )(inputs_t, gate_grad, up_grad)


def on_device(n_z, n_t, xq, xs, xo, xc, gq, gs, go, gc, gate_pre, up_pre, w_gate, w_up, w_down):
    place = jnp.stack([lax.axis_index(name) for name in ("core", "z", "tensor")]).astype(jnp.int32)
    ff = gate_pre.shape[1]
    width = -(-ff // 256) * 128

    def to_tensor(value, s):
        return lax.ppermute(value, "tensor", [(p, p ^ s) for p in range(n_t)])

    both, rows = prep(xq, xs, xo, xc, gq, gs, go, gc, gate_pre, up_pre)
    both = [both] + [to_tensor(both, s) for s in range(1, n_t)]
    bit = n_z // 2
    rows = {0: rows, bit: to_chip(rows, bit, n_z), 1: to_chip(rows, 1, n_z)}
    grads, grads_t, *send = first_half(place, both, w_down, n_z, width)
    got = [to_core(part) for part in send]
    mine = second_half(place, grads_t, w_down, n_z, ff - width, 0, width, rows[1], rows[bit])
    rows[bit | 1] = to_chip(rows[bit], 1, n_z)
    *evens, odds = pair_sum(place, mine, got, 0)
    spans = [(0, width, evens, odds)]
    rows = complete_z(rows, n_z)
    gate_up = (rows, [to_core(part) for part in rows])
    grad_down, token = down_grad(place, *gate_up, grads, 0, ff - width)
    early = [part for m, part in enumerate(gate_up[1]) if m != bit | 1]
    inputs_t = turn_inputs(place, both, n_z)
    hidden = {0: reduce_z(spans, n_z, ([inputs_t, *early], [token]))}
    hidden |= {bit: to_chip(hidden[0], bit, n_z), 1: to_chip(hidden[0], 1, n_z)}
    grad_down, token = down_grad(place, *gate_up, grads, ff - width, width, grad_down)
    hidden[bit] = add_all([(0, width, [(hidden[bit], None, 0)])], [token, hidden[1]])
    hidden = complete_z(hidden, n_z)
    gate_grad, up_grad, kept, *sends = input_grad(
        place, (hidden, [to_core(part) for part in hidden]), gate_up, w_gate, w_up, n_t
    )
    terms = [kept] + [to_tensor(part, s) for s, part in enumerate(sends, 1)]
    grad_gate, grad_up = weight_grads(inputs_t, gate_grad, up_grad)
    grad_input = add_all([(0, kept.shape[1], [(term, None, 0) for term in terms])], [])
    return grad_input, grad_gate, grad_up, grad_down


def solution(mesh):
    n_dp, n_t = mesh.shape["dp"], mesh.shape["tensor"]
    fine = Mesh(mesh.devices.reshape(n_dp // 2, 2, n_t), ("z", "core", "tensor"))
    by_token, by_dp = P("tensor", ("z", "core")), P(("z", "core"), "tensor")
    return jax.shard_map(
        functools.partial(on_device, n_dp // 2, n_t),
        mesh=fine,
        in_specs=(by_token,) * 8 + (by_dp,) * 4 + (by_token,),
        out_specs=(by_token, by_dp, by_dp, by_token),
        check_vma=False,
    )
```
